32 devices in a mesh: req: 4 (over y, x), seq: 4 (over z), hid: 2 (over core).
Axes of the slice: x: 2, y: 2, z: 4, core: 2. Of those that a mesh axis runs over, the one named last changes fastest.
Arguments:
- tokens: bfloat16 [16384, 2048], P(('req', 'seq')), may hold values from -6 to 6
- attention_gain: bfloat16 [2048], replicated, may hold values from 0.099609375 to 1.8984375
- project_weight: bfloat16 [2048, 2048], P(None, 'hid'), may hold values from -0.125 to 0.125
- conv_weight: bfloat16 [4, 2048], P(None, 'hid'), may hold values from -3 to 3
- decay_down: bfloat16 [2048, 16], replicated, may hold values from -0.125 to 0.125
- decay_up: bfloat16 [16, 512], P(None, 'hid'), may hold values from -1.5 to 1.5
- decay_bias: float32 [512], P('hid'), may hold values from -2 to 10
- output_gate: bfloat16 [2048, 1024], P(None, 'hid'), may hold values from -0.125 to 0.125
- head_gain: bfloat16 [512], replicated, may hold values from 0.099609375 to 1.8984375
- output_weight: bfloat16 [1024, 2048], P('hid'), may hold values from -0.1875 to 0.1875
- mixer_gain: bfloat16 [2048], replicated, may hold values from 0.099609375 to 1.8984375
- gate_weight: bfloat16 [2048, 2816], P('req', 'hid'), may hold values from -0.125 to 0.125
- up_weight: bfloat16 [2048, 2816], P('req', 'hid'), may hold values from -0.125 to 0.125
- down_weight: bfloat16 [2816, 2048], P('hid', 'req'), may hold values from -0.109375 to 0.109375
- prompt_pages: int32 [4, 16], P('req'), may hold values from 0 to 64, as said below
- prompt_start: int32 [4, 16], P('req'), may hold values from 0 to 63, as said below
Outputs:
- hidden_out: bfloat16 [16384, 2048], P(('req', 'seq', 'hid'))
- page_states: bfloat16 [256, 2, 256, 512], P(('req', 'seq'), 'hid')
- conv_edges: bfloat16 [256, 3, 2048], P(('req', 'seq'), None, 'hid')
The draws below stay inside these ranges and needn't reach their ends.
Inputs may be any that keep to these rules, and one draw needn't show every extreme that they name: `prompt_pages`: row r lists the page counts of the prompts of group r; 0 marks an unused slot; in every draw some group holds one prompt of all its 64 pages. `prompt_start`: the slots of a row that are used cover pages in increasing order without intersection and end by page 64; pages between prompts belong to none; an unused slot starts at page 64 - 1, and every draw has one.
All inputs are finite; a program needn't handle non-finite values.
Results may differ from the reference program's by a relative error of at most 0.014.
Values may be sent and summed in bfloat16 or wider, within the bound.
No kernel may reach another device: no remote copies, remote signals or barrier semaphores. Data moves between devices by JAX's collectives and lax.ppermute only.
A program may use at most 192 MiB of HBM per device.

```python
import jax
import jax.numpy as jnp
from jax import lax

D = 2048
HEADS = 2
HK = 256
HV = 512
RANK = 16
FF = 2816
KCONV = 4
PAGE = 64
GROUP = 4096
TOKENS = 16384
PAGES_G = 64
PAGES = 256
REQ_G = 16
CONVW = 1024
N_REQ = 4
N_HID = 2


def draw_decay_bias(key, part):
    pick_key, slow_key, fast_key = jax.random.split(key, 3)
    channel_count = HEADS * HK
    slow_share = 0.5
    slow_mask = jax.random.uniform(pick_key, (channel_count,)) < slow_share
    slow_rate = jax.random.uniform(slow_key, (channel_count,), minval=0.1, maxval=1.5) / GROUP
    fast_rate = 1.0 / jax.random.uniform(fast_key, (channel_count,), minval=10.0, maxval=60.0)
    step_rate = jnp.where(slow_mask, slow_rate, fast_rate)
    retained = jnp.exp(-16.0 * step_rate)
    return (jnp.log(retained) - jnp.log1p(-retained)).astype(jnp.float32)


def prompt_layout(key):
    folded = jax.random.fold_in(key, 11)
    order_key, length_key, gap_key = jax.random.split(folded, 3)
    group_count = TOKENS // GROUP
    ranking = jax.random.permutation(order_key, group_count)
    long_rows = (ranking < 2)[:, None]
    lengths = jax.random.randint(length_key, (group_count, REQ_G), 1, 4)
    gap_pages = jax.random.randint(gap_key, (group_count, REQ_G), 0, 2)
    starts = jnp.cumsum(lengths + gap_pages, axis=1) - lengths
    slot_index = jnp.arange(REQ_G)[None, :]
    long_lengths = jnp.where(slot_index == 0, PAGES_G, 0)
    long_starts = jnp.where(slot_index == 0, 0, PAGES_G - 1)
    page_counts = jnp.where(long_rows, long_lengths, lengths).astype(jnp.int32)
    begins = jnp.where(long_rows, long_starts, starts).astype(jnp.int32)
    return (page_counts, begins)


def draw_prompt_pages(key, part):
    return prompt_layout(key)[0]


def draw_prompt_start(key, part):
    return prompt_layout(key)[1]


def block_levels(own_key, shape, cuts, smallest, top_value):
    factor_of, own = 1.0, jax.random.fold_in(own_key, 6)
    for dim, shards_of in cuts:
        draws = jnp.exp(jax.random.uniform(jax.random.fold_in(own, dim), (shards_of,), jnp.float32, smallest / len(cuts), top_value / len(cuts)))
        factor_of = factor_of * jnp.repeat(draws, shape[dim] // shards_of).reshape([-1 if axis == dim else 1 for axis in range(len(shape))])
    return factor_of


def noise(key, shape, deviation, reach, shards=(), kind=jnp.bfloat16):
    factor_of = block_levels(key, shape, shards, -0.22, 0.18) if shards else 1.0
    values = jax.random.normal(key, shape, jnp.float32) * deviation * factor_of
    return jnp.minimum(jnp.maximum(values, -reach), reach).astype(kind)


def setup_inputs(seed: int = 0) -> dict:
    seeds = jax.random.split(jax.random.key(seed), 17)
    tokens = noise(seeds[0], (TOKENS, D), 1.0, 6.0, ((0, 16),))
    attention_gain = jnp.clip(1.0 + 0.18 * jax.random.normal(seeds[1], (D,), jnp.float32), 0.099609375, 1.8984375).astype(jnp.bfloat16)
    project_weight = noise(seeds[2], (D, HEADS * CONVW), D ** -0.5, 0.125, ((1, 2),))
    conv_weight = noise(seeds[3], (KCONV, HEADS * CONVW), KCONV ** -0.5, 3.0, ((1, 2),))
    decay_down = noise(seeds[4], (D, RANK), D ** -0.5, 0.125)
    decay_up = noise(seeds[5], (RANK, HEADS * HK), RANK ** -0.5, 1.5, ((1, 2),))
    decay_bias = draw_decay_bias(jax.random.fold_in(seeds[16], 71), 0)
    output_gate = noise(seeds[7], (D, HEADS * HV), D ** -0.5, 0.125, ((1, 2),))
    head_gain = jnp.clip(1.0 + 0.18 * jax.random.normal(seeds[8], (HV,), jnp.float32), 0.099609375, 1.8984375).astype(jnp.bfloat16)
    output_weight = noise(seeds[9], (HEADS * HV, D), (HEADS * HV) ** -0.5, 0.1875, ((0, 2),))
    mixer_gain = jnp.clip(1.0 + 0.18 * jax.random.normal(seeds[10], (D,), jnp.float32), 0.099609375, 1.8984375).astype(jnp.bfloat16)
    gate_weight = noise(seeds[11], (D, FF), D ** -0.5, 0.125, ((0, 4), (1, 2)))
    up_weight = noise(seeds[12], (D, FF), D ** -0.5, 0.125, ((0, 4), (1, 2)))
    down_weight = noise(seeds[13], (FF, D), FF ** -0.5, 0.109375, ((0, 2), (1, 4)))
    prompt_pages = draw_prompt_pages(jax.random.fold_in(seeds[16], 71), 0)
    prompt_start = draw_prompt_start(jax.random.fold_in(seeds[16], 71), 0)
    return {"tokens": tokens, "attention_gain": attention_gain, "project_weight": project_weight, "conv_weight": conv_weight, "decay_down": decay_down, "decay_up": decay_up, "decay_bias": decay_bias, "output_gate": output_gate, "head_gain": head_gain, "output_weight": output_weight, "mixer_gain": mixer_gain, "gate_weight": gate_weight, "up_weight": up_weight, "down_weight": down_weight, "prompt_pages": prompt_pages, "prompt_start": prompt_start}


EPSILON = 1e-06
TOP_PRECISION = lax.Precision.HIGHEST

def rms_scaled(values, scale_gain):
    values = values.astype(jnp.float32)
    return values * lax.rsqrt(lax.optimization_barrier(jnp.mean(values * values, axis=-1, keepdims=True)) + EPSILON) * scale_gain.astype(jnp.float32)

def round_trip(values):
    return lax.optimization_barrier(values.astype(jnp.bfloat16)).astype(jnp.float32)

def page_segments(page_counts, starts, total_pages):
    position = jnp.arange(total_pages, dtype=jnp.int32)
    inside = (position[None, :] >= starts[:, None]) & (position[None, :] < starts[:, None] + page_counts[:, None])
    labels = jnp.arange(1, page_counts.shape[0] + 1, dtype=jnp.int32)
    segment = lax.optimization_barrier(jnp.sum(jnp.where(inside, labels[:, None], 0), axis=0)).astype(jnp.int32) - 1
    earlier = jnp.concatenate([jnp.full((1,), -1, jnp.int32), segment[:-1]])
    return ((segment == earlier) & (segment >= 0)).astype(jnp.float32)

def short_conv(by_page, before, carried, conv_taps):
    kept_rows = before.astype(jnp.float32) * carried[:, None, None]
    widened = jnp.concatenate([kept_rows, by_page.astype(jnp.float32)], axis=1)
    tap_count = conv_taps.shape[0]
    length = by_page.shape[1]
    result = jnp.zeros(by_page.shape, jnp.float32)
    for offset in range(tap_count):
        result = result + conv_taps[offset].astype(jnp.float32) * widened[:, tap_count - 1 - offset:tap_count - 1 - offset + length]
    return result

def split_features(mixed_rows, key_width):
    query_rows = jax.nn.silu(mixed_rows[..., :key_width])
    key_rows = jax.nn.silu(mixed_rows[..., key_width:2 * key_width]) * key_width ** (-0.5)
    value_matrix = mixed_rows[..., 2 * key_width:]
    return (query_rows.transpose(0, 2, 1, 3), key_rows.transpose(0, 2, 1, 3), value_matrix.transpose(0, 2, 1, 3))

def page_step(memory_state, inputs):
    query_rows, key_rows, value_matrix, decay_sum, carried = inputs
    memory_state = memory_state * carried
    length = query_rows.shape[1]
    raised_rows = query_rows * jnp.exp(decay_sum)
    lowered = key_rows * jnp.exp(-decay_sum)
    scores = jnp.einsum('hik,hjk->hij', raised_rows, lowered, precision=TOP_PRECISION)
    rows_index = jnp.arange(length)
    causal = rows_index[:, None] >= rows_index[None, :]
    scores = jnp.where(causal[None], scores, 0.0)
    layer_output = jnp.einsum('hij,hjv->hiv', scores, value_matrix, precision=TOP_PRECISION)
    layer_output = layer_output + jnp.einsum('eow,ews->eos', raised_rows, memory_state, precision=TOP_PRECISION)
    closing_sum = decay_sum[:, -1:, :]
    weighted_rows = key_rows * jnp.exp(closing_sum - decay_sum)
    memory_state = jnp.exp(closing_sum[:, 0, :])[:, :, None] * memory_state + jnp.einsum('lte,ltb->leb', weighted_rows, value_matrix, precision=TOP_PRECISION)
    return (memory_state, (layer_output, memory_state))

def reference(tokens, attention_gain, project_weight, conv_weight, decay_down, decay_up, decay_bias, output_gate, head_gain, output_weight, mixer_gain, gate_weight, up_weight, down_weight, prompt_pages, prompt_start):
    page_total = GROUP // PAGE
    rim_rows = KCONV - 1

    def one_group(packed):
        group_rows, page_counts, starts = packed
        normed = rms_scaled(group_rows, attention_gain).astype(jnp.bfloat16)
        projected = jnp.dot(normed, project_weight, preferred_element_type=jnp.float32).astype(jnp.bfloat16)
        by_page = projected.reshape(page_total, PAGE, HEADS * CONVW)
        before = jnp.concatenate([jnp.zeros((1, rim_rows, HEADS * CONVW), jnp.bfloat16), by_page[:-1, PAGE - rim_rows:]], axis=0)
        carried = page_segments(page_counts, starts, page_total)
        mixed_rows = short_conv(by_page, before, carried, conv_weight).reshape(page_total, PAGE, HEADS, CONVW)
        query_rows, key_rows, value_matrix = split_features(mixed_rows, HK)
        lowrank = jnp.dot(normed, decay_down, preferred_element_type=jnp.float32).astype(jnp.bfloat16)
        decay_log = jax.nn.log_sigmoid(jnp.dot(lowrank, decay_up, preferred_element_type=jnp.float32) + decay_bias) / 16.0
        decay_log = decay_log.reshape(page_total, PAGE, HEADS, HK).transpose(0, 2, 1, 3)
        decay_sum = jnp.cumsum(decay_log, axis=2)
        start_memory = jnp.zeros((HEADS, HK, HV), jnp.float32)
        final_memory, (outputs, memories) = lax.scan(page_step, start_memory, (query_rows, key_rows, value_matrix, decay_sum, carried))
        attended = outputs.transpose(0, 2, 1, 3).reshape(GROUP, HEADS, HV)
        normed_heads = rms_scaled(attended, head_gain)
        opening = jax.nn.silu(jnp.dot(normed, output_gate, preferred_element_type=jnp.float32)).reshape(GROUP, HEADS, HV)
        gated_rows = (normed_heads * opening).astype(jnp.bfloat16).reshape(GROUP, HEADS * HV)
        mixed_sum = jnp.zeros((GROUP, D), jnp.float32)
        for head_index in range(HEADS):
            lower = head_index * HV
            mixed_sum = mixed_sum + round_trip(jnp.dot(gated_rows[:, lower:lower + HV], output_weight[lower:lower + HV], preferred_element_type=jnp.float32))
        residual = (group_rows.astype(jnp.float32) + mixed_sum).astype(jnp.bfloat16)
        feed_in = rms_scaled(residual, mixer_gain).astype(jnp.bfloat16)
        gate_part = jnp.dot(feed_in, gate_weight, preferred_element_type=jnp.float32)
        up_part = jnp.dot(feed_in, up_weight, preferred_element_type=jnp.float32)
        hidden = (jax.nn.silu(gate_part) * up_part).astype(jnp.bfloat16)
        block_width = FF // N_HID
        feed_sum = jnp.zeros((GROUP, D), jnp.float32)
        for part_index in range(N_HID):
            lower = part_index * block_width
            feed_sum = feed_sum + round_trip(jnp.dot(hidden[:, lower:lower + block_width], down_weight[lower:lower + block_width], preferred_element_type=jnp.float32))
        result = (residual.astype(jnp.float32) + feed_sum).astype(jnp.bfloat16)
        return (result, memories.astype(jnp.bfloat16), by_page[:, PAGE - rim_rows:])
    results, memories, conv_edges = lax.map(one_group, (tokens.reshape(N_REQ, GROUP, D), prompt_pages, prompt_start))
    return (results.reshape(TOKENS, D), memories.reshape(PAGES, HEADS, HK, HV), conv_edges.reshape(PAGES, KCONV - 1, HEADS * CONVW))
```

```python
import functools

import jax
import jax.numpy as jnp
from jax import lax
from jax.experimental import pallas as pl
from jax.experimental.pallas import tpu as pltpu
from jax.sharding import PartitionSpec as P

HK = 256
HV = 512
KCONV = 4
PAGE = 64
CONVW = 1024
EPSILON = 1e-06
TILE = 256
PAGES_T = TILE // PAGE
RIM = 16
BF16 = jnp.bfloat16
F32 = jnp.float32
VMEM_LIMIT = 56 * 1024 * 1024


def params():
    return pltpu.CompilerParams(
        dimension_semantics=("arbitrary",), vmem_limit_bytes=VMEM_LIMIT
    )


def cost(flops, moved):
    return pl.CostEstimate(flops=flops, bytes_accessed=moved, transcendentals=0)


def fixed(shape):
    return pl.BlockSpec(
        shape, lambda *_: (0,) * len(shape), pipeline_mode=pl.Buffered(1)
    )


def whole_smem():
    return pl.BlockSpec(memory_space=pltpu.SMEM)


def dot(a, b):
    return jnp.dot(a, b, preferred_element_type=F32)


def dot_nt(a, b):
    return lax.dot_general(a, b, (((1,), (1,)), ((), ())), preferred_element_type=F32)


def dot_tn(a, b):
    return lax.dot_general(a, b, (((0,), (0,)), ((), ())), preferred_element_type=F32)


def silu(x):
    return x / (1.0 + jnp.exp(-x))


def column(row):
    return jnp.transpose(jnp.broadcast_to(row, (128, row.shape[1])))[:, :1]


def normalised(x, gain):
    return x * lax.rsqrt(jnp.mean(x * x, axis=-1, keepdims=True) + EPSILON) * gain


def front_kernel(
    carried_ref, tokens_ref, rim_ref, gain_ref, project_ref, gate_ref, down_ref, up_ref, bias_ref,
    conv_ref, raised_ref, lowered_ref, weighted_ref, value_ref, ends_ref, edges_ref, opening_ref,
    state_ref, decay_ref, carry, state, decay,
):
    step = pl.program_id(0)

    @pl.when(step == 0)
    def _():
        state[...] = jnp.zeros_like(state)
        decay[...] = jnp.ones_like(decay)

    gain = gain_ref[...].astype(F32)
    rows = jnp.concatenate([tokens_ref[...], rim_ref[...]], axis=0).astype(F32)
    normed_all = normalised(rows, gain).astype(BF16)
    normed = normed_all[:TILE]
    projected_low = dot(normed_all, project_ref[...]).astype(BF16)
    projected = projected_low[:TILE].astype(F32)
    rim = projected_low[TILE:].astype(F32)[RIM - 8 :]
    previous = jnp.where(step == 0, rim, carry[...])
    carry[...] = projected[TILE - 8 :]
    opening_ref[...] = silu(dot(normed, gate_ref[...])).astype(BF16)

    lowrank = dot(normed, down_ref[...]).astype(BF16)
    logits = dot(lowrank, up_ref[...]) + bias_ref[...]
    decay_log = (jnp.minimum(logits, 0.0) - jnp.log1p(jnp.exp(-jnp.abs(logits)))) / 16.0
    row = lax.broadcasted_iota(jnp.int32, (TILE, TILE), 0)
    col = lax.broadcasted_iota(jnp.int32, (TILE, TILE), 1)
    lower = jnp.where((row >= col) & ((row // PAGE) == (col // PAGE)), 1.0, 0.0).astype(F32)
    sums = jnp.dot(lower, decay_log, preferred_element_type=F32, precision=lax.Precision.HIGHEST)

    taps = conv_ref[...].astype(F32)
    suffix = jnp.ones((1, HK), F32)
    pieces = [None] * PAGES_T
    for j in reversed(range(PAGES_T)):
        carried = carried_ref[0, step * PAGES_T + j]
        now = projected[j * PAGE : (j + 1) * PAGE]
        before = previous if j == 0 else projected[j * PAGE - 8 : j * PAGE]
        widened = jnp.concatenate([before * carried, now], axis=0)
        mixed = taps[0:1] * now
        for i in range(1, KCONV):
            mixed = mixed + taps[i : i + 1] * widened[8 - i : 8 - i + PAGE]
        query = silu(mixed[:, :HK])
        key = silu(mixed[:, HK : 2 * HK]) * HK ** (-0.5)
        value = mixed[:, 2 * HK :].astype(BF16)
        sums_j = sums[j * PAGE : (j + 1) * PAGE]
        end = sums_j[PAGE - 1 :]
        weighted = key * jnp.exp(end - sums_j)
        span = pl.ds(j * PAGE, PAGE)
        raised_ref[span, :] = (query * jnp.exp(sums_j)).astype(BF16)
        lowered_ref[span, :] = (key * jnp.exp(-sums_j)).astype(BF16)
        weighted_ref[span, :] = weighted.astype(BF16)
        value_ref[span, :] = value
        kept = jnp.exp(end)
        ends_ref[j] = jnp.broadcast_to(kept, (8, HK))
        edges_ref[j] = projected_low[(j + 1) * PAGE - (KCONV - 1) : (j + 1) * PAGE]
        pieces[j] = ((weighted * suffix).astype(BF16), value)
        suffix = suffix * (kept * carried)
    keys = jnp.concatenate([p[0] for p in pieces], axis=0)
    values = jnp.concatenate([p[1] for p in pieces], axis=0)
    state[...] = column(suffix) * state[...] + dot_tn(keys, values)
    decay[...] = decay[...] * suffix

    @pl.when(step == pl.num_programs(0) - 1)
    def _():
        state_ref[...] = state[...].astype(BF16)
        decay_ref[...] = decay[...]


def front(carried, tokens, rim, gain, project, gate, down, up, bias, conv):
    count, width = tokens.shape
    rank = down.shape[1]
    pages = count // PAGE
    rows = lambda n: pl.BlockSpec((TILE, n), lambda i: (i, 0))
    shape = jax.ShapeDtypeStruct
    return pl.pallas_call(
        front_kernel,
        name="front",
        grid=(count // TILE,),
        in_specs=[
            whole_smem(), rows(width), fixed((RIM, width)), fixed((1, width)),
            fixed((width, CONVW)), fixed((width, HV)), fixed((width, rank)), fixed((rank, HK)),
            fixed((1, HK)), fixed((KCONV, CONVW)),
        ],
        out_specs=[
            rows(HK), rows(HK), rows(HK), rows(HV),
            pl.BlockSpec((PAGES_T, 8, HK), lambda i: (i, 0, 0)),
            pl.BlockSpec((PAGES_T, KCONV - 1, CONVW), lambda i: (i, 0, 0)),
            rows(HV), fixed((HK, HV)), fixed((8, HK)),
        ],
        out_shape=[
            shape((count, HK), BF16), shape((count, HK), BF16), shape((count, HK), BF16),
            shape((count, HV), BF16), shape((pages, 8, HK), F32),
            shape((pages, KCONV - 1, CONVW), BF16), shape((count, HV), BF16),
            shape((HK, HV), BF16), shape((8, HK), F32),
        ],
        scratch_shapes=[
            pltpu.VMEM((8, CONVW), F32), pltpu.VMEM((HK, HV), F32), pltpu.VMEM((8, HK), F32)
        ],
        compiler_params=params(),
        cost_estimate=cost(1000, 1000),
    )(carried, tokens, rim, gain, project, gate, down, up, bias, conv)


def pages_kernel(
    carried_ref, raised_ref, lowered_ref, weighted_ref, value_ref, ends_ref, opening_ref, gain_ref,
    one_ref, two_ref, three_ref, decay_one_ref, decay_two_ref, states_ref, gated_ref, memory,
):
    step = pl.program_id(0)

    @pl.when(step == 0)
    def _():
        far = two_ref[...].astype(F32) + column(decay_two_ref[:1]) * three_ref[...].astype(F32)
        memory[...] = one_ref[...].astype(F32) + column(decay_one_ref[:1]) * far

    row = lax.broadcasted_iota(jnp.int32, (PAGE, PAGE), 0)
    col = lax.broadcasted_iota(jnp.int32, (PAGE, PAGE), 1)
    gain = gain_ref[...].astype(F32)
    held = memory[...]
    for j in range(PAGES_T):
        span = pl.ds(j * PAGE, PAGE)
        raised, value = raised_ref[span, :], value_ref[span, :]
        held = held * carried_ref[0, step * PAGES_T + j]
        scores = dot_nt(raised, lowered_ref[span, :])
        scores = jnp.where(row >= col, scores, 0.0).astype(BF16)
        attended = dot(scores, value) + dot(raised, held.astype(BF16))
        held = column(ends_ref[j][:1]) * held + dot_tn(weighted_ref[span, :], value)
        states_ref[j, 0] = held.astype(BF16)
        gated = normalised(attended, gain) * opening_ref[span, :].astype(F32)
        gated_ref[span, :] = gated.astype(BF16)
    memory[...] = held


def pages(carried, raised, lowered, weighted, value, ends, opening, gain, one, two, three, decay_one, decay_two):
    count = raised.shape[0]
    total = count // PAGE
    rows = lambda n: pl.BlockSpec((TILE, n), lambda i: (i, 0))
    return pl.pallas_call(
        pages_kernel,
        name="pages",
        grid=(count // TILE,),
        in_specs=[
            whole_smem(), rows(HK), rows(HK), rows(HK), rows(HV),
            pl.BlockSpec((PAGES_T, 8, HK), lambda i: (i, 0, 0)), rows(HV), fixed((1, HV)),
            fixed((HK, HV)), fixed((HK, HV)), fixed((HK, HV)), fixed((8, HK)), fixed((8, HK)),
        ],
        out_specs=[
            pl.BlockSpec((PAGES_T, 1, HK, HV), lambda i: (i, 0, 0, 0)), rows(HV),
        ],
        out_shape=[
            jax.ShapeDtypeStruct((total, 1, HK, HV), BF16),
            jax.ShapeDtypeStruct((count, HV), BF16),
        ],
        scratch_shapes=[pltpu.VMEM((HK, HV), F32)],
        compiler_params=params(),
        cost_estimate=cost(1000, 1000),
    )(carried, raised, lowered, weighted, value, ends, opening, gain, one, two, three, decay_one, decay_two)


def mix_kernel(tokens_ref, own_ref, other_ref, own_weight_ref, other_weight_ref, gain_ref, residual_ref, feed_ref):
    mixed = dot(own_ref[...], own_weight_ref[...]) + dot(other_ref[...], other_weight_ref[...])
    residual = (tokens_ref[...].astype(F32) + mixed).astype(BF16)
    residual_ref[...] = residual
    feed_ref[...] = normalised(residual.astype(F32), gain_ref[...].astype(F32)).astype(BF16)


def mix(tokens, own, other, own_weight, other_weight, gain):
    count, width = tokens.shape
    rows = lambda n: pl.BlockSpec((TILE, n), lambda i: (i, 0))
    return pl.pallas_call(
        mix_kernel,
        name="mix",
        grid=(count // TILE,),
        in_specs=[
            rows(width), rows(HV), rows(HV), fixed((HV, width)), fixed((HV, width)), fixed((1, width)),
        ],
        out_specs=[rows(width), rows(width)],
        out_shape=[jax.ShapeDtypeStruct((count, width), BF16)] * 2,
        compiler_params=params(),
        cost_estimate=cost(1000, 1000),
    )(tokens, own, other, own_weight, other_weight, gain)


def widen_kernel(places, offset_ref, feed_ref, *refs):
    out_ref = refs[-1]
    sums = []
    slot = 0
    for matrix in places:
        total = None
        for size in matrix:
            start = pl.multiple_of(offset_ref[0, slot], 128)
            part = dot(feed_ref[:, pl.ds(start, size)], refs[slot][...])
            total = part if total is None else total + part
            slot += 1
        sums.append(total)
    out_ref[...] = (silu(sums[0]) * sums[1]).astype(BF16)


def widen(feed, matrices):
    count, width = feed.shape
    pieces = [piece for matrix in matrices for piece, _ in matrix]
    offsets = jnp.stack([jnp.asarray(at, jnp.int32) for matrix in matrices for _, at in matrix])
    places = [[piece.shape[0] for piece, _ in matrix] for matrix in matrices]
    hidden = pieces[0].shape[1]
    wide = 256
    return pl.pallas_call(
        functools.partial(widen_kernel, places),
        name="widen",
        grid=(pl.cdiv(hidden, wide),),
        in_specs=[whole_smem(), fixed((count, width))]
        + [pl.BlockSpec((piece.shape[0], wide), lambda i: (0, i)) for piece in pieces],
        out_specs=pl.BlockSpec((count, wide), lambda i: (0, i)),
        out_shape=jax.ShapeDtypeStruct((count, hidden), BF16),
        compiler_params=params(),
        cost_estimate=cost(1000, 1000),
    )(offsets[None], feed, *pieces)


def narrow_kernel(offset_ref, hidden_ref, *refs):
    out_ref = refs[-1]
    hidden = hidden_ref[...]
    for slot, ref in enumerate(refs[:-1]):
        start = pl.multiple_of(offset_ref[slot + 1], 128)
        out_ref[:, pl.ds(start, ref.shape[1])] = dot(hidden, ref[...]).astype(BF16)


def narrow(hidden, half, pieces, width):
    count, depth = hidden.shape
    rows = count // 2
    tiles = rows // TILE
    offsets = jnp.stack([jnp.asarray(at, jnp.int32) for at in [half] + [at for _, at in pieces]])
    whole = lambda shape: pl.BlockSpec(
        shape, lambda i, s: (0, 0), pipeline_mode=pl.Buffered(1)
    )
    return pl.pallas_call(
        narrow_kernel,
        name="narrow",
        grid_spec=pltpu.PrefetchScalarGridSpec(
            num_scalar_prefetch=1,
            grid=(tiles,),
            in_specs=[pl.BlockSpec((TILE, depth), lambda i, s: (s[0] * tiles + i, 0))]
            + [whole(piece.shape) for piece, _ in pieces],
            out_specs=pl.BlockSpec((TILE, width), lambda i, s: (i, 0)),
        ),
        out_shape=jax.ShapeDtypeStruct((rows, width), BF16),
        compiler_params=params(),
        cost_estimate=cost(1000, 1000),
    )(offsets, hidden, *[piece for piece, _ in pieces])


def page_segments(page_counts, starts, total_pages):
    position = jnp.arange(total_pages, dtype=jnp.int32)
    inside = (position[None, :] >= starts[:, None]) & (
        position[None, :] < starts[:, None] + page_counts[:, None]
    )
    labels = jnp.arange(1, page_counts.shape[0] + 1, dtype=jnp.int32)
    segment = jnp.sum(jnp.where(inside, labels[:, None], 0), axis=0) - 1
    earlier = jnp.concatenate([jnp.full((1,), -1, jnp.int32), segment[:-1]])
    return ((segment == earlier) & (segment >= 0)).astype(F32)


def shifted(value, steps):
    count = lax.axis_size("seq")
    return lax.ppermute(value, "seq", [(i, i + steps) for i in range(count - steps)])


def swapped(value, axis, flip):
    count = lax.axis_size(axis)
    return lax.ppermute(value, axis, [(i, i ^ flip) for i in range(count)])


def after(value, *others):
    return lax.optimization_barrier((value, *others))[0]


def on_device(
    tokens, attention_gain, project_weight, conv_weight, decay_down, decay_up, decay_bias,
    output_gate, head_gain, output_weight, mixer_gain, gate_weight, up_weight, down_weight,
    prompt_pages, prompt_start,
):
    count, width = tokens.shape
    page_count = count // PAGE
    seq_index, hid_index = lax.axis_index("seq"), lax.axis_index("hid")
    req_index = lax.axis_index("req")
    two_by_two = lax.axis_size("req") == 4 and lax.axis_size("seq") % 2 == 0
    group_pages = page_count * lax.axis_size("seq")
    flags = page_segments(prompt_pages[0], prompt_start[0], group_pages)
    carried = lax.dynamic_slice_in_dim(flags, seq_index * page_count, page_count)[None]

    rim = shifted(tokens[-RIM:], 1)
    other_output = swapped(output_weight, "hid", 1)

    depth = gate_weight.shape[0]
    half = depth // 2
    if two_by_two:
        parity = lax.rem(seq_index, 2)
        up_mine = lax.dynamic_slice_in_dim(up_weight, parity * half, half, 0)
        down_mine = lax.dynamic_slice_in_dim(down_weight, parity * half, half, 1)
        gate_0, gate_1 = gate_weight[:half], gate_weight[half:]
        up_a, up_b = swapped(up_mine, "req", 1), swapped(up_mine, "req", 2)
        down_mine = after(down_mine, rim)
        down_a, down_b = swapped(down_mine, "req", 1), swapped(down_mine, "req", 2)

    front_out = front(
        carried, tokens, rim, attention_gain[None], project_weight, output_gate, decay_down,
        decay_up, decay_bias[None], conv_weight,
    )
    raised, lowered, weighted, value, ends, edges, opening, state, decay = front_out
    one, two, three = (shifted(state, i) for i in (1, 2, 3))
    decay_one, decay_two = shifted(decay, 1), shifted(decay, 2)
    if two_by_two:
        up_a, up_b, raised = lax.optimization_barrier((up_a, up_b, raised))
        up_c = swapped(up_b, "req", 1)
        far_a, far_b = swapped(up_a, "seq", 1), swapped(up_b, "seq", 1)
        gate_0 = after(gate_0, up_a, up_b)
        gate_a0, gate_b0 = swapped(gate_0, "req", 1), swapped(gate_0, "req", 2)
    states, gated = pages(
        carried, raised, lowered, weighted, value, ends, opening, head_gain[None],
        one, two, three, decay_one, decay_two,
    )
    other_gated = swapped(gated, "hid", 1)
    if two_by_two:
        up_c, down_a, down_b, gated = lax.optimization_barrier((up_c, down_a, down_b, gated))
        down_c = swapped(down_a, "req", 2)
        far_c = swapped(up_c, "seq", 1)
        gate_1 = after(gate_1, down_a, down_b)
        gate_a1, gate_b1 = swapped(gate_1, "req", 1), swapped(gate_1, "req", 2)
        gate_c0 = swapped(gate_b0, "req", 1)
        gate_c1 = swapped(gate_a1, "req", 2)
        down_far = [swapped(piece, "seq", 1) for piece in (down_a, down_b, down_c)]
    residual, feed = mix(tokens, gated, other_gated, output_weight, other_output, mixer_gain[None])

    if two_by_two:
        base = [(req_index ^ flip) * depth for flip in (0, 1, 2, 3)]
        mine, theirs = parity * half, (1 - parity) * half
        gate_list = [(gate_weight, base[0])]
        for at, pair in zip(base[1:], ((gate_a0, gate_a1), (gate_b0, gate_b1), (gate_c0, gate_c1))):
            gate_list += [(pair[0], at), (pair[1], at + half)]
        up_list = [(up_weight, base[0])]
        down_list = [(down_weight, base[0])]
        for at, near, far in zip(base[1:], (up_a, up_b, up_c), (far_a, far_b, far_c)):
            up_list += [(near, at + mine), (far, at + theirs)]
        for at, near, far in zip(base[1:], (down_a, down_b, down_c), down_far):
            down_list += [(near, at + mine), (far, at + theirs)]
    else:
        gate_list = [(lax.all_gather(gate_weight, "req", axis=0, tiled=True), 0)]
        up_list = [(lax.all_gather(up_weight, "req", axis=0, tiled=True), 0)]
        down_list = [(lax.all_gather(down_weight, "req", axis=1, tiled=True), 0)]

    hidden = widen(feed, (gate_list, up_list))
    theirs_sum = narrow(hidden, 1 - hid_index, down_list, width)
    received = swapped(theirs_sum, "hid", 1)
    own_sum = narrow(hidden, hid_index, down_list, width)
    own_rows = lax.dynamic_slice_in_dim(residual, hid_index * (count // 2), count // 2, 0)
    result = (
        own_rows.astype(F32) + (own_sum.astype(F32) + received.astype(F32))
    ).astype(BF16)
    return result, states, edges


def solution(mesh):
    return jax.shard_map(
        on_device,
        mesh=mesh,
        in_specs=(
            P(("req", "seq"), None),
            P(),
            P(None, "hid"),
            P(None, "hid"),
            P(),
            P(None, "hid"),
            P("hid"),
            P(None, "hid"),
            P(),
            P("hid", None),
            P(),
            P("req", "hid"),
            P("req", "hid"),
            P("hid", "req"),
            P("req", None),
            P("req", None),
        ),
        out_specs=(
            P(("req", "seq", "hid"), None),
            P(("req", "seq"), "hid", None, None),
            P(("req", "seq"), None, "hid"),
        ),
        check_vma=False,
    )
```

```python
import functools

import jax
import jax.numpy as jnp
from jax import lax
from jax.experimental import pallas as pl
from jax.experimental.pallas import tpu as pltpu
from jax.sharding import PartitionSpec as P

HK = 256
HV = 512
KCONV = 4
PAGE = 64
CONVW = 1024
EPSILON = 1e-06
TILE = 256
PAGES_T = TILE // PAGE
RIM = 16
BF16 = jnp.bfloat16
F32 = jnp.float32
VMEM_LIMIT = 56 * 1024 * 1024
WIDE = 256


def params():
    return pltpu.CompilerParams(
        dimension_semantics=("arbitrary",), vmem_limit_bytes=VMEM_LIMIT
    )


def cost(flops, moved):
    return pl.CostEstimate(flops=flops, bytes_accessed=moved, transcendentals=0)


def fixed(shape):
    return pl.BlockSpec(
        shape, lambda *_: (0,) * len(shape), pipeline_mode=pl.Buffered(1)
    )


def whole_smem():
    return pl.BlockSpec(memory_space=pltpu.SMEM)


def dot(a, b):
    return jnp.dot(a, b, preferred_element_type=F32)


def dot_nt(a, b):
    return lax.dot_general(a, b, (((1,), (1,)), ((), ())), preferred_element_type=F32)


def dot_tn(a, b):
    return lax.dot_general(a, b, (((0,), (0,)), ((), ())), preferred_element_type=F32)


def silu(x):
    return x / (1.0 + jnp.exp(-x))


def column(row):
    return jnp.transpose(jnp.broadcast_to(row, (128, row.shape[1])))[:, :1]


def normalised(x, gain):
    return x * lax.rsqrt(jnp.mean(x * x, axis=-1, keepdims=True) + EPSILON) * gain


def carried_flag(pages_ref, start_ref, page):
    page = lax.axis_index("seq") * (pl.num_programs(0) * PAGES_T) + page
    same = jnp.int32(0)
    for i in range(pages_ref.shape[1]):
        first = start_ref[0, i]
        same = jnp.where((page > first) & (page < first + pages_ref[0, i]), 1, same)
    return same.astype(F32)


def front_kernel(
    pages_ref, start_ref, tokens_ref, rim_ref, gain_ref, project_ref, gate_ref, down_ref, up_ref, bias_ref,
    conv_ref, raised_ref, lowered_ref, weighted_ref, value_ref, ends_ref, edges_ref, opening_ref,
    state_ref, carry, state, decay,
):
    step = pl.program_id(0)

    @pl.when(step == 0)
    def _():
        state[...] = jnp.zeros_like(state)
        decay[...] = jnp.ones_like(decay)

    gain = gain_ref[...].astype(F32)
    rows = jnp.concatenate([tokens_ref[...], rim_ref[...]], axis=0).astype(F32)
    normed_all = normalised(rows, gain).astype(BF16)
    normed = normed_all[:TILE]
    projected_low = dot(normed_all, project_ref[...]).astype(BF16)
    projected = projected_low[:TILE].astype(F32)
    rim = projected_low[TILE:].astype(F32)[RIM - 8 :]
    previous = jnp.where(step == 0, rim, carry[...])
    carry[...] = projected[TILE - 8 :]
    opening_ref[...] = silu(dot(normed, gate_ref[...])).astype(BF16)

    lowrank = dot_nt(normed, down_ref[...]).astype(BF16)
    logits = dot(lowrank, up_ref[...]) + bias_ref[...]
    decay_log = (jnp.minimum(logits, 0.0) - jnp.log1p(jnp.exp(-jnp.abs(logits)))) / 16.0
    row = lax.broadcasted_iota(jnp.int32, (TILE, TILE), 0)
    col = lax.broadcasted_iota(jnp.int32, (TILE, TILE), 1)
    lower = jnp.where((row >= col) & ((row // PAGE) == (col // PAGE)), 1.0, 0.0).astype(F32)
    sums = jnp.dot(lower, decay_log, preferred_element_type=F32, precision=lax.Precision.HIGHEST)

    taps = conv_ref[...].astype(F32)
    suffix = jnp.ones((1, HK), F32)
    pieces = [None] * PAGES_T
    for j in reversed(range(PAGES_T)):
        carried = carried_flag(pages_ref, start_ref, step * PAGES_T + j)
        now = projected[j * PAGE : (j + 1) * PAGE]
        before = previous if j == 0 else projected[j * PAGE - 8 : j * PAGE]
        widened = jnp.concatenate([before * carried, now], axis=0)
        mixed = taps[0:1] * now
        for i in range(1, KCONV):
            mixed = mixed + taps[i : i + 1] * widened[8 - i : 8 - i + PAGE]
        query = silu(mixed[:, :HK])
        key = silu(mixed[:, HK : 2 * HK]) * HK ** (-0.5)
        value = mixed[:, 2 * HK :].astype(BF16)
        sums_j = sums[j * PAGE : (j + 1) * PAGE]
        end = sums_j[PAGE - 1 :]
        weighted = key * jnp.exp(end - sums_j)
        span = pl.ds(j * PAGE, PAGE)
        raised_ref[span, :] = (query * jnp.exp(sums_j)).astype(BF16)
        lowered_ref[span, :] = (key * jnp.exp(-sums_j)).astype(BF16)
        weighted_ref[span, :] = weighted.astype(BF16)
        value_ref[span, :] = value
        kept = jnp.exp(end)
        ends_ref[j] = jnp.broadcast_to(kept, (8, HK))
        edges_ref[j] = projected_low[(j + 1) * PAGE - (KCONV - 1) : (j + 1) * PAGE]
        pieces[j] = ((weighted * suffix).astype(BF16), value)
        suffix = suffix * (kept * carried)
    keys = jnp.concatenate([p[0] for p in pieces], axis=0)
    values = jnp.concatenate([p[1] for p in pieces], axis=0)
    state[...] = column(suffix) * state[...] + dot_tn(keys, values)
    decay[...] = decay[...] * suffix

    @pl.when(step == pl.num_programs(0) - 1)
    def _():
        state_ref[:HK] = state[...].astype(BF16)
        block = jnp.concatenate([decay[...]] * (HV // HK), axis=1)
        state_ref[HK:] = jnp.concatenate([block] * (RIM // 8), axis=0).astype(BF16)


def front(prompts, tokens, rim, gain, project, gate, down, up, bias, conv):
    count, width = tokens.shape
    rank = down.shape[0]
    pages = count // PAGE
    rows = lambda n: pl.BlockSpec((TILE, n), lambda i: (i, 0))
    shape = jax.ShapeDtypeStruct
    return pl.pallas_call(
        front_kernel,
        name="front",
        grid=(count // TILE,),
        in_specs=[
            whole_smem(), whole_smem(), rows(width), fixed((RIM, width)), fixed((1, width)),
            fixed((width, CONVW)), fixed((width, HV)), fixed((rank, width)), fixed((rank, HK)),
            fixed((1, HK)), fixed((KCONV, CONVW)),
        ],
        out_specs=[
            rows(HK), rows(HK), rows(HK), rows(HV),
            pl.BlockSpec((PAGES_T, 8, HK), lambda i: (i, 0, 0)),
            pl.BlockSpec((PAGES_T, KCONV - 1, CONVW), lambda i: (i, 0, 0)),
            rows(HV), fixed((HK + RIM, HV)),
        ],
        out_shape=[
            shape((count, HK), BF16), shape((count, HK), BF16), shape((count, HK), BF16),
            shape((count, HV), BF16), shape((pages, 8, HK), F32),
            shape((pages, KCONV - 1, CONVW), BF16), shape((count, HV), BF16),
            shape((HK + RIM, HV), BF16),
        ],
        scratch_shapes=[
            pltpu.VMEM((8, CONVW), F32), pltpu.VMEM((HK, HV), F32), pltpu.VMEM((8, HK), F32)
        ],
        compiler_params=params(),
        cost_estimate=cost(1000, 1000),
    )(*prompts, tokens, rim, gain, project, gate, down, up, bias, conv)


def halves(count):
    half = count // TILE // 2
    return [
        pl.BlockSpec((TILE, HV), lambda i: (jnp.minimum(i, half - 1), 0)),
        pl.BlockSpec((TILE, HV), lambda i: (jnp.maximum(i - half, 0), 0)),
    ]


def pages_kernel(
    pages_ref, start_ref, raised_ref, lowered_ref, weighted_ref, value_ref, ends_ref, opening_ref, gain_ref,
    one_ref, two_ref, three_ref, states_ref, low_ref, high_ref, memory,
):
    step = pl.program_id(0)

    @pl.when(step == 0)
    def _():
        part = lambda ref: ref[:HK].astype(F32)
        kept = lambda ref: column(ref[HK:].astype(F32)[:1, :HK])
        memory[...] = part(one_ref) + kept(one_ref) * (part(two_ref) + kept(two_ref) * part(three_ref))

    row = lax.broadcasted_iota(jnp.int32, (PAGE, PAGE), 0)
    col = lax.broadcasted_iota(jnp.int32, (PAGE, PAGE), 1)
    gain = gain_ref[...].astype(F32)
    held = memory[...]
    gated_tile = []
    for j in range(PAGES_T):
        span = pl.ds(j * PAGE, PAGE)
        raised, value = raised_ref[span, :], value_ref[span, :]
        held = held * carried_flag(pages_ref, start_ref, step * PAGES_T + j)
        scores = dot_nt(raised, lowered_ref[span, :])
        scores = jnp.where(row >= col, scores, 0.0).astype(BF16)
        attended = dot(scores, value) + dot(raised, held.astype(BF16))
        held = column(ends_ref[j][:1]) * held + dot_tn(weighted_ref[span, :], value)
        states_ref[j, 0] = held.astype(BF16)
        gated = normalised(attended, gain) * opening_ref[span, :].astype(F32)
        gated_tile.append(gated.astype(BF16))
    memory[...] = held
    half = pl.num_programs(0) // 2

    @pl.when(step < half)
    def _():
        low_ref[...] = jnp.concatenate(gated_tile, axis=0)

    @pl.when(step >= half)
    def _():
        high_ref[...] = jnp.concatenate(gated_tile, axis=0)


def pages(prompts, raised, lowered, weighted, value, ends, opening, gain, one, two, three):
    count = raised.shape[0]
    total = count // PAGE
    rows = lambda n: pl.BlockSpec((TILE, n), lambda i: (i, 0))
    return pl.pallas_call(
        pages_kernel,
        name="pages",
        grid=(count // TILE,),
        in_specs=[
            whole_smem(), whole_smem(), rows(HK), rows(HK), rows(HK), rows(HV),
            pl.BlockSpec((PAGES_T, 8, HK), lambda i: (i, 0, 0)), rows(HV), fixed((1, HV)),
            fixed((HK + RIM, HV)), fixed((HK + RIM, HV)), fixed((HK + RIM, HV)),
        ],
        out_specs=[
            pl.BlockSpec((PAGES_T, 1, HK, HV), lambda i: (i, 0, 0, 0)), *halves(count),
        ],
        out_shape=[
            jax.ShapeDtypeStruct((total, 1, HK, HV), BF16),
            jax.ShapeDtypeStruct((count // 2, HV), BF16),
            jax.ShapeDtypeStruct((count // 2, HV), BF16),
        ],
        scratch_shapes=[pltpu.VMEM((HK, HV), F32)],
        compiler_params=params(),
        cost_estimate=cost(1000, 1000),
    )(*prompts, raised, lowered, weighted, value, ends, opening, gain, one, two, three)


def mix_kernel(tokens_ref, low_ref, high_ref, other_low_ref, other_high_ref, weight_ref, gain_ref, residual_ref, feed_ref):
    step, half = pl.program_id(0), pl.num_programs(0) // 2
    own = jnp.where(step < half, low_ref[...], high_ref[...])
    other = jnp.where(step < half, other_low_ref[...], other_high_ref[...])
    mine = lax.axis_index("hid")
    rows = lambda head: pl.ds(pl.multiple_of(head * HV, HV), HV)
    mixed = dot(own, weight_ref[rows(mine), :]) + dot(other, weight_ref[rows(1 - mine), :])
    residual = (tokens_ref[...].astype(F32) + mixed).astype(BF16)
    residual_ref[...] = residual
    feed_ref[...] = normalised(residual.astype(F32), gain_ref[...].astype(F32)).astype(BF16)


def mix(tokens, own, others, weight, gain):
    count, width = tokens.shape
    rows = lambda n: pl.BlockSpec((TILE, n), lambda i: (i, 0))
    return pl.pallas_call(
        mix_kernel,
        name="mix",
        grid=(count // TILE,),
        in_specs=[
            rows(width), *halves(count), *halves(count), fixed(weight.shape), fixed((1, width)),
        ],
        out_specs=[rows(width), rows(width)],
        out_shape=[jax.ShapeDtypeStruct((count, width), BF16)] * 2,
        compiler_params=params(),
        cost_estimate=cost(1000, 1000),
    )(tokens, *own, *others, weight, gain)


def widen_kernel(places, feed_hbm, *refs):
    pieces, (out_ref, feed, weight, feed_sem, sems) = refs[:-5], refs[-5:]
    hidden = out_ref.shape[1]
    full = hidden // WIDE
    starts = [place() for _, place in places]

    def copies(chunk, wide):
        low = chunk * WIDE
        for i, ((matrix, _), start, ref) in enumerate(zip(places, starts, pieces)):
            rows = pl.ds(pl.multiple_of(start, 128), ref.shape[0])
            columns = pl.ds(pl.multiple_of(2 * low + matrix * wide, 128), wide)
            yield pltpu.make_async_copy(
                ref.at[:, pl.ds(pl.multiple_of(low, 128), wide)], weight.at[rows, columns], sems.at[chunk, i]
            )

    def compute(chunk, wide):
        for copy in copies(chunk, wide):
            copy.wait()
        low = pl.multiple_of(chunk * WIDE, 128)
        both = dot(feed[...], weight[:, pl.ds(pl.multiple_of(2 * low, 128), 2 * wide)])
        out_ref[:, pl.ds(low, wide)] = (silu(both[:, :wide]) * both[:, wide:]).astype(BF16)

    whole = pltpu.make_async_copy(feed_hbm, feed, feed_sem)
    whole.start()
    rest = hidden - full * WIDE
    for chunk in range(full):
        for copy in copies(chunk, WIDE):
            copy.start()
    if rest:
        for copy in copies(full, rest):
            copy.start()
    whole.wait()

    @pl.loop(0, full)
    def _(chunk):
        compute(chunk, WIDE)

    if rest:
        compute(full, rest)


def widen(feed, matrices):
    count, width = feed.shape
    pieces = [piece for matrix in matrices for piece, _ in matrix]
    places = [(i, place) for i, matrix in enumerate(matrices) for _, place in matrix]
    hidden = pieces[0].shape[1]
    chunks = pl.cdiv(hidden, WIDE)
    return pl.pallas_call(
        functools.partial(widen_kernel, places),
        name="widen",
        in_specs=[pl.BlockSpec(memory_space=pl.ANY)] * (1 + len(pieces)),
        out_specs=pl.BlockSpec(memory_space=pltpu.VMEM),
        out_shape=jax.ShapeDtypeStruct((count, hidden), BF16),
        scratch_shapes=[
            pltpu.VMEM((count, width), BF16), pltpu.VMEM((width, 2 * hidden), BF16),
            pltpu.SemaphoreType.DMA, pltpu.SemaphoreType.DMA((chunks, len(pieces))),
        ],
        compiler_params=pltpu.CompilerParams(vmem_limit_bytes=VMEM_LIMIT),
        cost_estimate=cost(1000, 1000),
    )(feed, *pieces)


def narrow_kernel(places, half, hidden_hbm, *refs):
    count = len(places)
    pieces, out_ref = refs[:count], refs[count]
    hidden, weights, sem, sems = refs[count + 1], refs[count + 2 : -2], refs[-2], refs[-1]
    rows = hidden.shape[0]
    start = pl.multiple_of(half() * rows, rows)
    whole = pltpu.make_async_copy(hidden_hbm.at[pl.ds(start, rows), :], hidden, sem)
    whole.start()
    copies = [
        pltpu.make_async_copy(ref, weight, sems.at[i])
        for i, (ref, weight) in enumerate(zip(pieces, weights))
    ]
    for copy in copies:
        copy.start()
    whole.wait()
    for place, copy, weight in zip(places, copies, weights):
        copy.wait()
        columns = pl.ds(pl.multiple_of(place(), 128), weight.shape[1])
        out_ref[:, columns] = dot(hidden[...], weight[...]).astype(BF16)


def narrow(hidden, half, pieces, width):
    count, depth = hidden.shape
    rows = count // 2
    return pl.pallas_call(
        functools.partial(narrow_kernel, [place for _, place in pieces], half),
        name="narrow",
        in_specs=[pl.BlockSpec(memory_space=pl.ANY)] * (1 + len(pieces)),
        out_specs=pl.BlockSpec(memory_space=pltpu.VMEM),
        out_shape=jax.ShapeDtypeStruct((rows, width), BF16),
        scratch_shapes=[pltpu.VMEM((rows, depth), BF16)]
        + [pltpu.VMEM(piece.shape, BF16) for piece, _ in pieces]
        + [pltpu.SemaphoreType.DMA, pltpu.SemaphoreType.DMA((len(pieces),))],
        compiler_params=pltpu.CompilerParams(vmem_limit_bytes=VMEM_LIMIT),
        cost_estimate=cost(1000, 1000),
    )(hidden, *[piece for piece, _ in pieces])


def shifted(value, steps):
    count = lax.axis_size("seq")
    return lax.ppermute(value, "seq", [(i, i + steps) for i in range(count - steps)])


def swapped(value, axis, flip):
    count = lax.axis_size(axis)
    return lax.ppermute(value, axis, [(i, i ^ flip) for i in range(count)])


def after(value, *others):
    return lax.optimization_barrier((value, *others))[0]


def on_device(
    tokens, attention_gain, project_weight, conv_weight, decay_down, decay_up, decay_bias,
    output_gate, head_gain, output_weight, mixer_gain, gate_weight, up_weight, down_weight,
    prompt_pages, prompt_start,
):
    count, width = tokens.shape
    prompts = (prompt_pages, prompt_start)
    two_by_two = lax.axis_size("req") == 4 and lax.axis_size("seq") % 2 == 0
    hid_index = lax.axis_index("hid")
    x, y = functools.partial(swapped, axis="req", flip=1), functools.partial(swapped, axis="req", flip=2)
    z = functools.partial(swapped, axis="seq", flip=1)
    depth = gate_weight.shape[0]
    half = depth // 2

    if two_by_two:
        parity = lax.rem(lax.axis_index("seq"), 2)
        up_mine = lax.dynamic_slice_in_dim(up_weight, parity * half, half, 0)
        up_a, up_b = x(up_mine), y(up_mine)
        gate_a, gate_b = x(gate_weight), y(gate_weight)
        down_mine = lax.dynamic_slice_in_dim(down_weight, parity * half, half, 1)
        down_rest = lax.dynamic_slice_in_dim(down_weight, (1 - parity) * half, half, 1)
    rim = shifted(tokens[-RIM:], 1)
    both_output = lax.all_gather(output_weight, "hid", axis=0, tiled=True)

    raised, lowered, weighted, value, ends, edges, opening, state = front(
        prompts, tokens, rim, attention_gain[None], project_weight, output_gate, decay_down.T,
        decay_up, decay_bias[None], conv_weight,
    )
    one, two, three = (shifted(state, i) for i in (1, 2, 3))
    if two_by_two:
        one, two, three, up_a, up_b, gate_a, gate_b = lax.optimization_barrier(
            (one, two, three, up_a, up_b, gate_a, gate_b)
        )
        up_c, down_a = y(up_a), x(down_mine)
        far_a, far_b = z(up_a), z(up_b)
        gate_c = x(gate_b)
    states, *gated = pages(
        prompts, raised, lowered, weighted, value, ends, opening, head_gain[None], one, two, three,
    )
    others = [swapped(part, "hid", 1) for part in gated]
    if two_by_two:
        others, up_c, down_a, far_a = lax.optimization_barrier((others, up_c, down_a, far_a))
        down_b_rest = y(down_rest)
        far_c = z(up_c)
        down_c = y(down_a)
        down_a_far = z(down_a)
    residual, feed = mix(tokens, gated, others, both_output, mixer_gain[None])

    if two_by_two:
        feed, far_b, far_c, gate_c, down_b_rest = lax.optimization_barrier(
            (feed, far_b, far_c, gate_c, down_b_rest)
        )
        down_c_rest = x(down_b_rest)
        down_b = y(down_mine)
        at = lambda flip, more=0: lambda: (lax.axis_index("req") ^ flip) * depth + more
        own = lambda flip: lambda: at(flip)() + lax.rem(lax.axis_index("seq"), 2) * half
        far = lambda flip: lambda: at(flip)() + (1 - lax.rem(lax.axis_index("seq"), 2)) * half
        gate_list = [(gate_weight, at(0)), (gate_a, at(1)), (gate_b, at(2)), (gate_c, at(3))]
        up_list = [
            (up_weight, at(0)), (up_a, own(1)), (far_a, far(1)), (up_b, own(2)), (far_b, far(2)),
            (up_c, own(3)), (far_c, far(3)),
        ]
        down_list = [
            (down_weight, at(0)), (down_a, own(1)), (down_b_rest, far(2)), (down_c, own(3)),
            (down_a_far, far(1)), (down_b, own(2)), (down_c_rest, far(3)),
        ]
    else:
        first = lambda: 0
        gate_list = [(lax.all_gather(gate_weight, "req", axis=0, tiled=True), first)]
        up_list = [(lax.all_gather(up_weight, "req", axis=0, tiled=True), first)]
        down_list = [(lax.all_gather(down_weight, "req", axis=1, tiled=True), first)]

    hidden = widen(feed, (gate_list, up_list))
    theirs_sum = narrow(hidden, lambda: 1 - lax.axis_index("hid"), down_list, width)
    received = swapped(theirs_sum, "hid", 1)
    own_sum = narrow(hidden, lambda: lax.axis_index("hid"), down_list, width)
    own_rows = lax.dynamic_slice_in_dim(residual, hid_index * (count // 2), count // 2, 0)
    result = (
        own_rows.astype(F32) + (own_sum.astype(F32) + received.astype(F32))
    ).astype(BF16)
    return result, states, edges


def solution(mesh):
    return jax.shard_map(
        on_device,
        mesh=mesh,
        in_specs=(
            P(("req", "seq"), None),
            P(),
            P(None, "hid"),
            P(None, "hid"),
            P(),
            P(None, "hid"),
            P("hid"),
            P(None, "hid"),
            P(),
            P("hid", None),
            P(),
            P("req", "hid"),
            P("req", "hid"),
            P("hid", "req"),
            P("req", None),
            P("req", None),
        ),
        out_specs=(
            P(("req", "seq", "hid"), None),
            P(("req", "seq"), "hid", None, None),
            P(("req", "seq"), None, "hid"),
        ),
        check_vma=False,
    )
```

```python
import functools

import jax
import jax.numpy as jnp
from jax import lax
from jax.experimental import pallas as pl
from jax.experimental.pallas import tpu as pltpu
from jax.sharding import PartitionSpec as P

HK = 256
HV = 512
KCONV = 4
PAGE = 64
CONVW = 1024
EPSILON = 1e-06
TILE = 256
PAGES_T = TILE // PAGE
RIM = 16
BF16 = jnp.bfloat16
F32 = jnp.float32
VMEM_LIMIT = 56 * 1024 * 1024
WIDE = 256


def params():
    return pltpu.CompilerParams(
        dimension_semantics=("arbitrary",), vmem_limit_bytes=VMEM_LIMIT
    )


def cost(flops, moved):
    return pl.CostEstimate(flops=flops, bytes_accessed=moved, transcendentals=0)


def fixed(shape):
    return pl.BlockSpec(
        shape, lambda *_: (0,) * len(shape), pipeline_mode=pl.Buffered(1)
    )


def whole_smem():
    return pl.BlockSpec(memory_space=pltpu.SMEM)


def dot(a, b):
    return jnp.dot(a, b, preferred_element_type=F32)


def dot_nt(a, b):
    return lax.dot_general(a, b, (((1,), (1,)), ((), ())), preferred_element_type=F32)


def dot_tn(a, b):
    return lax.dot_general(a, b, (((0,), (0,)), ((), ())), preferred_element_type=F32)


def silu(x):
    return x / (1.0 + jnp.exp(-x))


def column(row):
    return jnp.transpose(jnp.broadcast_to(row, (128, row.shape[1])))[:, :1]


def normalised(x, gain):
    return x * lax.rsqrt(jnp.mean(x * x, axis=-1, keepdims=True) + EPSILON) * gain


def carried_flag(pages_ref, start_ref, page):
    page = lax.axis_index("seq") * (pl.num_programs(0) * PAGES_T) + page
    same = jnp.int32(0)
    for i in range(pages_ref.shape[1]):
        first = start_ref[0, i]
        same = jnp.where((page > first) & (page < first + pages_ref[0, i]), 1, same)
    return same.astype(F32)


def front_kernel(
    pages_ref, start_ref, tokens_ref, rim_ref, gain_ref, project_ref, gate_ref, down_ref, up_ref, bias_ref,
    conv_ref, raised_ref, lowered_ref, weighted_ref, value_ref, ends_ref, edges_ref, opening_ref,
    state_ref, carry, state, decay,
):
    step = pl.program_id(0)

    @pl.when(step == 0)
    def _():
        state[...] = jnp.zeros_like(state)
        decay[...] = jnp.ones_like(decay)

    gain = gain_ref[...].astype(F32)
    rows = jnp.concatenate([tokens_ref[...], rim_ref[...]], axis=0).astype(F32)
    normed_all = normalised(rows, gain).astype(BF16)
    normed = normed_all[:TILE]
    projected_low = dot(normed_all, project_ref[...]).astype(BF16)
    projected = projected_low[:TILE].astype(F32)
    rim = projected_low[TILE:].astype(F32)[RIM - 8 :]
    previous = jnp.where(step == 0, rim, carry[...])
    carry[...] = projected[TILE - 8 :]
    opening_ref[...] = silu(dot(normed, gate_ref[...])).astype(BF16)

    lowrank = dot_nt(normed, down_ref[...]).astype(BF16)
    logits = dot(lowrank, up_ref[...]) + bias_ref[...]
    decay_log = (jnp.minimum(logits, 0.0) - jnp.log1p(jnp.exp(-jnp.abs(logits)))) / 16.0
    row = lax.broadcasted_iota(jnp.int32, (TILE, TILE), 0)
    col = lax.broadcasted_iota(jnp.int32, (TILE, TILE), 1)
    lower = jnp.where((row >= col) & ((row // PAGE) == (col // PAGE)), 1.0, 0.0).astype(F32)
    sums = jnp.dot(lower, decay_log, preferred_element_type=F32, precision=lax.Precision.HIGHEST)

    taps = conv_ref[...].astype(F32)
    suffix = jnp.ones((1, HK), F32)
    pieces = [None] * PAGES_T
    for j in reversed(range(PAGES_T)):
        carried = carried_flag(pages_ref, start_ref, step * PAGES_T + j)
        now = projected[j * PAGE : (j + 1) * PAGE]
        before = previous if j == 0 else projected[j * PAGE - 8 : j * PAGE]
        widened = jnp.concatenate([before * carried, now], axis=0)
        mixed = taps[0:1] * now
        for i in range(1, KCONV):
            mixed = mixed + taps[i : i + 1] * widened[8 - i : 8 - i + PAGE]
        query = silu(mixed[:, :HK])
        key = silu(mixed[:, HK : 2 * HK]) * HK ** (-0.5)
        value = mixed[:, 2 * HK :].astype(BF16)
        sums_j = sums[j * PAGE : (j + 1) * PAGE]
        end = sums_j[PAGE - 1 :]
        weighted = key * jnp.exp(end - sums_j)
        span = pl.ds(j * PAGE, PAGE)
        raised_ref[span, :] = (query * jnp.exp(sums_j)).astype(BF16)
        lowered_ref[span, :] = (key * jnp.exp(-sums_j)).astype(BF16)
        weighted_ref[span, :] = weighted.astype(BF16)
        value_ref[span, :] = value
        kept = jnp.exp(end)
        ends_ref[j] = jnp.broadcast_to(kept, (8, HK))
        edges_ref[j] = projected_low[(j + 1) * PAGE - (KCONV - 1) : (j + 1) * PAGE]
        pieces[j] = ((weighted * suffix).astype(BF16), value)
        suffix = suffix * (kept * carried)
    keys = jnp.concatenate([p[0] for p in pieces], axis=0)
    values = jnp.concatenate([p[1] for p in pieces], axis=0)
    state[...] = column(suffix) * state[...] + dot_tn(keys, values)
    decay[...] = decay[...] * suffix

    @pl.when(step == pl.num_programs(0) - 1)
    def _():
        state_ref[:HK] = state[...].astype(BF16)
        block = jnp.concatenate([decay[...]] * (HV // HK), axis=1)
        state_ref[HK:] = jnp.concatenate([block] * (RIM // 8), axis=0).astype(BF16)


def front(prompts, tokens, rim, gain, project, gate, down, up, bias, conv):
    count, width = tokens.shape
    rank = down.shape[0]
    pages = count // PAGE
    rows = lambda n: pl.BlockSpec((TILE, n), lambda i: (i, 0))
    shape = jax.ShapeDtypeStruct
    return pl.pallas_call(
        front_kernel,
        name="front",
        grid=(count // TILE,),
        in_specs=[
            whole_smem(), whole_smem(), rows(width), fixed((RIM, width)), fixed((1, width)),
            fixed((width, CONVW)), fixed((width, HV)), fixed((rank, width)), fixed((rank, HK)),
            fixed((1, HK)), fixed((KCONV, CONVW)),
        ],
        out_specs=[
            rows(HK), rows(HK), rows(HK), rows(HV),
            pl.BlockSpec((PAGES_T, 8, HK), lambda i: (i, 0, 0)),
            pl.BlockSpec((PAGES_T, KCONV - 1, CONVW), lambda i: (i, 0, 0)),
            rows(HV), fixed((HK + RIM, HV)),
        ],
        out_shape=[
            shape((count, HK), BF16), shape((count, HK), BF16), shape((count, HK), BF16),
            shape((count, HV), BF16), shape((pages, 8, HK), F32),
            shape((pages, KCONV - 1, CONVW), BF16), shape((count, HV), BF16),
            shape((HK + RIM, HV), BF16),
        ],
        scratch_shapes=[
            pltpu.VMEM((8, CONVW), F32), pltpu.VMEM((HK, HV), F32), pltpu.VMEM((8, HK), F32)
        ],
        compiler_params=params(),
        cost_estimate=cost(1000, 1000),
    )(*prompts, tokens, rim, gain, project, gate, down, up, bias, conv)


def composed(later, earlier):
    kept = column(later[HK:].astype(F32)[:1, :HK])
    return later[:HK].astype(F32) + kept * earlier[:HK].astype(F32)


def joined_kernel(later_ref, earlier_ref, out_ref):
    out_ref[:HK] = composed(later_ref, earlier_ref).astype(BF16)
    out_ref[HK:] = later_ref[HK:]


def joined(later, earlier):
    return pl.pallas_call(
        joined_kernel, name="joined",
        in_specs=[pl.BlockSpec(memory_space=pltpu.VMEM)] * 2,
        out_specs=pl.BlockSpec(memory_space=pltpu.VMEM),
        out_shape=jax.ShapeDtypeStruct(later.shape, BF16),
        cost_estimate=cost(1000, 1000),
    )(later, earlier)


def halves(count):
    half = count // TILE // 2
    return [
        pl.BlockSpec((TILE, HV), lambda i: (jnp.minimum(i, half - 1), 0)),
        pl.BlockSpec((TILE, HV), lambda i: (jnp.maximum(i - half, 0), 0)),
    ]


def pages_kernel(
    pages_ref, start_ref, raised_ref, lowered_ref, weighted_ref, value_ref, ends_ref, opening_ref, gain_ref,
    one_ref, two_ref, states_ref, low_ref, high_ref, memory,
):
    step = pl.program_id(0)

    @pl.when(step == 0)
    def _():
        memory[...] = composed(one_ref, two_ref)

    row = lax.broadcasted_iota(jnp.int32, (PAGE, PAGE), 0)
    col = lax.broadcasted_iota(jnp.int32, (PAGE, PAGE), 1)
    gain = gain_ref[...].astype(F32)
    held = memory[...]
    gated_tile = []
    for j in range(PAGES_T):
        span = pl.ds(j * PAGE, PAGE)
        raised, value = raised_ref[span, :], value_ref[span, :]
        held = held * carried_flag(pages_ref, start_ref, step * PAGES_T + j)
        scores = dot_nt(raised, lowered_ref[span, :])
        scores = jnp.where(row >= col, scores, 0.0).astype(BF16)
        attended = dot(scores, value) + dot(raised, held.astype(BF16))
        held = column(ends_ref[j][:1]) * held + dot_tn(weighted_ref[span, :], value)
        states_ref[j, 0] = held.astype(BF16)
        gated = normalised(attended, gain) * opening_ref[span, :].astype(F32)
        gated_tile.append(gated.astype(BF16))
    memory[...] = held
    half = pl.num_programs(0) // 2

    @pl.when(step < half)
    def _():
        low_ref[...] = jnp.concatenate(gated_tile, axis=0)

    @pl.when(step >= half)
    def _():
        high_ref[...] = jnp.concatenate(gated_tile, axis=0)


def pages(prompts, raised, lowered, weighted, value, ends, opening, gain, one, two):
    count = raised.shape[0]
    total = count // PAGE
    rows = lambda n: pl.BlockSpec((TILE, n), lambda i: (i, 0))
    return pl.pallas_call(
        pages_kernel,
        name="pages",
        grid=(count // TILE,),
        in_specs=[
            whole_smem(), whole_smem(), rows(HK), rows(HK), rows(HK), rows(HV),
            pl.BlockSpec((PAGES_T, 8, HK), lambda i: (i, 0, 0)), rows(HV), fixed((1, HV)),
            fixed((HK + RIM, HV)), fixed((HK + RIM, HV)),
        ],
        out_specs=[
            pl.BlockSpec((PAGES_T, 1, HK, HV), lambda i: (i, 0, 0, 0)), *halves(count),
        ],
        out_shape=[
            jax.ShapeDtypeStruct((total, 1, HK, HV), BF16),
            jax.ShapeDtypeStruct((count // 2, HV), BF16),
            jax.ShapeDtypeStruct((count // 2, HV), BF16),
        ],
        scratch_shapes=[pltpu.VMEM((HK, HV), F32)],
        compiler_params=params(),
        cost_estimate=cost(1000, 1000),
    )(*prompts, raised, lowered, weighted, value, ends, opening, gain, one, two)


def mix_kernel(tokens_ref, low_ref, high_ref, other_low_ref, other_high_ref, weight_ref, gain_ref, residual_ref, feed_ref):
    step, half = pl.program_id(0), pl.num_programs(0) // 2
    own = jnp.where(step < half, low_ref[...], high_ref[...])
    other = jnp.where(step < half, other_low_ref[...], other_high_ref[...])
    mine = lax.axis_index("hid")
    rows = lambda head: pl.ds(pl.multiple_of(head * HV, HV), HV)
    mixed = dot(own, weight_ref[rows(mine), :]) + dot(other, weight_ref[rows(1 - mine), :])
    residual = (tokens_ref[...].astype(F32) + mixed).astype(BF16)
    residual_ref[...] = residual
    feed_ref[...] = normalised(residual.astype(F32), gain_ref[...].astype(F32)).astype(BF16)


def mix(tokens, own, others, weight, gain):
    count, width = tokens.shape
    rows = lambda n: pl.BlockSpec((TILE, n), lambda i: (i, 0))
    return pl.pallas_call(
        mix_kernel,
        name="mix",
        grid=(count // TILE,),
        in_specs=[
            rows(width), *halves(count), *halves(count), fixed(weight.shape), fixed((1, width)),
        ],
        out_specs=[rows(width), rows(width)],
        out_shape=[jax.ShapeDtypeStruct((count, width), BF16)] * 2,
        compiler_params=params(),
        cost_estimate=cost(1000, 1000),
    )(tokens, *own, *others, weight, gain)


def widen_kernel(places, feed_ref, *refs):
    pieces, out_ref = refs[:-1], refs[-1]
    sums = [None, None]
    for (matrix, place), ref in zip(places, pieces):
        columns = pl.ds(pl.multiple_of(place(), 128), ref.shape[0])
        part = dot(feed_ref[:, columns], ref[...])
        sums[matrix] = part if sums[matrix] is None else sums[matrix] + part
    out_ref[...] = (silu(sums[0]) * sums[1]).astype(BF16)


def widen(feed, matrices):
    count, width = feed.shape
    pieces = [piece for matrix in matrices for piece, _ in matrix]
    places = [(i, place) for i, matrix in enumerate(matrices) for _, place in matrix]
    hidden = pieces[0].shape[1]
    return pl.pallas_call(
        functools.partial(widen_kernel, places),
        name="widen",
        grid=(pl.cdiv(hidden, WIDE),),
        in_specs=[fixed((count, width))]
        + [pl.BlockSpec((piece.shape[0], WIDE), lambda i: (0, i)) for piece in pieces],
        out_specs=pl.BlockSpec((count, WIDE), lambda i: (0, i)),
        out_shape=jax.ShapeDtypeStruct((count, hidden), BF16),
        compiler_params=params(),
        cost_estimate=cost(1000, 1000),
    )(feed, *pieces)


def narrow_kernel(hidden_hbm, *refs):
    count = (len(refs) - 5) // 2
    pieces, theirs_ref, own_ref, hidden = refs[:count], *refs[count : count + 3]
    weights, sem, sems = refs[count + 3 : -2], refs[-2], refs[-1]
    rows = hidden.shape[0] // 2
    mine = lax.axis_index("hid")
    wholes = [
        pltpu.make_async_copy(
            hidden_hbm.at[pl.ds(pl.multiple_of(half * rows, rows), rows), :],
            hidden.at[pl.ds(i * rows, rows), :],
            sem.at[i],
        )
        for i, half in enumerate((1 - mine, mine))
    ]
    copies = [
        pltpu.make_async_copy(ref, weight, sems.at[i])
        for i, (ref, weight) in enumerate(zip(pieces, weights))
    ]
    for copy in wholes + copies:
        copy.start()
    for copy in wholes:
        copy.wait()
    depth = hidden.shape[1]
    at = 0
    for copy, weight in zip(copies, weights):
        copy.wait()
        for low in range(0, weight.shape[1], WIDE):
            total = None
            for k in range(0, depth, WIDE):
                span = pl.ds(k, min(WIDE, depth - k))
                part = dot(hidden[:, span], weight[span, pl.ds(low, WIDE)])
                total = part if total is None else total + part
            columns = pl.ds(at, WIDE)
            theirs_ref[:, columns] = total[:rows].astype(BF16)
            own_ref[:, columns] = total[rows:].astype(BF16)
            at += WIDE


def narrow(hidden, pieces):
    count, depth = hidden.shape
    width = sum(piece.shape[1] for piece in pieces)
    return pl.pallas_call(
        narrow_kernel,
        name="narrow",
        in_specs=[pl.BlockSpec(memory_space=pl.ANY)] * (1 + len(pieces)),
        out_specs=[pl.BlockSpec(memory_space=pltpu.VMEM)] * 2,
        out_shape=[jax.ShapeDtypeStruct((count // 2, width), BF16)] * 2,
        scratch_shapes=[pltpu.VMEM((count, depth), BF16)]
        + [pltpu.VMEM(piece.shape, BF16) for piece in pieces]
        + [pltpu.SemaphoreType.DMA((2,)), pltpu.SemaphoreType.DMA((len(pieces),))],
        compiler_params=pltpu.CompilerParams(vmem_limit_bytes=VMEM_LIMIT),
        cost_estimate=cost(1000, 1000),
    )(hidden, *pieces)


def close_kernel(places, residual_ref, *refs):
    out_ref = refs[-1]
    for group, (own_ref, received_ref) in zip(places, zip(refs[:-1:2], refs[1:-1:2])):
        at = 0
        for size, place in group:
            columns, span = pl.ds(pl.multiple_of(place(), 128), size), pl.ds(at, size)
            total = own_ref[:, span].astype(F32) + received_ref[:, span].astype(F32)
            out_ref[:, columns] = (residual_ref[:, columns].astype(F32) + total).astype(BF16)
            at += size


def close(hid_index, residual, groups):
    count, width = residual.shape
    tiles = count // TILE // 2
    rows = lambda n: pl.BlockSpec((TILE, n), lambda i, s: (i, 0))
    arrays = [array for own, received, _ in groups for array in (own, received)]
    return pl.pallas_call(
        functools.partial(close_kernel_, [group[2] for group in groups]),
        name="close",
        grid_spec=pltpu.PrefetchScalarGridSpec(
            num_scalar_prefetch=1,
            grid=(tiles,),
            in_specs=[pl.BlockSpec((TILE, width), lambda i, s: (s[0] * tiles + i, 0))]
            + [rows(array.shape[1]) for array in arrays],
            out_specs=rows(width),
        ),
        out_shape=jax.ShapeDtypeStruct((count // 2, width), BF16),
        compiler_params=params(),
        cost_estimate=cost(1000, 1000),
    )(hid_index.astype(jnp.int32)[None], residual, *arrays)


def close_kernel_(places, half_ref, *refs):
    close_kernel(places, *refs)


def shifted(value, steps):
    count = lax.axis_size("seq")
    return lax.ppermute(value, "seq", [(i, i + steps) for i in range(count - steps)])


def swapped(value, axis, flip):
    count = lax.axis_size(axis)
    return lax.ppermute(value, axis, [(i, i ^ flip) for i in range(count)])


def after(value, *others):
    return lax.optimization_barrier((value, *others))[0]


def on_device(
    tokens, attention_gain, project_weight, conv_weight, decay_down, decay_up, decay_bias,
    output_gate, head_gain, output_weight, mixer_gain, gate_weight, up_weight, down_weight,
    prompt_pages, prompt_start,
):
    count, width = tokens.shape
    prompts = (prompt_pages, prompt_start)
    two_by_two = lax.axis_size("req") == 4 and lax.axis_size("seq") % 2 == 0
    hid_index = lax.axis_index("hid")
    x, y = functools.partial(swapped, axis="req", flip=1), functools.partial(swapped, axis="req", flip=2)
    z = functools.partial(swapped, axis="seq", flip=1)
    depth = gate_weight.shape[0]
    half = depth // 2

    tied = lax.optimization_barrier
    if two_by_two:
        parity = lax.rem(lax.axis_index("seq"), 2)
        up_mine = lax.dynamic_slice_in_dim(up_weight, parity * half, half, 0)
        up_a, up_b = x(up_mine), y(up_mine)
        gate_a, gate_b = x(gate_weight), y(gate_weight)
    rim = shifted(tokens[-RIM:], 1)
    both_output = lax.all_gather(output_weight, "hid", axis=0, tiled=True)

    raised, lowered, weighted, value, ends, edges, opening, state = front(
        prompts, tokens, rim, attention_gain[None], project_weight, output_gate, decay_down.T,
        decay_up, decay_bias[None], conv_weight,
    )
    if two_by_two:
        state, gate_a, gate_b = tied((state, gate_a, gate_b))
        down_0, down_1 = down_weight[:, :half], down_weight[:, half:]
        gate_c, down_b1 = x(gate_b), y(down_1)
    one = shifted(state, 1)
    two = shifted(joined(state, one), 2)
    if two_by_two:
        one, two, up_a, up_b, down_0 = tied((one, two, up_a, up_b, down_0))
        up_c, far_a, far_b, down_a0 = y(up_a), z(up_a), z(up_b), x(down_0)
        down_c0 = y(down_a0)
    states, *gated = pages(
        prompts, raised, lowered, weighted, value, ends, opening, head_gain[None], one, two,
    )
    others = [swapped(part, "hid", 1) for part in gated]
    if two_by_two:
        others, up_c, gate_c, far_a, down_b1 = tied((others, up_c, gate_c, far_a, down_b1))
        far_c = y(far_a)
    residual, feed = mix(tokens, gated, others, both_output, mixer_gain[None])

    if two_by_two:
        feed, down_0, down_1 = tied((feed, down_0, down_1))
        down_b0, down_a1 = y(down_0), x(down_1)
        feed, far_b, far_c, down_b1 = tied((feed, far_b, far_c, down_b1))
        down_c1 = x(down_b1)
        at = lambda flip, more=0: lambda: (lax.axis_index("req") ^ flip) * depth + more
        own = lambda flip: lambda: at(flip)() + lax.rem(lax.axis_index("seq"), 2) * half
        far = lambda flip: lambda: at(flip)() + (1 - lax.rem(lax.axis_index("seq"), 2)) * half
        gate_list = [(gate_weight, at(0)), (gate_a, at(1)), (gate_b, at(2)), (gate_c, at(3))]
        up_list = [
            (up_weight, at(0)), (up_a, own(1)), (far_a, far(1)), (up_b, own(2)), (far_b, far(2)),
            (up_c, own(3)), (far_c, far(3)),
        ]
        down_lists = [
            [(down_weight, at(0)), (down_a0, at(1)), (down_b1, at(2, half)), (down_b0, at(2))],
            [(down_a1, at(1, half)), (down_c0, at(3)), (down_c1, at(3, half))],
        ]
    else:
        first = lambda: 0
        gate_list = [(lax.all_gather(gate_weight, "req", axis=0, tiled=True), first)]
        up_list = [(lax.all_gather(up_weight, "req", axis=0, tiled=True), first)]
        down_lists = [[(lax.all_gather(down_weight, "req", axis=1, tiled=True), first)]]

    hidden = widen(feed, (gate_list, up_list))
    groups = []
    for pieces in down_lists:
        theirs, mine = narrow(hidden, [piece for piece, _ in pieces])
        received = swapped(theirs, "hid", 1)
        groups.append((mine, received, [(piece.shape[1], place) for piece, place in pieces]))
    result = close(hid_index, residual, groups)
    return result, states, edges


def solution(mesh):
    return jax.shard_map(
        on_device,
        mesh=mesh,
        in_specs=(
            P(("req", "seq"), None),
            P(),
            P(None, "hid"),
            P(None, "hid"),
            P(),
            P(None, "hid"),
            P("hid"),
            P(None, "hid"),
            P(),
            P("hid", None),
            P(),
            P("req", "hid"),
            P("req", "hid"),
            P("hid", "req"),
            P("req", None),
            P("req", None),
        ),
        out_specs=(
            P(("req", "seq", "hid"), None),
            P(("req", "seq"), "hid", None, None),
            P(("req", "seq"), None, "hid"),
        ),
        check_vma=False,
    )
```

```python
import functools

import jax
import jax.numpy as jnp
from jax import lax
from jax.experimental import pallas as pl
from jax.experimental.pallas import tpu as pltpu
from jax.sharding import PartitionSpec as P

HK = 256
HV = 512
KCONV = 4
PAGE = 64
CONVW = 1024
EPSILON = 1e-06
TILE = 256
PAGES_T = TILE // PAGE
RIM = 16
BF16 = jnp.bfloat16
F32 = jnp.float32
VMEM_LIMIT = 56 * 1024 * 1024
WIDE = 256
FRONT = 512
MIX = 256


def params():
    return pltpu.CompilerParams(
        dimension_semantics=("arbitrary",), vmem_limit_bytes=VMEM_LIMIT
    )


def cost(flops, moved):
    return pl.CostEstimate(flops=flops, bytes_accessed=moved, transcendentals=0)


def fixed(shape):
    return pl.BlockSpec(
        shape, lambda *_: (0,) * len(shape), pipeline_mode=pl.Buffered(1)
    )


def whole_smem():
    return pl.BlockSpec(memory_space=pltpu.SMEM)


def dot(a, b):
    return jnp.dot(a, b, preferred_element_type=F32)


def dot_nt(a, b):
    return lax.dot_general(a, b, (((1,), (1,)), ((), ())), preferred_element_type=F32)


def dot_tn(a, b):
    return lax.dot_general(a, b, (((0,), (0,)), ((), ())), preferred_element_type=F32)


def silu(x):
    return x / (1.0 + jnp.exp(-x))


def column(row):
    return jnp.transpose(jnp.broadcast_to(row, (128, row.shape[1])))[:, :1]


def normalised(x, gain):
    return x * lax.rsqrt(jnp.mean(x * x, axis=-1, keepdims=True) + EPSILON) * gain


def carried_flag(pages_ref, start_ref, page, count):
    page = lax.axis_index("seq") * count + page
    same = jnp.int32(0)
    for i in range(pages_ref.shape[1]):
        first = start_ref[0, i]
        same = jnp.where((page > first) & (page < first + pages_ref[0, i]), 1, same)
    return same.astype(F32)


def product(left, rows, weight_ref, columns, step=512):
    depth = weight_ref.shape[0]
    total = None
    for k in range(0, depth, step):
        span = pl.ds(k, min(step, depth - k))
        part = dot(left[rows, span], weight_ref[span, columns])
        total = part if total is None else total + part
    return total


def rms_columns(read, write, gain_ref, width):
    total = None
    for low in range(0, width, WIDE):
        x = read(pl.ds(low, WIDE))
        square = x * x
        part = square[:, : WIDE // 2] + square[:, WIDE // 2 :]
        total = part if total is None else total + part
    scale = lax.rsqrt(jnp.sum(total, axis=-1, keepdims=True) * (1.0 / width) + EPSILON)
    for low in range(0, width, WIDE):
        columns = pl.ds(low, WIDE)
        write(columns, read(columns) * scale * gain_ref[:, columns].astype(F32))


def front_kernel(
    pages_ref, start_ref, tokens_ref, rim_ref, gain_ref, project_ref, gate_ref, down_ref, up_ref, bias_ref,
    conv_ref, raised_ref, lowered_ref, weighted_ref, value_ref, ends_ref, edges_ref, opening_ref,
    state_ref, normed, carry, state, decay, keys,
):
    step = pl.program_id(0)
    tile, width = tokens_ref.shape
    pages = tile // PAGE

    @pl.when(step == 0)
    def _():
        state[...] = jnp.zeros_like(state)
        decay[...] = jnp.ones_like(decay)

    blocks = [(rim_ref, 0, tile, RIM)] + [(tokens_ref, r, r, 128) for r in range(0, tile, 128)]
    for ref, source, target, count in blocks:
        def write(columns, x, target=target, count=count):
            normed[pl.ds(target, count), columns] = x.astype(BF16)
        rms_columns(
            lambda columns, ref=ref, source=source, count=count: ref[pl.ds(source, count), columns].astype(F32),
            write, gain_ref, width,
        )

    lowrank = dot_nt(normed[:tile], down_ref[...]).astype(BF16)
    logits = dot(lowrank, up_ref[...]) + bias_ref[...]
    decay_log = (jnp.minimum(logits, 0.0) - jnp.log1p(jnp.exp(-jnp.abs(logits)))) / 16.0
    row = lax.broadcasted_iota(jnp.int32, (HK, HK), 0)
    col = lax.broadcasted_iota(jnp.int32, (HK, HK), 1)
    lower = jnp.where((row >= col) & ((row // PAGE) == (col // PAGE)), 1.0, 0.0).astype(F32)
    sums = [
        jnp.dot(lower, decay_log[r : r + HK], preferred_element_type=F32, precision=lax.Precision.HIGHEST)
        for r in range(0, tile, HK)
    ]
    sums = [part[r : r + PAGE] for part in sums for r in range(0, HK, PAGE)]
    ends = [part[PAGE - 1 :] for part in sums]
    carried = [carried_flag(pages_ref, start_ref, step * pages + j, pl.num_programs(0) * pages) for j in range(pages)]
    suffix = [None] * pages + [jnp.ones((1, HK), F32)]
    for j in reversed(range(pages)):
        kept = jnp.exp(ends[j])
        ends_ref[j] = jnp.broadcast_to(kept, (8, HK))
        suffix[j] = suffix[j + 1] * (kept * carried[j])

    everything = slice(None)
    for chunk in (1, 2, 3, 0):
        columns = pl.ds(chunk * WIDE, WIDE)
        low = product(normed, everything, project_ref, columns).astype(BF16)
        projected = low[:tile].astype(F32)
        previous = jnp.where(step == 0, low[tile:].astype(F32)[RIM - 8 :], carry[:, columns])
        carry[:, columns] = projected[tile - 8 :]
        taps = conv_ref[:, columns].astype(F32)
        for j in range(pages):
            now = projected[j * PAGE : (j + 1) * PAGE]
            before = previous if j == 0 else projected[j * PAGE - 8 : j * PAGE]
            widened = jnp.concatenate([before * carried[j], now], axis=0)
            mixed = taps[0:1] * now
            for i in range(1, KCONV):
                mixed = mixed + taps[i : i + 1] * widened[8 - i : 8 - i + PAGE]
            span = pl.ds(j * PAGE, PAGE)
            edges_ref[j, :, columns] = low[(j + 1) * PAGE - (KCONV - 1) : (j + 1) * PAGE]
            if chunk == 0:
                raised_ref[span, :] = (silu(mixed) * jnp.exp(sums[j])).astype(BF16)
            elif chunk == 1:
                key = silu(mixed) * HK ** (-0.5)
                weighted = key * jnp.exp(ends[j] - sums[j])
                lowered_ref[span, :] = (key * jnp.exp(-sums[j])).astype(BF16)
                weighted_ref[span, :] = weighted.astype(BF16)
                keys[span, :] = (weighted * suffix[j + 1]).astype(BF16)
            else:
                at = pl.ds((chunk - 2) * WIDE, WIDE)
                value_ref[span, at] = mixed.astype(BF16)
    state[...] = column(suffix[0]) * state[...] + dot_tn(keys[...], value_ref[...])
    decay[...] = decay[...] * suffix[0]
    for low in range(0, HV, WIDE):
        columns = pl.ds(low, WIDE)
        opening_ref[:, columns] = silu(product(normed, pl.ds(0, tile), gate_ref, columns)).astype(BF16)

    @pl.when(step == pl.num_programs(0) - 1)
    def _():
        state_ref[:HK] = state[...].astype(BF16)
        block = jnp.concatenate([decay[...]] * (HV // HK), axis=1)
        state_ref[HK:] = jnp.concatenate([block] * (RIM // 8), axis=0).astype(BF16)


def front(prompts, tokens, rim, gain, project, gate, down, up, bias, conv):
    count, width = tokens.shape
    rank = down.shape[0]
    pages = count // PAGE
    tile = FRONT
    rows = lambda n: pl.BlockSpec((tile, n), lambda i: (i, 0))
    shape = jax.ShapeDtypeStruct
    return pl.pallas_call(
        front_kernel,
        name="front",
        grid=(count // tile,),
        in_specs=[
            whole_smem(), whole_smem(), rows(width), fixed((RIM, width)), fixed((1, width)),
            fixed((width, CONVW)), fixed((width, HV)), fixed((rank, width)), fixed((rank, HK)),
            fixed((1, HK)), fixed((KCONV, CONVW)),
        ],
        out_specs=[
            rows(HK), rows(HK), rows(HK), rows(HV),
            pl.BlockSpec((tile // PAGE, 8, HK), lambda i: (i, 0, 0)),
            pl.BlockSpec((tile // PAGE, KCONV - 1, CONVW), lambda i: (i, 0, 0)),
            rows(HV), fixed((HK + RIM, HV)),
        ],
        out_shape=[
            shape((count, HK), BF16), shape((count, HK), BF16), shape((count, HK), BF16),
            shape((count, HV), BF16), shape((pages, 8, HK), F32),
            shape((pages, KCONV - 1, CONVW), BF16), shape((count, HV), BF16),
            shape((HK + RIM, HV), BF16),
        ],
        scratch_shapes=[
            pltpu.VMEM((tile + RIM, width), BF16), pltpu.VMEM((8, CONVW), F32),
            pltpu.VMEM((HK, HV), F32), pltpu.VMEM((8, HK), F32), pltpu.VMEM((tile, HK), BF16),
        ],
        compiler_params=params(),
        cost_estimate=cost(1000, 1000),
    )(*prompts, tokens, rim, gain, project, gate, down, up, bias, conv)


def composed(later, earlier):
    kept = column(later[HK:].astype(F32)[:1, :HK])
    return later[:HK].astype(F32) + kept * earlier[:HK].astype(F32)


def joined_kernel(later_ref, earlier_ref, out_ref):
    out_ref[:HK] = composed(later_ref, earlier_ref).astype(BF16)
    out_ref[HK:] = later_ref[HK:]


def joined(later, earlier):
    return pl.pallas_call(
        joined_kernel, name="joined",
        in_specs=[pl.BlockSpec(memory_space=pltpu.VMEM)] * 2,
        out_specs=pl.BlockSpec(memory_space=pltpu.VMEM),
        out_shape=jax.ShapeDtypeStruct(later.shape, BF16),
        cost_estimate=cost(1000, 1000),
    )(later, earlier)


def halves(count, tile):
    half = count // tile // 2
    return [
        pl.BlockSpec((tile, HV), lambda i: (jnp.minimum(i, half - 1), 0)),
        pl.BlockSpec((tile, HV), lambda i: (jnp.maximum(i - half, 0), 0)),
    ]


def pages_kernel(
    pages_ref, start_ref, raised_ref, lowered_ref, weighted_ref, value_ref, ends_ref, opening_ref, gain_ref,
    one_ref, two_ref, states_ref, low_ref, high_ref, memory,
):
    step = pl.program_id(0)

    @pl.when(step == 0)
    def _():
        memory[...] = composed(one_ref, two_ref)

    row = lax.broadcasted_iota(jnp.int32, (PAGE, PAGE), 0)
    col = lax.broadcasted_iota(jnp.int32, (PAGE, PAGE), 1)
    gain = gain_ref[...].astype(F32)
    held = memory[...]
    gated_tile = []
    for j in range(PAGES_T):
        span = pl.ds(j * PAGE, PAGE)
        raised, value = raised_ref[span, :], value_ref[span, :]
        held = held * carried_flag(pages_ref, start_ref, step * PAGES_T + j, pl.num_programs(0) * PAGES_T)
        scores = dot_nt(raised, lowered_ref[span, :])
        scores = jnp.where(row >= col, scores, 0.0).astype(BF16)
        attended = dot(scores, value) + dot(raised, held.astype(BF16))
        held = column(ends_ref[j][:1]) * held + dot_tn(weighted_ref[span, :], value)
        states_ref[j, 0] = held.astype(BF16)
        gated = normalised(attended, gain) * opening_ref[span, :].astype(F32)
        gated_tile.append(gated.astype(BF16))
    memory[...] = held
    half = pl.num_programs(0) // 2

    @pl.when(step < half)
    def _():
        low_ref[...] = jnp.concatenate(gated_tile, axis=0)

    @pl.when(step >= half)
    def _():
        high_ref[...] = jnp.concatenate(gated_tile, axis=0)


def pages(prompts, raised, lowered, weighted, value, ends, opening, gain, one, two):
    count = raised.shape[0]
    total = count // PAGE
    rows = lambda n: pl.BlockSpec((TILE, n), lambda i: (i, 0))
    return pl.pallas_call(
        pages_kernel,
        name="pages",
        grid=(count // TILE,),
        in_specs=[
            whole_smem(), whole_smem(), rows(HK), rows(HK), rows(HK), rows(HV),
            pl.BlockSpec((PAGES_T, 8, HK), lambda i: (i, 0, 0)), rows(HV), fixed((1, HV)),
            fixed((HK + RIM, HV)), fixed((HK + RIM, HV)),
        ],
        out_specs=[
            pl.BlockSpec((PAGES_T, 1, HK, HV), lambda i: (i, 0, 0, 0)), *halves(count, TILE),
        ],
        out_shape=[
            jax.ShapeDtypeStruct((total, 1, HK, HV), BF16),
            jax.ShapeDtypeStruct((count // 2, HV), BF16),
            jax.ShapeDtypeStruct((count // 2, HV), BF16),
        ],
        scratch_shapes=[pltpu.VMEM((HK, HV), F32)],
        compiler_params=params(),
        cost_estimate=cost(1000, 1000),
    )(*prompts, raised, lowered, weighted, value, ends, opening, gain, one, two)


def mix_kernel(
    tokens_ref, low_ref, high_ref, other_low_ref, other_high_ref, own_weight_ref, other_weight_ref,
    gain_ref, residual_ref, feed_ref,
):
    first = pl.program_id(0) < pl.num_programs(0) // 2
    own = jnp.where(first, low_ref[...], high_ref[...])
    other = jnp.where(first, other_low_ref[...], other_high_ref[...])
    width = tokens_ref.shape[1]
    for at in range(0, width, WIDE):
        columns = pl.ds(at, WIDE)
        mixed = dot(own, own_weight_ref[:, columns]) + dot(other, other_weight_ref[:, columns])
        residual_ref[:, columns] = (tokens_ref[:, columns].astype(F32) + mixed).astype(BF16)

    def write(columns, x):
        feed_ref[:, columns] = x.astype(BF16)

    rms_columns(lambda columns: residual_ref[:, columns].astype(F32), write, gain_ref, width)


def mix(tokens, own, others, own_weight, other_weight, gain):
    count, width = tokens.shape
    tile = MIX
    rows = pl.BlockSpec((tile, width), lambda i: (i, 0))
    return pl.pallas_call(
        mix_kernel,
        name="mix",
        grid=(count // tile,),
        in_specs=[
            rows, *halves(count, tile), *halves(count, tile), fixed((HV, width)), fixed((HV, width)),
            fixed((1, width)),
        ],
        out_specs=[rows, rows],
        out_shape=[jax.ShapeDtypeStruct((count, width), BF16)] * 2,
        compiler_params=params(),
        cost_estimate=cost(1000, 1000),
    )(tokens, *own, *others, own_weight, other_weight, gain)


def widen_kernel(places, feed_ref, *refs):
    pieces, out_ref = refs[:-1], refs[-1]
    sums = [None, None]
    for (matrix, place), ref in zip(places, pieces):
        columns = pl.ds(pl.multiple_of(place(), 128), ref.shape[0])
        part = dot(feed_ref[:, columns], ref[...])
        sums[matrix] = part if sums[matrix] is None else sums[matrix] + part
    out_ref[...] = (silu(sums[0]) * sums[1]).astype(BF16)


def widen(feed, matrices):
    count, width = feed.shape
    pieces = [piece for matrix in matrices for piece, _ in matrix]
    places = [(i, place) for i, matrix in enumerate(matrices) for _, place in matrix]
    hidden = pieces[0].shape[1]
    return pl.pallas_call(
        functools.partial(widen_kernel, places),
        name="widen",
        grid=(pl.cdiv(hidden, WIDE),),
        in_specs=[fixed((count, width))]
        + [pl.BlockSpec((piece.shape[0], WIDE), lambda i: (0, i)) for piece in pieces],
        out_specs=pl.BlockSpec((count, WIDE), lambda i: (0, i)),
        out_shape=jax.ShapeDtypeStruct((count, hidden), BF16),
        compiler_params=params(),
        cost_estimate=cost(1000, 1000),
    )(feed, *pieces)


def narrow_kernel(block, hidden_hbm, *refs):
    count = (len(refs) - 5) // 2
    pieces, theirs_ref, own_ref, hidden = refs[:count], *refs[count : count + 3]
    weights, sem, sems = refs[count + 3 : -2], refs[-2], refs[-1]
    rows = hidden.shape[0] // 2
    mine = lax.axis_index("hid")
    wholes = [
        pltpu.make_async_copy(
            hidden_hbm.at[pl.ds(pl.multiple_of(half * rows, rows), rows), :],
            hidden.at[pl.ds(i * rows, rows), :],
            sem.at[i],
        )
        for i, half in enumerate((1 - mine, mine))
    ]
    copies = [
        pltpu.make_async_copy(ref, weight, sems.at[i])
        for i, (ref, weight) in enumerate(zip(pieces, weights))
    ]
    for copy in wholes + copies:
        copy.start()
    for copy in wholes:
        copy.wait()
    at = 0
    for copy, weight in zip(copies, weights):
        copy.wait()
        for low in range(0, weight.shape[1], WIDE):
            for first in range(0, 2 * rows, block):
                total = product(hidden, pl.ds(first, block), weight, pl.ds(low, WIDE)).astype(BF16)
                for out_ref, start in ((theirs_ref, 0), (own_ref, rows)):
                    if first < start + rows and start < first + block:
                        taken = total[max(start - first, 0) : start + rows - first]
                        out_ref[pl.ds(max(first - start, 0), taken.shape[0]), pl.ds(at, WIDE)] = taken
            at += WIDE


def narrow(hidden, pieces, block):
    count, depth = hidden.shape
    width = sum(piece.shape[1] for piece in pieces)
    return pl.pallas_call(
        functools.partial(narrow_kernel, block),
        name="narrow",
        in_specs=[pl.BlockSpec(memory_space=pl.ANY)] * (1 + len(pieces)),
        out_specs=[pl.BlockSpec(memory_space=pltpu.VMEM)] * 2,
        out_shape=[jax.ShapeDtypeStruct((count // 2, width), BF16)] * 2,
        scratch_shapes=[pltpu.VMEM((count, depth), BF16)]
        + [pltpu.VMEM(piece.shape, BF16) for piece in pieces]
        + [pltpu.SemaphoreType.DMA((2,)), pltpu.SemaphoreType.DMA((len(pieces),))],
        compiler_params=pltpu.CompilerParams(vmem_limit_bytes=VMEM_LIMIT),
        cost_estimate=cost(1000, 1000),
    )(hidden, *pieces)


def close_kernel(places, residual_ref, *refs):
    out_ref = refs[-1]
    for group, (own_ref, received_ref) in zip(places, zip(refs[:-1:2], refs[1:-1:2])):
        at = 0
        for size, place in group:
            columns, span = pl.ds(pl.multiple_of(place(), 128), size), pl.ds(at, size)
            total = own_ref[:, span].astype(F32) + received_ref[:, span].astype(F32)
            out_ref[:, columns] = (residual_ref[:, columns].astype(F32) + total).astype(BF16)
            at += size


def close(hid_index, residual, groups):
    count, width = residual.shape
    tiles = count // TILE // 2
    rows = lambda n: pl.BlockSpec((TILE, n), lambda i, s: (i, 0))
    arrays = [array for own, received, _ in groups for array in (own, received)]
    return pl.pallas_call(
        functools.partial(close_kernel_, [group[2] for group in groups]),
        name="close",
        grid_spec=pltpu.PrefetchScalarGridSpec(
            num_scalar_prefetch=1,
            grid=(tiles,),
            in_specs=[pl.BlockSpec((TILE, width), lambda i, s: (s[0] * tiles + i, 0))]
            + [rows(array.shape[1]) for array in arrays],
            out_specs=rows(width),
        ),
        out_shape=jax.ShapeDtypeStruct((count // 2, width), BF16),
        compiler_params=params(),
        cost_estimate=cost(1000, 1000),
    )(hid_index.astype(jnp.int32)[None], residual, *arrays)


def close_kernel_(places, half_ref, *refs):
    close_kernel(places, *refs)


def shifted(value, steps):
    count = lax.axis_size("seq")
    return lax.ppermute(value, "seq", [(i, i + steps) for i in range(count - steps)])


def swapped(value, axis, flip):
    count = lax.axis_size(axis)
    return lax.ppermute(value, axis, [(i, i ^ flip) for i in range(count)])


def after(value, *others):
    return lax.optimization_barrier((value, *others))[0]


def on_device(
    tokens, attention_gain, project_weight, conv_weight, decay_down, decay_up, decay_bias,
    output_gate, head_gain, output_weight, mixer_gain, gate_weight, up_weight, down_weight,
    prompt_pages, prompt_start,
):
    count, width = tokens.shape
    prompts = (prompt_pages, prompt_start)
    two_by_two = lax.axis_size("req") == 4 and lax.axis_size("seq") % 2 == 0
    hid_index = lax.axis_index("hid")
    x, y = functools.partial(swapped, axis="req", flip=1), functools.partial(swapped, axis="req", flip=2)
    z = functools.partial(swapped, axis="seq", flip=1)
    depth = gate_weight.shape[0]
    half = depth // 2

    tied = lax.optimization_barrier
    if two_by_two:
        parity = lax.rem(lax.axis_index("seq"), 2)
        up_mine = lax.dynamic_slice_in_dim(up_weight, parity * half, half, 0)
        up_a, up_b = x(up_mine), y(up_mine)
        gate_a, gate_b = x(gate_weight), y(gate_weight)
    rim = shifted(tokens[-RIM:], 1)
    rim, other_output = lax.optimization_barrier((rim, swapped(output_weight, "hid", 1)))

    raised, lowered, weighted, value, ends, edges, opening, state = front(
        prompts, tokens, rim, attention_gain[None], project_weight, output_gate, decay_down.T,
        decay_up, decay_bias[None], conv_weight,
    )
    if two_by_two:
        state, gate_a, gate_b = tied((state, gate_a, gate_b))
        down_0, down_1 = down_weight[:, :half], down_weight[:, half:]
        gate_c, down_b1 = x(gate_b), y(down_1)
    one = shifted(state, 1)
    two = shifted(joined(state, one), 2)
    if two_by_two:
        one, two, up_a, up_b, down_0 = tied((one, two, up_a, up_b, down_0))
        up_c, far_a, far_b, down_a0 = y(up_a), z(up_a), z(up_b), x(down_0)
        down_c0 = y(down_a0)
    states, *gated = pages(
        prompts, raised, lowered, weighted, value, ends, opening, head_gain[None], one, two,
    )
    others = [swapped(part, "hid", 1) for part in gated]
    if two_by_two:
        others, up_c, gate_c, far_a, down_b1 = tied((others, up_c, gate_c, far_a, down_b1))
        far_c = y(far_a)
    residual, feed = mix(tokens, gated, others, output_weight, other_output, mixer_gain[None])

    if two_by_two:
        feed, down_0, down_1 = tied((feed, down_0, down_1))
        down_b0, down_a1 = y(down_0), x(down_1)
        feed, far_b, far_c, down_b1 = tied((feed, far_b, far_c, down_b1))
        down_c1 = x(down_b1)
        at = lambda flip, more=0: lambda: (lax.axis_index("req") ^ flip) * depth + more
        own = lambda flip: lambda: at(flip)() + lax.rem(lax.axis_index("seq"), 2) * half
        far = lambda flip: lambda: at(flip)() + (1 - lax.rem(lax.axis_index("seq"), 2)) * half
        gate_list = [(gate_weight, at(0)), (gate_a, at(1)), (gate_b, at(2)), (gate_c, at(3))]
        up_list = [
            (up_weight, at(0)), (up_a, own(1)), (far_a, far(1)), (up_b, own(2)), (far_b, far(2)),
            (up_c, own(3)), (far_c, far(3)),
        ]
        down_lists = [
            [(down_weight, at(0)), (down_a0, at(1)), (down_b1, at(2, half)), (down_b0, at(2))],
            [(down_a1, at(1, half)), (down_c0, at(3)), (down_c1, at(3, half))],
        ]
    else:
        first = lambda: 0
        gate_list = [(lax.all_gather(gate_weight, "req", axis=0, tiled=True), first)]
        up_list = [(lax.all_gather(up_weight, "req", axis=0, tiled=True), first)]
        down_lists = [[(lax.all_gather(down_weight, "req", axis=1, tiled=True), first)]]

    hidden = widen(feed, (gate_list, up_list))
    groups = []
    for pieces, parts in zip(down_lists, (1, 2)):
        theirs, mine = narrow(hidden, [piece for piece, _ in pieces], count // parts)
        received = swapped(theirs, "hid", 1)
        groups.append((mine, received, [(piece.shape[1], place) for piece, place in pieces]))
    result = close(hid_index, residual, groups)
    return result, states, edges


def solution(mesh):
    return jax.shard_map(
        on_device,
        mesh=mesh,
        in_specs=(
            P(("req", "seq"), None),
            P(),
            P(None, "hid"),
            P(None, "hid"),
            P(),
            P(None, "hid"),
            P("hid"),
            P(None, "hid"),
            P(),
            P("hid", None),
            P(),
            P("req", "hid"),
            P("req", "hid"),
            P("hid", "req"),
            P("req", None),
            P("req", None),
        ),
        out_specs=(
            P(("req", "seq", "hid"), None),
            P(("req", "seq"), "hid", None, None),
            P(("req", "seq"), None, "hid"),
        ),
        check_vma=False,
    )
```

```python
import functools

import jax
import jax.numpy as jnp
from jax import lax
from jax.experimental import pallas as pl
from jax.experimental.pallas import tpu as pltpu
from jax.sharding import PartitionSpec as P

HK = 256
HV = 512
KCONV = 4
PAGE = 64
CONVW = 1024
EPSILON = 1e-06
TILE = 256
PAGES_T = TILE // PAGE
RIM = 16
BF16 = jnp.bfloat16
F32 = jnp.float32
VMEM_LIMIT = 60 * 1024 * 1024
WIDE = 256
FRONT = 512
MIX = 256
ROWS = 512


def params():
    return pltpu.CompilerParams(
        dimension_semantics=("arbitrary",), vmem_limit_bytes=VMEM_LIMIT
    )


def cost(flops, moved):
    return pl.CostEstimate(flops=flops, bytes_accessed=moved, transcendentals=0)


def fixed(shape):
    return pl.BlockSpec(
        shape, lambda *_: (0,) * len(shape), pipeline_mode=pl.Buffered(1)
    )


def whole_smem():
    return pl.BlockSpec(memory_space=pltpu.SMEM)


def dot(a, b):
    return jnp.dot(a, b, preferred_element_type=F32)


def dot_nt(a, b):
    return lax.dot_general(a, b, (((1,), (1,)), ((), ())), preferred_element_type=F32)


def dot_tn(a, b):
    return lax.dot_general(a, b, (((0,), (0,)), ((), ())), preferred_element_type=F32)


def silu(x):
    return x / (1.0 + jnp.exp(-x))


def column(row):
    return jnp.transpose(jnp.broadcast_to(row, (128, row.shape[1])))[:, :1]


def normalised(x, gain):
    return x * lax.rsqrt(jnp.mean(x * x, axis=-1, keepdims=True) + EPSILON) * gain


def carried_flag(pages_ref, start_ref, page, count):
    page = lax.axis_index("seq") * count + page
    same = jnp.int32(0)
    for i in range(pages_ref.shape[1]):
        first = start_ref[0, i]
        same = jnp.where((page > first) & (page < first + pages_ref[0, i]), 1, same)
    return same.astype(F32)


def product(left, rows, weight_ref, columns, step=512):
    depth = weight_ref.shape[0]
    total = None
    for k in range(0, depth, step):
        span = pl.ds(k, min(step, depth - k))
        part = dot(left[rows, span], weight_ref[span, columns])
        total = part if total is None else total + part
    return total


def rms_columns(read, write, gain_ref, width):
    total = None
    for low in range(0, width, WIDE):
        x = read(pl.ds(low, WIDE))
        square = x * x
        part = square[:, : WIDE // 2] + square[:, WIDE // 2 :]
        total = part if total is None else total + part
    scale = lax.rsqrt(jnp.sum(total, axis=-1, keepdims=True) * (1.0 / width) + EPSILON)
    for low in range(0, width, WIDE):
        columns = pl.ds(low, WIDE)
        write(columns, read(columns) * scale * gain_ref[:, columns].astype(F32))


def norm_into(normed, gain_ref, blocks):
    for ref, source, target, count in blocks:
        def read(columns, ref=ref, source=source, count=count):
            return ref[pl.ds(source, count), columns].astype(F32)

        def write(columns, x, target=target, count=count):
            normed[pl.ds(target, count), columns] = x.astype(BF16)

        rms_columns(read, write, gain_ref, normed.shape[1])


def short_conv(projected, previous, carried, taps, j):
    now = projected[j * PAGE : (j + 1) * PAGE]
    before = previous if j == 0 else projected[j * PAGE - 8 : j * PAGE]
    widened = jnp.concatenate([before * carried, now], axis=0)
    mixed = taps[0:1] * now
    for i in range(1, KCONV):
        mixed = mixed + taps[i : i + 1] * widened[8 - i : 8 - i + PAGE]
    return mixed


def page_edge(low, j):
    return low[(j + 1) * PAGE - (KCONV - 1) : (j + 1) * PAGE]


def front_kernel(
    pages_ref, start_ref, tokens_ref, rim_ref, gain_ref, key_ref, first_ref, second_ref, down_ref, up_ref,
    bias_ref, conv_ref, normed_ref, sums_ref, lowered_ref, weighted_ref, value_ref, ends_ref, edges_ref,
    state_ref, normed, carry, state, decay, keys,
):
    step = pl.program_id(0)
    tile = tokens_ref.shape[0]
    pages = tile // PAGE

    @pl.when(step == 0)
    def _():
        state[...] = jnp.zeros_like(state)
        decay[...] = jnp.ones_like(decay)

    norm_into(
        normed, gain_ref,
        [(rim_ref, 0, tile, RIM)] + [(tokens_ref, r, r, 128) for r in range(0, tile, 128)],
    )
    normed_ref[...] = normed[:tile]
    lowrank = dot_nt(normed[:tile], down_ref[...]).astype(BF16)
    logits = dot(lowrank, up_ref[...]) + bias_ref[...]
    decay_log = (jnp.minimum(logits, 0.0) - jnp.log1p(jnp.exp(-jnp.abs(logits)))) / 16.0
    row = lax.broadcasted_iota(jnp.int32, (HK, HK), 0)
    col = lax.broadcasted_iota(jnp.int32, (HK, HK), 1)
    lower = jnp.where((row >= col) & ((row // PAGE) == (col // PAGE)), 1.0, 0.0).astype(F32)
    for r in range(0, tile, HK):
        sums_ref[pl.ds(r, HK), :] = jnp.dot(
            lower, decay_log[r : r + HK], preferred_element_type=F32, precision=lax.Precision.HIGHEST
        )
    carried = [
        carried_flag(pages_ref, start_ref, step * pages + j, pl.num_programs(0) * pages)
        for j in range(pages)
    ]
    ends = [sums_ref[pl.ds((j + 1) * PAGE - 8, 8), :][7:] for j in range(pages)]
    suffix = [None] * pages + [jnp.ones((1, HK), F32)]
    for j in reversed(range(pages)):
        kept = jnp.exp(ends[j])
        ends_ref[j] = jnp.broadcast_to(kept, (8, HK))
        suffix[j] = suffix[j + 1] * (kept * carried[j])

    for chunk, weight_ref in enumerate((key_ref, first_ref, second_ref)):
        columns = pl.ds(chunk * WIDE, WIDE)
        low = product(normed, slice(None), weight_ref, slice(None)).astype(BF16)
        projected = low[:tile].astype(F32)
        previous = jnp.where(step == 0, low[tile:].astype(F32)[RIM - 8 :], carry[:, columns])
        carry[:, columns] = projected[tile - 8 :]
        taps = conv_ref[:, pl.ds(HK + chunk * WIDE, WIDE)].astype(F32)
        for j in range(pages):
            mixed = short_conv(projected, previous, carried[j], taps, j)
            span = pl.ds(j * PAGE, PAGE)
            edges_ref[j, :, columns] = page_edge(low, j)
            if chunk == 0:
                key = silu(mixed) * HK ** (-0.5)
                sums = sums_ref[span, :]
                weighted = key * jnp.exp(ends[j] - sums)
                lowered_ref[span, :] = (key * jnp.exp(-sums)).astype(BF16)
                weighted_ref[span, :] = weighted.astype(BF16)
                keys[span, :] = (weighted * suffix[j + 1]).astype(BF16)
            else:
                value_ref[span, pl.ds((chunk - 1) * WIDE, WIDE)] = mixed.astype(BF16)
    state[...] = column(suffix[0]) * state[...] + dot_tn(keys[...], value_ref[...])
    decay[...] = decay[...] * suffix[0]

    @pl.when(step == pl.num_programs(0) - 1)
    def _():
        state_ref[:HK] = state[...].astype(BF16)
        block = jnp.concatenate([decay[...]] * (HV // HK), axis=1)
        state_ref[HK:] = jnp.concatenate([block] * (RIM // 8), axis=0).astype(BF16)


def column_block(height, i):
    return pl.BlockSpec((height, WIDE), lambda *_: (0, i), pipeline_mode=pl.Buffered(1))


def front(prompts, tokens, rim, gain, project, down, up, bias, conv):
    count, width = tokens.shape
    rank = down.shape[0]
    pages = count // PAGE
    tile = FRONT
    rows = lambda n: pl.BlockSpec((tile, n), lambda i: (i, 0))
    shape = jax.ShapeDtypeStruct
    return pl.pallas_call(
        front_kernel,
        name="front",
        grid=(count // tile,),
        in_specs=[
            whole_smem(), whole_smem(), rows(width), fixed((RIM, width)), fixed((1, width)),
            column_block(width, 1), column_block(width, 2), column_block(width, 3),
            fixed((rank, width)), fixed((rank, HK)), fixed((1, HK)), fixed((KCONV, CONVW)),
        ],
        out_specs=[
            rows(width), rows(HK), rows(HK), rows(HK), rows(HV),
            pl.BlockSpec((tile // PAGE, 8, HK), lambda i: (i, 0, 0)),
            pl.BlockSpec((tile // PAGE, KCONV - 1, HK + HV), lambda i: (i, 0, 0)),
            fixed((HK + RIM, HV)),
        ],
        out_shape=[
            shape((count, width), BF16), shape((count, HK), F32), shape((count, HK), BF16),
            shape((count, HK), BF16), shape((count, HV), BF16), shape((pages, 8, HK), F32),
            shape((pages, KCONV - 1, HK + HV), BF16), shape((HK + RIM, HV), BF16),
        ],
        scratch_shapes=[
            pltpu.VMEM((tile + RIM, width), BF16), pltpu.VMEM((8, HK + HV), F32),
            pltpu.VMEM((HK, HV), F32), pltpu.VMEM((8, HK), F32), pltpu.VMEM((tile, HK), BF16),
        ],
        compiler_params=params(),
        cost_estimate=cost(1000, 1000),
    )(*prompts, tokens, rim, gain, project, project, project, down, up, bias, conv)


def query_kernel(
    pages_ref, start_ref, normed_ref, rim_ref, gain_ref, query_ref, gate_ref, conv_ref, sums_ref,
    raised_ref, edges_ref, opening_ref, normed_rim, carry,
):
    step = pl.program_id(0)
    tile = normed_ref.shape[0]
    pages = tile // PAGE

    @pl.when(step == 0)
    def _():
        norm_into(normed_rim, gain_ref, [(rim_ref, 0, 0, RIM)])
        low = product(normed_rim, slice(None), query_ref, slice(None)).astype(BF16)
        carry[...] = low.astype(F32)[RIM - 8 :]

    low = product(normed_ref, slice(None), query_ref, slice(None)).astype(BF16)
    projected = low.astype(F32)
    previous = carry[...]
    taps = conv_ref[:, :HK].astype(F32)
    for j in range(pages):
        carried = carried_flag(pages_ref, start_ref, step * pages + j, pl.num_programs(0) * pages)
        mixed = short_conv(projected, previous, carried, taps, j)
        span = pl.ds(j * PAGE, PAGE)
        edges_ref[j] = page_edge(low, j)
        raised_ref[span, :] = (silu(mixed) * jnp.exp(sums_ref[span, :])).astype(BF16)
    carry[...] = projected[tile - 8 :]
    for at in range(0, HV, WIDE):
        columns = pl.ds(at, WIDE)
        opening_ref[:, columns] = silu(product(normed_ref, slice(None), gate_ref, columns)).astype(BF16)


def query(prompts, normed, rim, gain, project, gate, conv, sums):
    count, width = normed.shape
    pages = count // PAGE
    tile = FRONT
    rows = lambda n: pl.BlockSpec((tile, n), lambda i: (i, 0))
    shape = jax.ShapeDtypeStruct
    return pl.pallas_call(
        query_kernel,
        name="query",
        grid=(count // tile,),
        in_specs=[
            whole_smem(), whole_smem(), rows(width), fixed((RIM, width)), fixed((1, width)),
            column_block(width, 0), fixed((width, HV)), fixed((KCONV, CONVW)), rows(HK),
        ],
        out_specs=[
            rows(HK), pl.BlockSpec((tile // PAGE, KCONV - 1, HK), lambda i: (i, 0, 0)), rows(HV),
        ],
        out_shape=[
            shape((count, HK), BF16), shape((pages, KCONV - 1, HK), BF16), shape((count, HV), BF16),
        ],
        scratch_shapes=[pltpu.VMEM((RIM, width), BF16), pltpu.VMEM((8, HK), F32)],
        compiler_params=params(),
        cost_estimate=cost(2 * count * width * (HK + HV), 2 * count * width),
    )(*prompts, normed, rim, gain, project, gate, conv, sums)


def composed(later, earlier):
    kept = column(later[HK:].astype(F32)[:1, :HK])
    return later[:HK].astype(F32) + kept * earlier[:HK].astype(F32)


def joined_kernel(later_ref, earlier_ref, out_ref):
    out_ref[:HK] = composed(later_ref, earlier_ref).astype(BF16)
    out_ref[HK:] = later_ref[HK:]


def joined(later, earlier):
    return pl.pallas_call(
        joined_kernel, name="joined",
        in_specs=[pl.BlockSpec(memory_space=pltpu.VMEM)] * 2,
        out_specs=pl.BlockSpec(memory_space=pltpu.VMEM),
        out_shape=jax.ShapeDtypeStruct(later.shape, BF16),
        cost_estimate=cost(1000, 1000),
    )(later, earlier)


def halves(count, tile):
    half = count // tile // 2
    return [
        pl.BlockSpec((tile, HV), lambda i: (jnp.minimum(i, half - 1), 0)),
        pl.BlockSpec((tile, HV), lambda i: (jnp.maximum(i - half, 0), 0)),
    ]


def pages_kernel(
    pages_ref, start_ref, raised_ref, lowered_ref, weighted_ref, value_ref, ends_ref, opening_ref, gain_ref,
    one_ref, two_ref, states_ref, low_ref, high_ref, memory,
):
    step = pl.program_id(0)

    @pl.when(step == 0)
    def _():
        memory[...] = composed(one_ref, two_ref)

    row = lax.broadcasted_iota(jnp.int32, (PAGE, PAGE), 0)
    col = lax.broadcasted_iota(jnp.int32, (PAGE, PAGE), 1)
    gain = gain_ref[...].astype(F32)
    held = memory[...]
    gated_tile = []
    for j in range(PAGES_T):
        span = pl.ds(j * PAGE, PAGE)
        raised, value = raised_ref[span, :], value_ref[span, :]
        held = held * carried_flag(pages_ref, start_ref, step * PAGES_T + j, pl.num_programs(0) * PAGES_T)
        scores = dot_nt(raised, lowered_ref[span, :])
        scores = jnp.where(row >= col, scores, 0.0).astype(BF16)
        attended = dot(scores, value) + dot(raised, held.astype(BF16))
        held = column(ends_ref[j][:1]) * held + dot_tn(weighted_ref[span, :], value)
        states_ref[j, 0] = held.astype(BF16)
        gated = normalised(attended, gain) * opening_ref[span, :].astype(F32)
        gated_tile.append(gated.astype(BF16))
    memory[...] = held
    half = pl.num_programs(0) // 2

    @pl.when(step < half)
    def _():
        low_ref[...] = jnp.concatenate(gated_tile, axis=0)

    @pl.when(step >= half)
    def _():
        high_ref[...] = jnp.concatenate(gated_tile, axis=0)


def pages(prompts, raised, lowered, weighted, value, ends, opening, gain, one, two):
    count = raised.shape[0]
    total = count // PAGE
    rows = lambda n: pl.BlockSpec((TILE, n), lambda i: (i, 0))
    return pl.pallas_call(
        pages_kernel,
        name="pages",
        grid=(count // TILE,),
        in_specs=[
            whole_smem(), whole_smem(), rows(HK), rows(HK), rows(HK), rows(HV),
            pl.BlockSpec((PAGES_T, 8, HK), lambda i: (i, 0, 0)), rows(HV), fixed((1, HV)),
            fixed((HK + RIM, HV)), fixed((HK + RIM, HV)),
        ],
        out_specs=[
            pl.BlockSpec((PAGES_T, 1, HK, HV), lambda i: (i, 0, 0, 0)), *halves(count, TILE),
        ],
        out_shape=[
            jax.ShapeDtypeStruct((total, 1, HK, HV), BF16),
            jax.ShapeDtypeStruct((count // 2, HV), BF16),
            jax.ShapeDtypeStruct((count // 2, HV), BF16),
        ],
        scratch_shapes=[pltpu.VMEM((HK, HV), F32)],
        compiler_params=params(),
        cost_estimate=cost(1000, 1000),
    )(*prompts, raised, lowered, weighted, value, ends, opening, gain, one, two)


def mix_kernel(
    tokens_ref, low_ref, high_ref, other_low_ref, other_high_ref, own_weight_ref, other_weight_ref,
    gain_ref, residual_ref, feed_ref, residual,
):
    first = pl.program_id(0) < pl.num_programs(0) // 2
    own = jnp.where(first, low_ref[...], high_ref[...])
    other = jnp.where(first, other_low_ref[...], other_high_ref[...])
    width = tokens_ref.shape[1]
    for at in range(0, width, WIDE):
        columns = pl.ds(at, WIDE)
        mixed = dot(own, own_weight_ref[:, columns]) + dot(other, other_weight_ref[:, columns])
        residual[:, columns] = (tokens_ref[:, columns].astype(F32) + mixed).astype(BF16)

    @pl.when(first == (lax.axis_index("hid") == 0))
    def _():
        residual_ref[...] = residual[...]

    def write(columns, x):
        feed_ref[:, columns] = x.astype(BF16)

    rms_columns(lambda columns: residual[:, columns].astype(F32), write, gain_ref, width)


def mix(hid_index, tokens, own, others, own_weight, other_weight, gain):
    count, width = tokens.shape
    tile = MIX
    half = count // tile // 2
    rows = pl.BlockSpec((tile, width), lambda i, s: (i, 0))
    halves = [
        pl.BlockSpec((tile, HV), lambda i, s: (jnp.minimum(i, half - 1), 0)),
        pl.BlockSpec((tile, HV), lambda i, s: (jnp.maximum(i - half, 0), 0)),
    ]
    mine = pl.BlockSpec((tile, width), lambda i, s: (jnp.clip(i - s[0] * half, 0, half - 1), 0))
    return pl.pallas_call(
        lambda s, *refs: mix_kernel(*refs),
        name="mix",
        grid_spec=pltpu.PrefetchScalarGridSpec(
            num_scalar_prefetch=1,
            grid=(count // tile,),
            in_specs=[rows, *halves, *halves, fixed((HV, width)), fixed((HV, width)), fixed((1, width))],
            out_specs=[mine, rows],
            scratch_shapes=[pltpu.VMEM((tile, width), BF16)],
        ),
        out_shape=[
            jax.ShapeDtypeStruct((count // 2, width), BF16), jax.ShapeDtypeStruct((count, width), BF16),
        ],
        compiler_params=params(),
        cost_estimate=cost(1000, 1000),
    )(hid_index, tokens, *own, *others, own_weight, other_weight, gain)


def widen_kernel(places, feed_ref, *refs):
    pieces, out_ref = refs[:-1], refs[-1]
    count = feed_ref.shape[0]
    for first in range(0, count, ROWS):
        rows = pl.ds(first, ROWS)
        sums = [None, None]
        for (matrix, place), ref in zip(places, pieces):
            columns = pl.ds(pl.multiple_of(place(), 128), ref.shape[0])
            part = dot(feed_ref[rows, columns], ref[...])
            sums[matrix] = part if sums[matrix] is None else sums[matrix] + part
        out_ref[rows, :] = (silu(sums[0]) * sums[1]).astype(BF16)


def widen(feed, matrices):
    count, width = feed.shape
    pieces = [piece for matrix in matrices for piece, _ in matrix]
    places = [(i, place) for i, matrix in enumerate(matrices) for _, place in matrix]
    hidden = pieces[0].shape[1]
    return pl.pallas_call(
        functools.partial(widen_kernel, places),
        name="widen",
        grid=(pl.cdiv(hidden, WIDE),),
        in_specs=[fixed((count, width))]
        + [pl.BlockSpec((piece.shape[0], WIDE), lambda i: (0, i)) for piece in pieces],
        out_specs=pl.BlockSpec((count, WIDE), lambda i: (0, i)),
        out_shape=jax.ShapeDtypeStruct((count, hidden), BF16),
        compiler_params=params(),
        cost_estimate=cost(1000, 1000),
    )(feed, *pieces)


def narrow_kernel(block, hidden_hbm, *refs):
    count = (len(refs) - 5) // 2
    pieces, theirs_ref, own_ref, hidden = refs[:count], *refs[count : count + 3]
    weights, sem, sems = refs[count + 3 : -2], refs[-2], refs[-1]
    rows = hidden.shape[0] // 2
    mine = lax.axis_index("hid")
    wholes = [
        pltpu.make_async_copy(
            hidden_hbm.at[pl.ds(pl.multiple_of(half * rows, rows), rows), :],
            hidden.at[pl.ds(i * rows, rows), :],
            sem.at[i],
        )
        for i, half in enumerate((1 - mine, mine))
    ]
    copies = [
        pltpu.make_async_copy(ref, weight, sems.at[i])
        for i, (ref, weight) in enumerate(zip(pieces, weights))
    ]
    for copy in wholes + copies:
        copy.start()
    for copy in wholes:
        copy.wait()
    at = 0
    for copy, weight in zip(copies, weights):
        copy.wait()
        for low in range(0, weight.shape[1], WIDE):
            for first in range(0, 2 * rows, block):
                total = product(hidden, pl.ds(first, block), weight, pl.ds(low, WIDE)).astype(BF16)
                for out_ref, start in ((theirs_ref, 0), (own_ref, rows)):
                    if first < start + rows and start < first + block:
                        taken = total[max(start - first, 0) : start + rows - first]
                        out_ref[pl.ds(max(first - start, 0), taken.shape[0]), pl.ds(at, WIDE)] = taken
            at += WIDE


def narrow(hidden, pieces, block):
    count, depth = hidden.shape
    width = sum(piece.shape[1] for piece in pieces)
    return pl.pallas_call(
        functools.partial(narrow_kernel, block),
        name="narrow",
        in_specs=[pl.BlockSpec(memory_space=pl.ANY)] * (1 + len(pieces)),
        out_specs=[pl.BlockSpec(memory_space=pltpu.VMEM)] * 2,
        out_shape=[jax.ShapeDtypeStruct((count // 2, width), BF16)] * 2,
        scratch_shapes=[pltpu.VMEM((count, depth), BF16)]
        + [pltpu.VMEM(piece.shape, BF16) for piece in pieces]
        + [pltpu.SemaphoreType.DMA((2,)), pltpu.SemaphoreType.DMA((len(pieces),))],
        compiler_params=pltpu.CompilerParams(vmem_limit_bytes=VMEM_LIMIT),
        cost_estimate=cost(1000, 1000),
    )(hidden, *pieces)


def close_kernel(places, residual_ref, *refs):
    out_ref = refs[-1]
    for group, (own_ref, received_ref) in zip(places, zip(refs[:-1:2], refs[1:-1:2])):
        at = 0
        for size, place in group:
            columns, span = pl.ds(pl.multiple_of(place(), 128), size), pl.ds(at, size)
            total = own_ref[:, span].astype(F32) + received_ref[:, span].astype(F32)
            out_ref[:, columns] = (residual_ref[:, columns].astype(F32) + total).astype(BF16)
            at += size


def close(residual, groups):
    count, width = residual.shape
    rows = lambda n: pl.BlockSpec((TILE, n), lambda i: (i, 0))
    arrays = [array for own, received, _ in groups for array in (own, received)]
    return pl.pallas_call(
        functools.partial(close_kernel, [group[2] for group in groups]),
        name="close",
        grid=(count // TILE,),
        in_specs=[rows(width)] + [rows(array.shape[1]) for array in arrays],
        out_specs=rows(width),
        out_shape=jax.ShapeDtypeStruct((count, width), BF16),
        compiler_params=params(),
        cost_estimate=cost(1000, 1000),
    )(residual, *arrays)


def shifted(value, steps):
    count = lax.axis_size("seq")
    return lax.ppermute(value, "seq", [(i, i + steps) for i in range(count - steps)])


def swapped(value, axis, flip):
    count = lax.axis_size(axis)
    return lax.ppermute(value, axis, [(i, i ^ flip) for i in range(count)])


def after(value, *others):
    return lax.optimization_barrier((value, *others))[0]


def on_device(
    tokens, attention_gain, project_weight, conv_weight, decay_down, decay_up, decay_bias,
    output_gate, head_gain, output_weight, mixer_gain, gate_weight, up_weight, down_weight,
    prompt_pages, prompt_start,
):
    count, width = tokens.shape
    prompts = (prompt_pages, prompt_start)
    two_by_two = lax.axis_size("req") == 4 and lax.axis_size("seq") % 2 == 0
    hid_index = lax.axis_index("hid").astype(jnp.int32)[None]
    x, y = functools.partial(swapped, axis="req", flip=1), functools.partial(swapped, axis="req", flip=2)
    z = functools.partial(swapped, axis="seq", flip=1)
    depth = gate_weight.shape[0]
    half = depth // 2

    tied = lax.optimization_barrier
    if two_by_two:
        parity = lax.rem(lax.axis_index("seq"), 2)
        up_mine = lax.dynamic_slice_in_dim(up_weight, parity * half, half, 0)
        up_a, up_b = x(up_mine), y(up_mine)
        gate_a, gate_b = x(gate_weight), y(gate_weight)
    rim = shifted(tokens[-RIM:], 1)
    rim, other_output = lax.optimization_barrier((rim, swapped(output_weight, "hid", 1)))

    normed, sums, lowered, weighted, value, ends, edges, state = front(
        prompts, tokens, rim, attention_gain[None], project_weight, decay_down.T, decay_up,
        decay_bias[None], conv_weight,
    )
    one = shifted(state, 1)
    two = shifted(joined(state, one), 2)
    if two_by_two:
        down_0, down_1 = down_weight[:, :half], down_weight[:, half:]
        normed, gate_a, gate_b = tied((normed, gate_a, gate_b))
        gate_c, down_b1 = x(gate_b), y(down_1)
    raised, query_edges, opening = query(
        prompts, normed, rim, attention_gain[None], project_weight, output_gate, conv_weight, sums,
    )
    if two_by_two:
        one, two, raised, up_a, up_b, down_0 = tied((one, two, raised, up_a, up_b, down_0))
        up_c, far_a, far_b, down_a0 = y(up_a), z(up_a), z(up_b), x(down_0)
        down_c0 = y(down_a0)
    states, *gated = pages(
        prompts, raised, lowered, weighted, value, ends, opening, head_gain[None], one, two,
    )
    others = [swapped(part, "hid", 1) for part in gated]
    if two_by_two:
        others, up_c, gate_c, far_a, down_b1 = tied((others, up_c, gate_c, far_a, down_b1))
        far_c = y(far_a)
    residual, feed = mix(hid_index, tokens, gated, others, output_weight, other_output, mixer_gain[None])

    if two_by_two:
        feed, down_0, down_1 = tied((feed, down_0, down_1))
        down_b0, down_a1 = y(down_0), x(down_1)
        feed, far_b, far_c, down_b1 = tied((feed, far_b, far_c, down_b1))
        down_c1 = x(down_b1)
        at = lambda flip, more=0: lambda: (lax.axis_index("req") ^ flip) * depth + more
        own = lambda flip: lambda: at(flip)() + lax.rem(lax.axis_index("seq"), 2) * half
        far = lambda flip: lambda: at(flip)() + (1 - lax.rem(lax.axis_index("seq"), 2)) * half
        gate_list = [(gate_weight, at(0)), (gate_a, at(1)), (gate_b, at(2)), (gate_c, at(3))]
        up_list = [
            (up_weight, at(0)), (up_a, own(1)), (far_a, far(1)), (up_b, own(2)), (far_b, far(2)),
            (up_c, own(3)), (far_c, far(3)),
        ]
        down_lists = [
            [(down_weight, at(0)), (down_a0, at(1)), (down_b1, at(2, half)), (down_b0, at(2))],
            [(down_a1, at(1, half)), (down_c0, at(3)), (down_c1, at(3, half))],
        ]
    else:
        first = lambda: 0
        gate_list = [(lax.all_gather(gate_weight, "req", axis=0, tiled=True), first)]
        up_list = [(lax.all_gather(up_weight, "req", axis=0, tiled=True), first)]
        down_lists = [[(lax.all_gather(down_weight, "req", axis=1, tiled=True), first)]]

    hidden = widen(feed, (gate_list, up_list))
    groups = []
    for pieces in down_lists:
        theirs, mine = narrow(hidden, [piece for piece, _ in pieces], ROWS)
        received = swapped(theirs, "hid", 1)
        groups.append((mine, received, [(piece.shape[1], place) for piece, place in pieces]))
    result = close(residual, groups)
    return result, states, jnp.concatenate([query_edges, edges], axis=-1)


def solution(mesh):
    return jax.shard_map(
        on_device,
        mesh=mesh,
        in_specs=(
            P(("req", "seq"), None),
            P(),
            P(None, "hid"),
            P(None, "hid"),
            P(),
            P(None, "hid"),
            P("hid"),
            P(None, "hid"),
            P(),
            P("hid", None),
            P(),
            P("req", "hid"),
            P("req", "hid"),
            P("hid", "req"),
            P("req", None),
            P("req", None),
        ),
        out_specs=(
            P(("req", "seq", "hid"), None),
            P(("req", "seq"), "hid", None, None),
            P(("req", "seq"), None, "hid"),
        ),
        check_vma=False,
    )
```

```python
import functools

import jax
import jax.numpy as jnp
from jax import lax
from jax.experimental import pallas as pl
from jax.experimental.pallas import tpu as pltpu
from jax.sharding import PartitionSpec as P

HK = 256
HV = 512
KCONV = 4
PAGE = 64
CONVW = 1024
EPSILON = 1e-06
TILE = 256
PAGES_T = TILE // PAGE
RIM = 16
BF16 = jnp.bfloat16
F32 = jnp.float32
WIDE = 256
FRONT = 256
QUERY = 512
MIX = 256
ROWS = 512


def params(mebibytes):
    return pltpu.CompilerParams(vmem_limit_bytes=mebibytes * 1024 * 1024)


def cost(flops, moved):
    return pl.CostEstimate(flops=flops, bytes_accessed=moved, transcendentals=0)


def fixed(shape):
    return pl.BlockSpec(
        shape, lambda *_: (0,) * len(shape), pipeline_mode=pl.Buffered(1)
    )


def whole_smem():
    return pl.BlockSpec(memory_space=pltpu.SMEM)


def dot(a, b):
    return jnp.dot(a, b, preferred_element_type=F32)


def dot_nt(a, b):
    return lax.dot_general(a, b, (((1,), (1,)), ((), ())), preferred_element_type=F32)


def dot_tn(a, b):
    return lax.dot_general(a, b, (((0,), (0,)), ((), ())), preferred_element_type=F32)


def silu(x):
    return x / (1.0 + jnp.exp(-x))


def column(row):
    return jnp.transpose(jnp.broadcast_to(row, (128, row.shape[1])))[:, :1]


def normalised(x, gain):
    return x * lax.rsqrt(jnp.mean(x * x, axis=-1, keepdims=True) + EPSILON) * gain


def carried_flag(pages_ref, start_ref, page, count):
    page = lax.axis_index("seq") * count + page
    same = jnp.int32(0)
    for i in range(pages_ref.shape[1]):
        first = start_ref[0, i]
        same = jnp.where((page > first) & (page < first + pages_ref[0, i]), 1, same)
    return same.astype(F32)


def product(left, rows, weight_ref, columns, step=512):
    depth = weight_ref.shape[0]
    total = None
    for k in range(0, depth, step):
        span = pl.ds(k, min(step, depth - k))
        part = dot(left[rows, span], weight_ref[span, columns])
        total = part if total is None else total + part
    return total


def rms_columns(read, write, gain_ref, width):
    total = None
    for low in range(0, width, WIDE):
        x = read(pl.ds(low, WIDE))
        square = x * x
        part = square[:, : WIDE // 2] + square[:, WIDE // 2 :]
        total = part if total is None else total + part
    scale = lax.rsqrt(jnp.sum(total, axis=-1, keepdims=True) * (1.0 / width) + EPSILON)
    for low in range(0, width, WIDE):
        columns = pl.ds(low, WIDE)
        write(columns, read(columns) * scale * gain_ref[:, columns].astype(F32))


def norm_into(normed, gain_ref, blocks):
    for ref, source, target, count in blocks:
        def read(columns, ref=ref, source=source, count=count):
            return ref[pl.ds(source, count), columns].astype(F32)

        def write(columns, x, target=target, count=count):
            normed[pl.ds(target, count), columns] = x.astype(BF16)

        rms_columns(read, write, gain_ref, normed.shape[1])


def short_conv(projected, previous, carried, taps, j):
    now = projected[j * PAGE : (j + 1) * PAGE]
    before = previous if j == 0 else projected[j * PAGE - 8 : j * PAGE]
    widened = jnp.concatenate([before * carried, now], axis=0)
    mixed = taps[0:1] * now
    for i in range(1, KCONV):
        mixed = mixed + taps[i : i + 1] * widened[8 - i : 8 - i + PAGE]
    return mixed


def page_edge(low, j):
    return low[(j + 1) * PAGE - (KCONV - 1) : (j + 1) * PAGE]


def front_kernel(
    pages_ref, start_ref, tokens_ref, rim_ref, gain_ref, key_ref, first_ref, second_ref, down_ref, up_ref,
    bias_ref, conv_ref, normed_ref, sums_ref, lowered_ref, weighted_ref, value_ref, ends_ref, edges_ref,
    state_ref, normed, carry, state, decay, keys,
):
    step = pl.program_id(0)
    tile = tokens_ref.shape[0]
    pages = tile // PAGE

    @pl.when(step == 0)
    def _():
        state[...] = jnp.zeros_like(state)
        decay[...] = jnp.ones_like(decay)

    norm_into(
        normed, gain_ref,
        [(rim_ref, 0, tile, RIM)] + [(tokens_ref, r, r, 128) for r in range(0, tile, 128)],
    )
    normed_ref[...] = normed[:tile]
    lowrank = dot_nt(normed[:tile], down_ref[...]).astype(BF16)
    logits = dot(lowrank, up_ref[...]) + bias_ref[...]
    decay_log = (jnp.minimum(logits, 0.0) - jnp.log1p(jnp.exp(-jnp.abs(logits)))) / 16.0
    row = lax.broadcasted_iota(jnp.int32, (HK, HK), 0)
    col = lax.broadcasted_iota(jnp.int32, (HK, HK), 1)
    lower = jnp.where((row >= col) & ((row // PAGE) == (col // PAGE)), 1.0, 0.0).astype(F32)
    for r in range(0, tile, HK):
        sums_ref[pl.ds(r, HK), :] = jnp.dot(
            lower, decay_log[r : r + HK], preferred_element_type=F32, precision=lax.Precision.HIGHEST
        )
    carried = [
        carried_flag(pages_ref, start_ref, step * pages + j, pl.num_programs(0) * pages)
        for j in range(pages)
    ]
    ends = [sums_ref[pl.ds((j + 1) * PAGE - 8, 8), :][7:] for j in range(pages)]
    suffix = [None] * pages + [jnp.ones((1, HK), F32)]
    for j in reversed(range(pages)):
        kept = jnp.exp(ends[j])
        ends_ref[j] = jnp.broadcast_to(kept, (8, HK))
        suffix[j] = suffix[j + 1] * (kept * carried[j])

    for chunk, weight_ref in enumerate((key_ref, first_ref, second_ref)):
        columns = pl.ds(chunk * WIDE, WIDE)
        low = product(normed, slice(None), weight_ref, slice(None)).astype(BF16)
        projected = low[:tile].astype(F32)
        previous = jnp.where(step == 0, low[tile:].astype(F32)[RIM - 8 :], carry[:, columns])
        carry[:, columns] = projected[tile - 8 :]
        taps = conv_ref[:, pl.ds(HK + chunk * WIDE, WIDE)].astype(F32)
        for j in range(pages):
            mixed = short_conv(projected, previous, carried[j], taps, j)
            span = pl.ds(j * PAGE, PAGE)
            edges_ref[j, :, columns] = page_edge(low, j)
            if chunk == 0:
                key = silu(mixed) * HK ** (-0.5)
                sums = sums_ref[span, :]
                weighted = key * jnp.exp(ends[j] - sums)
                lowered_ref[span, :] = (key * jnp.exp(-sums)).astype(BF16)
                weighted_ref[span, :] = weighted.astype(BF16)
                keys[span, :] = (weighted * suffix[j + 1]).astype(BF16)
            else:
                value_ref[span, pl.ds((chunk - 1) * WIDE, WIDE)] = mixed.astype(BF16)
    state[...] = column(suffix[0]) * state[...] + dot_tn(keys[...], value_ref[...])
    decay[...] = decay[...] * suffix[0]

    @pl.when(step == pl.num_programs(0) - 1)
    def _():
        state_ref[:HK] = state[...].astype(BF16)
        block = jnp.concatenate([decay[...]] * (HV // HK), axis=1)
        state_ref[HK:] = jnp.concatenate([block] * (RIM // 8), axis=0).astype(BF16)


def column_block(height, i):
    return pl.BlockSpec((height, WIDE), lambda *_: (0, i), pipeline_mode=pl.Buffered(1))


def front(prompts, tokens, rim, gain, project, down, up, bias, conv):
    count, width = tokens.shape
    rank = down.shape[0]
    pages = count // PAGE
    tile = FRONT
    rows = lambda n: pl.BlockSpec((tile, n), lambda i: (i, 0))
    shape = jax.ShapeDtypeStruct
    return pl.pallas_call(
        front_kernel,
        name="front",
        grid=(count // tile,),
        in_specs=[
            whole_smem(), whole_smem(), rows(width), fixed((RIM, width)), fixed((1, width)),
            column_block(width, 1), column_block(width, 2), column_block(width, 3),
            fixed((rank, width)), fixed((rank, HK)), fixed((1, HK)), fixed((KCONV, CONVW)),
        ],
        out_specs=[
            rows(width), rows(HK), rows(HK), rows(HK), rows(HV),
            pl.BlockSpec((tile // PAGE, 8, HK), lambda i: (i, 0, 0)),
            pl.BlockSpec((tile // PAGE, KCONV - 1, HK + HV), lambda i: (i, 0, 0)),
            fixed((HK + RIM, HV)),
        ],
        out_shape=[
            shape((count, width), BF16), shape((count, HK), F32), shape((count, HK), BF16),
            shape((count, HK), BF16), shape((count, HV), BF16), shape((pages, 8, HK), F32),
            shape((pages, KCONV - 1, HK + HV), BF16), shape((HK + RIM, HV), BF16),
        ],
        scratch_shapes=[
            pltpu.VMEM((tile + RIM, width), BF16), pltpu.VMEM((8, HK + HV), F32),
            pltpu.VMEM((HK, HV), F32), pltpu.VMEM((8, HK), F32), pltpu.VMEM((tile, HK), BF16),
        ],
        compiler_params=params(20),
        cost_estimate=cost(1000, 1000),
    )(*prompts, tokens, rim, gain, project, project, project, down, up, bias, conv)


def query_kernel(
    pages_ref, start_ref, normed_ref, rim_ref, gain_ref, query_ref, gate_ref, conv_ref, sums_ref,
    raised_ref, edges_ref, opening_ref, normed_rim, carry,
):
    step = pl.program_id(0)
    tile = normed_ref.shape[0]
    pages = tile // PAGE

    @pl.when(step == 0)
    def _():
        norm_into(normed_rim, gain_ref, [(rim_ref, 0, 0, RIM)])
        low = product(normed_rim, slice(None), query_ref, slice(None)).astype(BF16)
        carry[...] = low.astype(F32)[RIM - 8 :]

    low = product(normed_ref, slice(None), query_ref, slice(None)).astype(BF16)
    projected = low.astype(F32)
    previous = carry[...]
    taps = conv_ref[:, :HK].astype(F32)
    for j in range(pages):
        carried = carried_flag(pages_ref, start_ref, step * pages + j, pl.num_programs(0) * pages)
        mixed = short_conv(projected, previous, carried, taps, j)
        span = pl.ds(j * PAGE, PAGE)
        edges_ref[j] = page_edge(low, j)
        raised_ref[span, :] = (silu(mixed) * jnp.exp(sums_ref[span, :])).astype(BF16)
    carry[...] = projected[tile - 8 :]
    for at in range(0, HV, WIDE):
        columns = pl.ds(at, WIDE)
        opening_ref[:, columns] = silu(product(normed_ref, slice(None), gate_ref, columns)).astype(BF16)


def query(prompts, normed, rim, gain, project, gate, conv, sums):
    count, width = normed.shape
    pages = count // PAGE
    tile = QUERY
    rows = lambda n: pl.BlockSpec((tile, n), lambda i: (i, 0))
    shape = jax.ShapeDtypeStruct
    return pl.pallas_call(
        query_kernel,
        name="query",
        grid=(count // tile,),
        in_specs=[
            whole_smem(), whole_smem(), rows(width), fixed((RIM, width)), fixed((1, width)),
            column_block(width, 0), fixed((width, HV)), fixed((KCONV, CONVW)), rows(HK),
        ],
        out_specs=[
            rows(HK), pl.BlockSpec((tile // PAGE, KCONV - 1, HK), lambda i: (i, 0, 0)), rows(HV),
        ],
        out_shape=[
            shape((count, HK), BF16), shape((pages, KCONV - 1, HK), BF16), shape((count, HV), BF16),
        ],
        scratch_shapes=[pltpu.VMEM((RIM, width), BF16), pltpu.VMEM((8, HK), F32)],
        compiler_params=params(20),
        cost_estimate=cost(2 * count * width * (HK + HV), 2 * count * width),
    )(*prompts, normed, rim, gain, project, gate, conv, sums)


def composed(later, earlier):
    kept = column(later[HK:].astype(F32)[:1, :HK])
    return later[:HK].astype(F32) + kept * earlier[:HK].astype(F32)


def joined_kernel(later_ref, earlier_ref, out_ref):
    out_ref[:HK] = composed(later_ref, earlier_ref).astype(BF16)
    out_ref[HK:] = later_ref[HK:]


def joined(later, earlier):
    return pl.pallas_call(
        joined_kernel, name="joined",
        in_specs=[pl.BlockSpec(memory_space=pltpu.VMEM)] * 2,
        out_specs=pl.BlockSpec(memory_space=pltpu.VMEM),
        out_shape=jax.ShapeDtypeStruct(later.shape, BF16),
        compiler_params=params(6),
        cost_estimate=cost(1000, 1000),
    )(later, earlier)


def halves(count, tile):
    half = count // tile // 2
    return [
        pl.BlockSpec((tile, HV), lambda i: (jnp.minimum(i, half - 1), 0)),
        pl.BlockSpec((tile, HV), lambda i: (jnp.maximum(i - half, 0), 0)),
    ]


def pages_kernel(
    pages_ref, start_ref, raised_ref, lowered_ref, weighted_ref, value_ref, ends_ref, opening_ref, gain_ref,
    one_ref, two_ref, states_ref, low_ref, high_ref, memory,
):
    step = pl.program_id(0)

    @pl.when(step == 0)
    def _():
        memory[...] = composed(one_ref, two_ref)

    row = lax.broadcasted_iota(jnp.int32, (PAGE, PAGE), 0)
    col = lax.broadcasted_iota(jnp.int32, (PAGE, PAGE), 1)
    gain = gain_ref[...].astype(F32)
    held = memory[...]
    gated_tile = []
    for j in range(PAGES_T):
        span = pl.ds(j * PAGE, PAGE)
        raised, value = raised_ref[span, :], value_ref[span, :]
        held = held * carried_flag(pages_ref, start_ref, step * PAGES_T + j, pl.num_programs(0) * PAGES_T)
        scores = dot_nt(raised, lowered_ref[span, :])
        scores = jnp.where(row >= col, scores, 0.0).astype(BF16)
        attended = dot(scores, value) + dot(raised, held.astype(BF16))
        held = column(ends_ref[j][:1]) * held + dot_tn(weighted_ref[span, :], value)
        states_ref[j, 0] = held.astype(BF16)
        gated = normalised(attended, gain) * opening_ref[span, :].astype(F32)
        gated_tile.append(gated.astype(BF16))
    memory[...] = held
    half = pl.num_programs(0) // 2

    @pl.when(step < half)
    def _():
        low_ref[...] = jnp.concatenate(gated_tile, axis=0)

    @pl.when(step >= half)
    def _():
        high_ref[...] = jnp.concatenate(gated_tile, axis=0)


def pages(prompts, raised, lowered, weighted, value, ends, opening, gain, one, two):
    count = raised.shape[0]
    total = count // PAGE
    rows = lambda n: pl.BlockSpec((TILE, n), lambda i: (i, 0))
    return pl.pallas_call(
        pages_kernel,
        name="pages",
        grid=(count // TILE,),
        in_specs=[
            whole_smem(), whole_smem(), rows(HK), rows(HK), rows(HK), rows(HV),
            pl.BlockSpec((PAGES_T, 8, HK), lambda i: (i, 0, 0)), rows(HV), fixed((1, HV)),
            fixed((HK + RIM, HV)), fixed((HK + RIM, HV)),
        ],
        out_specs=[
            pl.BlockSpec((PAGES_T, 1, HK, HV), lambda i: (i, 0, 0, 0)), *halves(count, TILE),
        ],
        out_shape=[
            jax.ShapeDtypeStruct((total, 1, HK, HV), BF16),
            jax.ShapeDtypeStruct((count // 2, HV), BF16),
            jax.ShapeDtypeStruct((count // 2, HV), BF16),
        ],
        scratch_shapes=[pltpu.VMEM((HK, HV), F32)],
        compiler_params=params(12),
        cost_estimate=cost(1000, 1000),
    )(*prompts, raised, lowered, weighted, value, ends, opening, gain, one, two)


def mix_kernel(
    tokens_ref, low_ref, high_ref, other_low_ref, other_high_ref, own_weight_ref, other_weight_ref,
    gain_ref, residual_ref, feed_ref, residual,
):
    first = pl.program_id(0) < pl.num_programs(0) // 2
    own = jnp.where(first, low_ref[...], high_ref[...])
    other = jnp.where(first, other_low_ref[...], other_high_ref[...])
    width = tokens_ref.shape[1]
    for at in range(0, width, WIDE):
        columns = pl.ds(at, WIDE)
        mixed = dot(own, own_weight_ref[:, columns]) + dot(other, other_weight_ref[:, columns])
        residual[:, columns] = (tokens_ref[:, columns].astype(F32) + mixed).astype(BF16)

    @pl.when(first == (lax.axis_index("hid") == 0))
    def _():
        residual_ref[...] = residual[...]

    def write(columns, x):
        feed_ref[:, columns] = x.astype(BF16)

    rms_columns(lambda columns: residual[:, columns].astype(F32), write, gain_ref, width)


def mix(hid_index, tokens, own, others, own_weight, other_weight, gain):
    count, width = tokens.shape
    tile = MIX
    half = count // tile // 2
    rows = pl.BlockSpec((tile, width), lambda i, s: (i, 0))
    halves = [
        pl.BlockSpec((tile, HV), lambda i, s: (jnp.minimum(i, half - 1), 0)),
        pl.BlockSpec((tile, HV), lambda i, s: (jnp.maximum(i - half, 0), 0)),
    ]
    mine = pl.BlockSpec((tile, width), lambda i, s: (jnp.clip(i - s[0] * half, 0, half - 1), 0))
    return pl.pallas_call(
        lambda s, *refs: mix_kernel(*refs),
        name="mix",
        grid_spec=pltpu.PrefetchScalarGridSpec(
            num_scalar_prefetch=1,
            grid=(count // tile,),
            in_specs=[rows, *halves, *halves, fixed((HV, width)), fixed((HV, width)), fixed((1, width))],
            out_specs=[mine, rows],
            scratch_shapes=[pltpu.VMEM((tile, width), BF16)],
        ),
        out_shape=[
            jax.ShapeDtypeStruct((count // 2, width), BF16), jax.ShapeDtypeStruct((count, width), BF16),
        ],
        compiler_params=params(20),
        cost_estimate=cost(1000, 1000),
    )(hid_index, tokens, *own, *others, own_weight, other_weight, gain)


def widen_kernel(places, feed_ref, *refs):
    pieces, out_ref = refs[:-1], refs[-1]
    count = feed_ref.shape[0]
    for first in range(0, count, ROWS):
        rows = pl.ds(first, ROWS)
        sums = [None, None]
        for (matrix, place), ref in zip(places, pieces):
            columns = pl.ds(pl.multiple_of(place(), 128), ref.shape[0])
            part = dot(feed_ref[rows, columns], ref[...])
            sums[matrix] = part if sums[matrix] is None else sums[matrix] + part
        out_ref[rows, :] = (silu(sums[0]) * sums[1]).astype(BF16)


def widen(feed, matrices):
    count, width = feed.shape
    pieces = [piece for matrix in matrices for piece, _ in matrix]
    places = [(i, place) for i, matrix in enumerate(matrices) for _, place in matrix]
    hidden = pieces[0].shape[1]
    return pl.pallas_call(
        functools.partial(widen_kernel, places),
        name="widen",
        grid=(pl.cdiv(hidden, WIDE),),
        in_specs=[fixed((count, width))]
        + [pl.BlockSpec((piece.shape[0], WIDE), lambda i: (0, i)) for piece in pieces],
        out_specs=pl.BlockSpec((count, WIDE), lambda i: (0, i)),
        out_shape=jax.ShapeDtypeStruct((count, hidden), BF16),
        compiler_params=params(24),
        cost_estimate=cost(1000, 1000),
    )(feed, *pieces)


def narrow_kernel(block, hidden_hbm, *refs):
    count = (len(refs) - 5) // 2
    pieces, theirs_ref, own_ref, hidden = refs[:count], *refs[count : count + 3]
    weights, sem, sems = refs[count + 3 : -2], refs[-2], refs[-1]
    rows = hidden.shape[0] // 2
    mine = lax.axis_index("hid")
    wholes = [
        pltpu.make_async_copy(
            hidden_hbm.at[pl.ds(pl.multiple_of(half * rows, rows), rows), :],
            hidden.at[pl.ds(i * rows, rows), :],
            sem.at[i],
        )
        for i, half in enumerate((1 - mine, mine))
    ]
    copies = [
        pltpu.make_async_copy(ref, weight, sems.at[i])
        for i, (ref, weight) in enumerate(zip(pieces, weights))
    ]
    for copy in wholes + copies:
        copy.start()
    for copy in wholes:
        copy.wait()
    at = 0
    for copy, weight in zip(copies, weights):
        copy.wait()
        for low in range(0, weight.shape[1], WIDE):
            for first in range(0, 2 * rows, block):
                total = product(hidden, pl.ds(first, block), weight, pl.ds(low, WIDE)).astype(BF16)
                for out_ref, start in ((theirs_ref, 0), (own_ref, rows)):
                    if first < start + rows and start < first + block:
                        taken = total[max(start - first, 0) : start + rows - first]
                        out_ref[pl.ds(max(first - start, 0), taken.shape[0]), pl.ds(at, WIDE)] = taken
            at += WIDE


def narrow(hidden, pieces, block):
    count, depth = hidden.shape
    width = sum(piece.shape[1] for piece in pieces)
    return pl.pallas_call(
        functools.partial(narrow_kernel, block),
        name="narrow",
        in_specs=[pl.BlockSpec(memory_space=pl.ANY)] * (1 + len(pieces)),
        out_specs=[pl.BlockSpec(memory_space=pltpu.VMEM)] * 2,
        out_shape=[jax.ShapeDtypeStruct((count // 2, width), BF16)] * 2,
        scratch_shapes=[pltpu.VMEM((count, depth), BF16)]
        + [pltpu.VMEM(piece.shape, BF16) for piece in pieces]
        + [pltpu.SemaphoreType.DMA((2,)), pltpu.SemaphoreType.DMA((len(pieces),))],
        compiler_params=params(20),
        cost_estimate=cost(1000, 1000),
    )(hidden, *pieces)


def close_kernel(places, residual_ref, *refs):
    out_ref = refs[-1]
    for group, (own_ref, received_ref) in zip(places, zip(refs[:-1:2], refs[1:-1:2])):
        at = 0
        for size, place in group:
            columns, span = pl.ds(pl.multiple_of(place(), 128), size), pl.ds(at, size)
            total = own_ref[:, span].astype(F32) + received_ref[:, span].astype(F32)
            out_ref[:, columns] = (residual_ref[:, columns].astype(F32) + total).astype(BF16)
            at += size


def close(residual, groups):
    count, width = residual.shape
    rows = lambda n: pl.BlockSpec((TILE, n), lambda i: (i, 0))
    arrays = [array for own, received, _ in groups for array in (own, received)]
    return pl.pallas_call(
        functools.partial(close_kernel, [group[2] for group in groups]),
        name="close",
        grid=(count // TILE,),
        in_specs=[rows(width)] + [rows(array.shape[1]) for array in arrays],
        out_specs=rows(width),
        out_shape=jax.ShapeDtypeStruct((count, width), BF16),
        compiler_params=params(12),
        cost_estimate=cost(1000, 1000),
    )(residual, *arrays)


def shifted(value, steps):
    count = lax.axis_size("seq")
    return lax.ppermute(value, "seq", [(i, i + steps) for i in range(count - steps)])


def swapped(value, axis, flip):
    count = lax.axis_size(axis)
    return lax.ppermute(value, axis, [(i, i ^ flip) for i in range(count)])


def after(value, *others):
    return lax.optimization_barrier((value, *others))[0]


def on_device(
    tokens, attention_gain, project_weight, conv_weight, decay_down, decay_up, decay_bias,
    output_gate, head_gain, output_weight, mixer_gain, gate_weight, up_weight, down_weight,
    prompt_pages, prompt_start,
):
    count, width = tokens.shape
    prompts = (prompt_pages, prompt_start)
    two_by_two = lax.axis_size("req") == 4 and lax.axis_size("seq") % 2 == 0
    hid_index = lax.axis_index("hid").astype(jnp.int32)[None]
    x, y = functools.partial(swapped, axis="req", flip=1), functools.partial(swapped, axis="req", flip=2)
    z = functools.partial(swapped, axis="seq", flip=1)
    depth = gate_weight.shape[0]
    half = depth // 2

    tied = lax.optimization_barrier
    if two_by_two:
        parity = lax.rem(lax.axis_index("seq"), 2)
        up_mine = lax.dynamic_slice_in_dim(up_weight, parity * half, half, 0)
        up_a, up_b = x(up_mine), y(up_mine)
        gate_a, gate_b = x(gate_weight), y(gate_weight)
    rim = shifted(tokens[-RIM:], 1)
    rim, other_output = lax.optimization_barrier((rim, swapped(output_weight, "hid", 1)))

    normed, sums, lowered, weighted, value, ends, edges, state = front(
        prompts, tokens, rim, attention_gain[None], project_weight, decay_down.T, decay_up,
        decay_bias[None], conv_weight,
    )
    one = shifted(state, 1)
    two = shifted(joined(state, one), 2)
    if two_by_two:
        down_0, down_1 = down_weight[:, :half], down_weight[:, half:]
        normed, gate_a, gate_b = tied((normed, gate_a, gate_b))
        gate_c, down_b1 = x(gate_b), y(down_1)
    raised, query_edges, opening = query(
        prompts, normed, rim, attention_gain[None], project_weight, output_gate, conv_weight, sums,
    )
    if two_by_two:
        one, two, raised, up_a, up_b, down_0 = tied((one, two, raised, up_a, up_b, down_0))
        up_c, far_a, far_b, down_a0 = y(up_a), z(up_a), z(up_b), x(down_0)
        down_c0 = y(down_a0)
    states, *gated = pages(
        prompts, raised, lowered, weighted, value, ends, opening, head_gain[None], one, two,
    )
    others = [swapped(part, "hid", 1) for part in gated]
    if two_by_two:
        others, up_c, gate_c, far_a, down_b1 = tied((others, up_c, gate_c, far_a, down_b1))
        far_c = y(far_a)
    residual, feed = mix(hid_index, tokens, gated, others, output_weight, other_output, mixer_gain[None])

    if two_by_two:
        feed, down_0, down_1 = tied((feed, down_0, down_1))
        down_b0, down_a1 = y(down_0), x(down_1)
        feed, far_b, far_c, down_b1 = tied((feed, far_b, far_c, down_b1))
        down_c1 = x(down_b1)
        at = lambda flip, more=0: lambda: (lax.axis_index("req") ^ flip) * depth + more
        own = lambda flip: lambda: at(flip)() + lax.rem(lax.axis_index("seq"), 2) * half
        far = lambda flip: lambda: at(flip)() + (1 - lax.rem(lax.axis_index("seq"), 2)) * half
        gate_list = [(gate_weight, at(0)), (gate_a, at(1)), (gate_b, at(2)), (gate_c, at(3))]
        up_list = [
            (up_weight, at(0)), (up_a, own(1)), (far_a, far(1)), (up_b, own(2)), (far_b, far(2)),
            (up_c, own(3)), (far_c, far(3)),
        ]
        down_lists = [
            [(down_weight, at(0)), (down_a0, at(1)), (down_b1, at(2, half)), (down_b0, at(2))],
            [(down_a1, at(1, half)), (down_c0, at(3)), (down_c1, at(3, half))],
        ]
    else:
        first = lambda: 0
        gate_list = [(lax.all_gather(gate_weight, "req", axis=0, tiled=True), first)]
        up_list = [(lax.all_gather(up_weight, "req", axis=0, tiled=True), first)]
        down_lists = [[(lax.all_gather(down_weight, "req", axis=1, tiled=True), first)]]

    hidden = widen(feed, (gate_list, up_list))
    groups = []
    for pieces in down_lists:
        theirs, mine = narrow(hidden, [piece for piece, _ in pieces], ROWS)
        received = swapped(theirs, "hid", 1)
        groups.append((mine, received, [(piece.shape[1], place) for piece, place in pieces]))
    result = close(residual, groups)
    return result, states, jnp.concatenate([query_edges, edges], axis=-1)


def solution(mesh):
    return jax.shard_map(
        on_device,
        mesh=mesh,
        in_specs=(
            P(("req", "seq"), None),
            P(),
            P(None, "hid"),
            P(None, "hid"),
            P(),
            P(None, "hid"),
            P("hid"),
            P(None, "hid"),
            P(),
            P("hid", None),
            P(),
            P("req", "hid"),
            P("req", "hid"),
            P("hid", "req"),
            P("req", None),
            P("req", None),
        ),
        out_specs=(
            P(("req", "seq", "hid"), None),
            P(("req", "seq"), "hid", None, None),
            P(("req", "seq"), None, "hid"),
        ),
        check_vma=False,
    )
```

```python
import functools

import jax
import jax.numpy as jnp
from jax import lax
from jax.experimental import pallas as pl
from jax.experimental.pallas import tpu as pltpu
from jax.sharding import PartitionSpec as P

HK = 256
HV = 512
KCONV = 4
PAGE = 64
CONVW = 1024
EPSILON = 1e-06
TILE = 256
PAGES_T = TILE // PAGE
RIM = 16
BF16 = jnp.bfloat16
F32 = jnp.float32
WIDE = 256
WIDEN_VMEM = 30
FINISH_VMEM = 24
FRONT = 256
QUERY = 512
MIX = 256
ROWS = 512


def params(mebibytes):
    return pltpu.CompilerParams(vmem_limit_bytes=mebibytes * 1024 * 1024)


def cost(flops, moved):
    return pl.CostEstimate(flops=flops, bytes_accessed=moved, transcendentals=0)


def fixed(shape):
    return pl.BlockSpec(
        shape, lambda *_: (0,) * len(shape), pipeline_mode=pl.Buffered(1)
    )


def whole_smem():
    return pl.BlockSpec(memory_space=pltpu.SMEM)


def dot(a, b):
    return jnp.dot(a, b, preferred_element_type=F32)


def dot_nt(a, b):
    return lax.dot_general(a, b, (((1,), (1,)), ((), ())), preferred_element_type=F32)


def dot_tn(a, b):
    return lax.dot_general(a, b, (((0,), (0,)), ((), ())), preferred_element_type=F32)


def silu(x):
    return x / (1.0 + jnp.exp(-x))


def column(row):
    return jnp.transpose(jnp.broadcast_to(row, (128, row.shape[1])))[:, :1]


def normalised(x, gain):
    return x * lax.rsqrt(jnp.mean(x * x, axis=-1, keepdims=True) + EPSILON) * gain


def carried_flag(pages_ref, start_ref, page, count):
    page = lax.axis_index("seq") * count + page
    same = jnp.int32(0)
    for i in range(pages_ref.shape[1]):
        first = start_ref[0, i]
        same = jnp.where((page > first) & (page < first + pages_ref[0, i]), 1, same)
    return same.astype(F32)


def product(left, rows, weight_ref, columns, step=512):
    depth = weight_ref.shape[0]
    total = None
    for k in range(0, depth, step):
        span = pl.ds(k, min(step, depth - k))
        part = dot(left[rows, span], weight_ref[span, columns])
        total = part if total is None else total + part
    return total


def rms_columns(read, write, gain_ref, width):
    total = None
    for low in range(0, width, WIDE):
        x = read(pl.ds(low, WIDE))
        square = x * x
        part = square[:, : WIDE // 2] + square[:, WIDE // 2 :]
        total = part if total is None else total + part
    scale = lax.rsqrt(jnp.sum(total, axis=-1, keepdims=True) * (1.0 / width) + EPSILON)
    for low in range(0, width, WIDE):
        columns = pl.ds(low, WIDE)
        write(columns, read(columns) * scale * gain_ref[:, columns].astype(F32))


def norm_into(normed, gain_ref, blocks):
    for ref, source, target, count in blocks:
        def read(columns, ref=ref, source=source, count=count):
            return ref[pl.ds(source, count), columns].astype(F32)

        def write(columns, x, target=target, count=count):
            normed[pl.ds(target, count), columns] = x.astype(BF16)

        rms_columns(read, write, gain_ref, normed.shape[1])


def short_conv(projected, previous, carried, taps, j):
    now = projected[j * PAGE : (j + 1) * PAGE]
    before = previous if j == 0 else projected[j * PAGE - 8 : j * PAGE]
    widened = jnp.concatenate([before * carried, now], axis=0)
    mixed = taps[0:1] * now
    for i in range(1, KCONV):
        mixed = mixed + taps[i : i + 1] * widened[8 - i : 8 - i + PAGE]
    return mixed


def page_edge(low, j):
    return low[(j + 1) * PAGE - (KCONV - 1) : (j + 1) * PAGE]


def front_kernel(
    pages_ref, start_ref, tokens_ref, rim_ref, gain_ref, key_ref, first_ref, second_ref, down_ref, up_ref,
    bias_ref, conv_ref, normed_ref, sums_ref, lowered_ref, weighted_ref, value_ref, ends_ref, edges_ref,
    state_ref, normed, carry, state, decay, keys,
):
    step = pl.program_id(0)
    tile = tokens_ref.shape[0]
    pages = tile // PAGE

    @pl.when(step == 0)
    def _():
        state[...] = jnp.zeros_like(state)
        decay[...] = jnp.ones_like(decay)

    norm_into(
        normed, gain_ref,
        [(rim_ref, 0, tile, RIM)] + [(tokens_ref, r, r, 128) for r in range(0, tile, 128)],
    )
    normed_ref[...] = normed[:tile]
    lowrank = dot_nt(normed[:tile], down_ref[...]).astype(BF16)
    logits = dot(lowrank, up_ref[...]) + bias_ref[...]
    decay_log = (jnp.minimum(logits, 0.0) - jnp.log1p(jnp.exp(-jnp.abs(logits)))) / 16.0
    row = lax.broadcasted_iota(jnp.int32, (HK, HK), 0)
    col = lax.broadcasted_iota(jnp.int32, (HK, HK), 1)
    lower = jnp.where((row >= col) & ((row // PAGE) == (col // PAGE)), 1.0, 0.0).astype(F32)
    for r in range(0, tile, HK):
        sums_ref[pl.ds(r, HK), :] = jnp.dot(
            lower, decay_log[r : r + HK], preferred_element_type=F32, precision=lax.Precision.HIGHEST
        )
    carried = [
        carried_flag(pages_ref, start_ref, step * pages + j, pl.num_programs(0) * pages)
        for j in range(pages)
    ]
    ends = [sums_ref[pl.ds((j + 1) * PAGE - 8, 8), :][7:] for j in range(pages)]
    suffix = [None] * pages + [jnp.ones((1, HK), F32)]
    for j in reversed(range(pages)):
        kept = jnp.exp(ends[j])
        ends_ref[j] = jnp.broadcast_to(kept, (8, HK))
        suffix[j] = suffix[j + 1] * (kept * carried[j])

    for chunk, weight_ref in enumerate((key_ref, first_ref, second_ref)):
        columns = pl.ds(chunk * WIDE, WIDE)
        low = product(normed, slice(None), weight_ref, slice(None)).astype(BF16)
        projected = low[:tile].astype(F32)
        previous = jnp.where(step == 0, low[tile:].astype(F32)[RIM - 8 :], carry[:, columns])
        carry[:, columns] = projected[tile - 8 :]
        taps = conv_ref[:, pl.ds(HK + chunk * WIDE, WIDE)].astype(F32)
        for j in range(pages):
            mixed = short_conv(projected, previous, carried[j], taps, j)
            span = pl.ds(j * PAGE, PAGE)
            edges_ref[j, :, columns] = page_edge(low, j)
            if chunk == 0:
                key = silu(mixed) * HK ** (-0.5)
                sums = sums_ref[span, :]
                weighted = key * jnp.exp(ends[j] - sums)
                lowered_ref[span, :] = (key * jnp.exp(-sums)).astype(BF16)
                weighted_ref[span, :] = weighted.astype(BF16)
                keys[span, :] = (weighted * suffix[j + 1]).astype(BF16)
            else:
                value_ref[span, pl.ds((chunk - 1) * WIDE, WIDE)] = mixed.astype(BF16)
    state[...] = column(suffix[0]) * state[...] + dot_tn(keys[...], value_ref[...])
    decay[...] = decay[...] * suffix[0]

    @pl.when(step == pl.num_programs(0) - 1)
    def _():
        state_ref[:HK] = state[...].astype(BF16)
        block = jnp.concatenate([decay[...]] * (HV // HK), axis=1)
        state_ref[HK:] = jnp.concatenate([block] * (RIM // 8), axis=0).astype(BF16)


def column_block(height, i):
    return pl.BlockSpec((height, WIDE), lambda *_: (0, i), pipeline_mode=pl.Buffered(1))


def front(prompts, tokens, rim, gain, project, down, up, bias, conv):
    count, width = tokens.shape
    rank = down.shape[0]
    pages = count // PAGE
    tile = FRONT
    rows = lambda n: pl.BlockSpec((tile, n), lambda i: (i, 0))
    shape = jax.ShapeDtypeStruct
    return pl.pallas_call(
        front_kernel,
        name="front",
        grid=(count // tile,),
        in_specs=[
            whole_smem(), whole_smem(), rows(width), fixed((RIM, width)), fixed((1, width)),
            column_block(width, 1), column_block(width, 2), column_block(width, 3),
            fixed((rank, width)), fixed((rank, HK)), fixed((1, HK)), fixed((KCONV, CONVW)),
        ],
        out_specs=[
            rows(width), rows(HK), rows(HK), rows(HK), rows(HV),
            pl.BlockSpec((tile // PAGE, 8, HK), lambda i: (i, 0, 0)),
            pl.BlockSpec((tile // PAGE, KCONV - 1, HK + HV), lambda i: (i, 0, 0)),
            fixed((HK + RIM, HV)),
        ],
        out_shape=[
            shape((count, width), BF16), shape((count, HK), F32), shape((count, HK), BF16),
            shape((count, HK), BF16), shape((count, HV), BF16), shape((pages, 8, HK), F32),
            shape((pages, KCONV - 1, HK + HV), BF16), shape((HK + RIM, HV), BF16),
        ],
        scratch_shapes=[
            pltpu.VMEM((tile + RIM, width), BF16), pltpu.VMEM((8, HK + HV), F32),
            pltpu.VMEM((HK, HV), F32), pltpu.VMEM((8, HK), F32), pltpu.VMEM((tile, HK), BF16),
        ],
        compiler_params=params(44),
        cost_estimate=cost(1000, 1000),
    )(*prompts, tokens, rim, gain, project, project, project, down, up, bias, conv)


def query_kernel(
    pages_ref, start_ref, normed_ref, rim_ref, gain_ref, query_ref, gate_ref, conv_ref, sums_ref,
    raised_ref, edges_ref, opening_ref, normed_rim, carry,
):
    step = pl.program_id(0)
    tile = normed_ref.shape[0]
    pages = tile // PAGE

    @pl.when(step == 0)
    def _():
        norm_into(normed_rim, gain_ref, [(rim_ref, 0, 0, RIM)])
        low = product(normed_rim, slice(None), query_ref, slice(None)).astype(BF16)
        carry[...] = low.astype(F32)[RIM - 8 :]

    low = product(normed_ref, slice(None), query_ref, slice(None)).astype(BF16)
    projected = low.astype(F32)
    previous = carry[...]
    taps = conv_ref[:, :HK].astype(F32)
    for j in range(pages):
        carried = carried_flag(pages_ref, start_ref, step * pages + j, pl.num_programs(0) * pages)
        mixed = short_conv(projected, previous, carried, taps, j)
        span = pl.ds(j * PAGE, PAGE)
        edges_ref[j] = page_edge(low, j)
        raised_ref[span, :] = (silu(mixed) * jnp.exp(sums_ref[span, :])).astype(BF16)
    carry[...] = projected[tile - 8 :]
    for at in range(0, HV, WIDE):
        columns = pl.ds(at, WIDE)
        opening_ref[:, columns] = silu(product(normed_ref, slice(None), gate_ref, columns)).astype(BF16)


def query(prompts, normed, rim, gain, project, gate, conv, sums):
    count, width = normed.shape
    pages = count // PAGE
    tile = QUERY
    rows = lambda n: pl.BlockSpec((tile, n), lambda i: (i, 0))
    shape = jax.ShapeDtypeStruct
    return pl.pallas_call(
        query_kernel,
        name="query",
        grid=(count // tile,),
        in_specs=[
            whole_smem(), whole_smem(), rows(width), fixed((RIM, width)), fixed((1, width)),
            column_block(width, 0), fixed((width, HV)), fixed((KCONV, CONVW)), rows(HK),
        ],
        out_specs=[
            rows(HK), pl.BlockSpec((tile // PAGE, KCONV - 1, HK), lambda i: (i, 0, 0)), rows(HV),
        ],
        out_shape=[
            shape((count, HK), BF16), shape((pages, KCONV - 1, HK), BF16), shape((count, HV), BF16),
        ],
        scratch_shapes=[pltpu.VMEM((RIM, width), BF16), pltpu.VMEM((8, HK), F32)],
        compiler_params=params(20),
        cost_estimate=cost(2 * count * width * (HK + HV), 2 * count * width),
    )(*prompts, normed, rim, gain, project, gate, conv, sums)


def composed(later, earlier):
    kept = column(later[HK:].astype(F32)[:1, :HK])
    return later[:HK].astype(F32) + kept * earlier[:HK].astype(F32)


def joined_kernel(later_ref, earlier_ref, out_ref):
    out_ref[:HK] = composed(later_ref, earlier_ref).astype(BF16)
    out_ref[HK:] = later_ref[HK:]


def joined(later, earlier):
    return pl.pallas_call(
        joined_kernel, name="joined",
        in_specs=[pl.BlockSpec(memory_space=pltpu.VMEM)] * 2,
        out_specs=pl.BlockSpec(memory_space=pltpu.VMEM),
        out_shape=jax.ShapeDtypeStruct(later.shape, BF16),
        compiler_params=params(6),
        cost_estimate=cost(1000, 1000),
    )(later, earlier)


def halves(count, tile):
    half = count // tile // 2
    return [
        pl.BlockSpec((tile, HV), lambda i: (jnp.minimum(i, half - 1), 0)),
        pl.BlockSpec((tile, HV), lambda i: (jnp.maximum(i - half, 0), 0)),
    ]


def pages_kernel(
    pages_ref, start_ref, raised_ref, lowered_ref, weighted_ref, value_ref, ends_ref, opening_ref, gain_ref,
    one_ref, two_ref, states_ref, low_ref, high_ref, memory,
):
    step = pl.program_id(0)

    @pl.when(step == 0)
    def _():
        memory[...] = composed(one_ref, two_ref)

    row = lax.broadcasted_iota(jnp.int32, (PAGE, PAGE), 0)
    col = lax.broadcasted_iota(jnp.int32, (PAGE, PAGE), 1)
    gain = gain_ref[...].astype(F32)
    held = memory[...]
    gated_tile = []
    for j in range(PAGES_T):
        span = pl.ds(j * PAGE, PAGE)
        raised, value = raised_ref[span, :], value_ref[span, :]
        held = held * carried_flag(pages_ref, start_ref, step * PAGES_T + j, pl.num_programs(0) * PAGES_T)
        scores = dot_nt(raised, lowered_ref[span, :])
        scores = jnp.where(row >= col, scores, 0.0).astype(BF16)
        attended = dot(scores, value) + dot(raised, held.astype(BF16))
        held = column(ends_ref[j][:1]) * held + dot_tn(weighted_ref[span, :], value)
        states_ref[j, 0] = held.astype(BF16)
        gated = normalised(attended, gain) * opening_ref[span, :].astype(F32)
        gated_tile.append(gated.astype(BF16))
    memory[...] = held
    half = pl.num_programs(0) // 2

    @pl.when(step < half)
    def _():
        low_ref[...] = jnp.concatenate(gated_tile, axis=0)

    @pl.when(step >= half)
    def _():
        high_ref[...] = jnp.concatenate(gated_tile, axis=0)


def pages(prompts, raised, lowered, weighted, value, ends, opening, gain, one, two):
    count = raised.shape[0]
    total = count // PAGE
    rows = lambda n: pl.BlockSpec((TILE, n), lambda i: (i, 0))
    return pl.pallas_call(
        pages_kernel,
        name="pages",
        grid=(count // TILE,),
        in_specs=[
            whole_smem(), whole_smem(), rows(HK), rows(HK), rows(HK), rows(HV),
            pl.BlockSpec((PAGES_T, 8, HK), lambda i: (i, 0, 0)), rows(HV), fixed((1, HV)),
            fixed((HK + RIM, HV)), fixed((HK + RIM, HV)),
        ],
        out_specs=[
            pl.BlockSpec((PAGES_T, 1, HK, HV), lambda i: (i, 0, 0, 0)), *halves(count, TILE),
        ],
        out_shape=[
            jax.ShapeDtypeStruct((total, 1, HK, HV), BF16),
            jax.ShapeDtypeStruct((count // 2, HV), BF16),
            jax.ShapeDtypeStruct((count // 2, HV), BF16),
        ],
        scratch_shapes=[pltpu.VMEM((HK, HV), F32)],
        compiler_params=params(12),
        cost_estimate=cost(1000, 1000),
    )(*prompts, raised, lowered, weighted, value, ends, opening, gain, one, two)


def mix_kernel(
    tokens_ref, low_ref, high_ref, other_low_ref, other_high_ref, own_weight_ref, other_weight_ref,
    gain_ref, residual_ref, feed_ref, residual,
):
    first = pl.program_id(0) < pl.num_programs(0) // 2
    own = jnp.where(first, low_ref[...], high_ref[...])
    other = jnp.where(first, other_low_ref[...], other_high_ref[...])
    width = tokens_ref.shape[1]
    for at in range(0, width, WIDE):
        columns = pl.ds(at, WIDE)
        mixed = dot(own, own_weight_ref[:, columns]) + dot(other, other_weight_ref[:, columns])
        residual[:, columns] = (tokens_ref[:, columns].astype(F32) + mixed).astype(BF16)

    @pl.when(first == (lax.axis_index("hid") == 0))
    def _():
        residual_ref[...] = residual[...]

    def write(columns, x):
        feed_ref[:, columns] = x.astype(BF16)

    rms_columns(lambda columns: residual[:, columns].astype(F32), write, gain_ref, width)


def mix(hid_index, tokens, own, others, own_weight, other_weight, gain):
    count, width = tokens.shape
    tile = MIX
    half = count // tile // 2
    rows = pl.BlockSpec((tile, width), lambda i, s: (i, 0))
    halves = [
        pl.BlockSpec((tile, HV), lambda i, s: (jnp.minimum(i, half - 1), 0)),
        pl.BlockSpec((tile, HV), lambda i, s: (jnp.maximum(i - half, 0), 0)),
    ]
    mine = pl.BlockSpec((tile, width), lambda i, s: (jnp.clip(i - s[0] * half, 0, half - 1), 0))
    return pl.pallas_call(
        lambda s, *refs: mix_kernel(*refs),
        name="mix",
        grid_spec=pltpu.PrefetchScalarGridSpec(
            num_scalar_prefetch=1,
            grid=(count // tile,),
            in_specs=[rows, *halves, *halves, fixed((HV, width)), fixed((HV, width)), fixed((1, width))],
            out_specs=[mine, rows],
            scratch_shapes=[pltpu.VMEM((tile, width), BF16)],
        ),
        out_shape=[
            jax.ShapeDtypeStruct((count // 2, width), BF16), jax.ShapeDtypeStruct((count, width), BF16),
        ],
        compiler_params=params(20),
        cost_estimate=cost(1000, 1000),
    )(hid_index, tokens, *own, *others, own_weight, other_weight, gain)


def widen_sums(places, pieces, feed_ref, rows):
    sums = {}
    for (matrix, place), ref in zip(places, pieces):
        columns = pl.ds(pl.multiple_of(place(), 128), ref.shape[0])
        part = dot(feed_ref[rows, columns], ref[...])
        sums[matrix] = part if matrix not in sums else sums[matrix] + part
    return sums


def widen_kernel(places, feed_ref, *refs):
    pieces, (gate_ref, up_ref) = refs[:-2], refs[-2:]
    for first in range(0, feed_ref.shape[0], ROWS):
        rows = pl.ds(first, ROWS)
        sums = widen_sums(places, pieces, feed_ref, rows)
        gate_ref[rows, :] = silu(sums[0]).astype(BF16)
        up_ref[rows, :] = sums[1]


def finish_kernel(places, feed_ref, gate_ref, up_ref, *refs):
    pieces, out_ref = refs[:-1], refs[-1]
    for first in range(0, feed_ref.shape[0], ROWS):
        rows = pl.ds(first, ROWS)
        total = up_ref[rows, :]
        if pieces:
            total = total + widen_sums(places, pieces, feed_ref, rows)[1]
        out_ref[rows, :] = (gate_ref[rows, :].astype(F32) * total).astype(BF16)


def widen_call(kernel, name, limit, kinds, feed, wholes, matrices):
    count, width = feed.shape
    pieces = [piece for matrix in matrices for piece, _ in matrix]
    places = [(i, place) for i, matrix in enumerate(matrices) for _, place in matrix]
    hidden = (wholes or pieces)[0].shape[1]
    block = pl.BlockSpec((count, WIDE), lambda i: (0, i))
    return pl.pallas_call(
        functools.partial(kernel, places),
        name=name,
        grid=(pl.cdiv(hidden, WIDE),),
        in_specs=[fixed((count, width))] + [block] * len(wholes)
        + [pl.BlockSpec((piece.shape[0], WIDE), lambda i: (0, i)) for piece in pieces],
        out_specs=[block] * len(kinds),
        out_shape=[jax.ShapeDtypeStruct((count, hidden), kind) for kind in kinds],
        compiler_params=params(limit),
        cost_estimate=cost(1000, 1000),
    )(feed, *wholes, *pieces)


def widen(feed, matrices):
    return widen_call(widen_kernel, "widen", WIDEN_VMEM, (BF16, F32), feed, (), matrices)


def finish(feed, wholes, pieces):
    return widen_call(finish_kernel, "finish", FINISH_VMEM, (BF16,), feed, wholes, ([], pieces))[0]


def narrow_kernel(block, hidden_hbm, *refs):
    count = (len(refs) - 5) // 2
    pieces, theirs_ref, own_ref, hidden = refs[:count], *refs[count : count + 3]
    weights, sem, sems = refs[count + 3 : -2], refs[-2], refs[-1]
    rows = hidden.shape[0] // 2
    mine = lax.axis_index("hid")
    wholes = [
        pltpu.make_async_copy(
            hidden_hbm.at[pl.ds(pl.multiple_of(half * rows, rows), rows), :],
            hidden.at[pl.ds(i * rows, rows), :],
            sem.at[i],
        )
        for i, half in enumerate((1 - mine, mine))
    ]
    copies = [
        pltpu.make_async_copy(ref, weight, sems.at[i])
        for i, (ref, weight) in enumerate(zip(pieces, weights))
    ]
    for copy in wholes + copies:
        copy.start()
    for copy in wholes:
        copy.wait()
    at = 0
    for copy, weight in zip(copies, weights):
        copy.wait()
        for low in range(0, weight.shape[1], WIDE):
            for first in range(0, 2 * rows, block):
                total = product(hidden, pl.ds(first, block), weight, pl.ds(low, WIDE)).astype(BF16)
                for out_ref, start in ((theirs_ref, 0), (own_ref, rows)):
                    if first < start + rows and start < first + block:
                        taken = total[max(start - first, 0) : start + rows - first]
                        out_ref[pl.ds(max(first - start, 0), taken.shape[0]), pl.ds(at, WIDE)] = taken
            at += WIDE


def narrow(hidden, pieces, block):
    count, depth = hidden.shape
    width = sum(piece.shape[1] for piece in pieces)
    return pl.pallas_call(
        functools.partial(narrow_kernel, block),
        name="narrow",
        in_specs=[pl.BlockSpec(memory_space=pl.ANY)] * (1 + len(pieces)),
        out_specs=[pl.BlockSpec(memory_space=pltpu.VMEM)] * 2,
        out_shape=[jax.ShapeDtypeStruct((count // 2, width), BF16)] * 2,
        scratch_shapes=[pltpu.VMEM((count, depth), BF16)]
        + [pltpu.VMEM(piece.shape, BF16) for piece in pieces]
        + [pltpu.SemaphoreType.DMA((2,)), pltpu.SemaphoreType.DMA((len(pieces),))],
        compiler_params=params(20),
        cost_estimate=cost(1000, 1000),
    )(hidden, *pieces)


def close_kernel(places, residual_ref, *refs):
    out_ref = refs[-1]
    for group, (own_ref, received_ref) in zip(places, zip(refs[:-1:2], refs[1:-1:2])):
        at = 0
        for size, place in group:
            columns, span = pl.ds(pl.multiple_of(place(), 128), size), pl.ds(at, size)
            total = own_ref[:, span].astype(F32) + received_ref[:, span].astype(F32)
            out_ref[:, columns] = (residual_ref[:, columns].astype(F32) + total).astype(BF16)
            at += size


def close(residual, groups):
    count, width = residual.shape
    rows = lambda n: pl.BlockSpec((TILE, n), lambda i: (i, 0))
    arrays = [array for own, received, _ in groups for array in (own, received)]
    return pl.pallas_call(
        functools.partial(close_kernel, [group[2] for group in groups]),
        name="close",
        grid=(count // TILE,),
        in_specs=[rows(width)] + [rows(array.shape[1]) for array in arrays],
        out_specs=rows(width),
        out_shape=jax.ShapeDtypeStruct((count, width), BF16),
        compiler_params=params(12),
        cost_estimate=cost(1000, 1000),
    )(residual, *arrays)


def shifted(value, steps):
    count = lax.axis_size("seq")
    return lax.ppermute(value, "seq", [(i, i + steps) for i in range(count - steps)])


def swapped(value, axis, flip):
    count = lax.axis_size(axis)
    return lax.ppermute(value, axis, [(i, i ^ flip) for i in range(count)])


def after(value, *others):
    return lax.optimization_barrier((value, *others))[0]


def on_device(
    tokens, attention_gain, project_weight, conv_weight, decay_down, decay_up, decay_bias,
    output_gate, head_gain, output_weight, mixer_gain, gate_weight, up_weight, down_weight,
    prompt_pages, prompt_start,
):
    count, width = tokens.shape
    prompts = (prompt_pages, prompt_start)
    two_by_two = lax.axis_size("req") == 4 and lax.axis_size("seq") % 2 == 0
    hid_index = lax.axis_index("hid").astype(jnp.int32)[None]
    x, y = functools.partial(swapped, axis="req", flip=1), functools.partial(swapped, axis="req", flip=2)
    z = functools.partial(swapped, axis="seq", flip=1)
    depth = gate_weight.shape[0]
    half = depth // 2

    tied = lax.optimization_barrier
    if two_by_two:
        parity = lax.rem(lax.axis_index("seq"), 2)
        up_mine = lax.dynamic_slice_in_dim(up_weight, parity * half, half, 0)
        up_a, up_b = x(up_mine), y(up_mine)
        gate_a, gate_b = x(gate_weight), y(gate_weight)
    rim = shifted(tokens[-RIM:], 1)
    rim, other_output = lax.optimization_barrier((rim, swapped(output_weight, "hid", 1)))

    normed, sums, lowered, weighted, value, ends, edges, state = front(
        prompts, tokens, rim, attention_gain[None], project_weight, decay_down.T, decay_up,
        decay_bias[None], conv_weight,
    )
    one = shifted(state, 1)
    both = joined(state, one)
    two = shifted(both, 2)
    if two_by_two:
        mine, rest = (
            lax.dynamic_slice_in_dim(down_weight, p * half, half, 1) for p in (parity, 1 - parity)
        )
        normed, gate_a, gate_b, both = tied((normed, gate_a, gate_b, both))
        gate_c = x(gate_b)
    raised, query_edges, opening = query(
        prompts, normed, rim, attention_gain[None], project_weight, output_gate, conv_weight, sums,
    )
    if two_by_two:
        raised, up_a, up_b = tied((raised, up_a, up_b))
        up_c, far_a = y(up_a), z(up_a)
    states, *gated = pages(
        prompts, raised, lowered, weighted, value, ends, opening, head_gain[None], one, two,
    )
    others = [swapped(part, "hid", 1) for part in gated]
    if two_by_two:
        far_b, down_b_rest, down_a = z(up_b), y(rest), x(mine)
        others, far_a, up_c = tied((others, far_a, up_c))
        far_c = z(up_c)
    residual, feed = mix(hid_index, tokens, gated, others, output_weight, other_output, mixer_gain[None])

    if two_by_two:
        feed, mine = tied((feed, mine))
        down_b = y(mine)
        at = lambda flip: lambda: (lax.axis_index("req") ^ flip) * depth
        own = lambda flip: lambda: at(flip)() + lax.rem(lax.axis_index("seq"), 2) * half
        far = lambda flip: lambda: at(flip)() + (1 - lax.rem(lax.axis_index("seq"), 2)) * half
        gate_list = [(gate_weight, at(0)), (gate_a, at(1)), (gate_b, at(2)), (gate_c, at(3))]
        up_list = [
            (up_weight, at(0)), (up_a, own(1)), (far_a, far(1)), (up_b, own(2)), (up_c, own(3)),
        ]
        sums = widen(feed, (gate_list, up_list))
        sums, down_b_rest, down_a = tied((sums, down_b_rest, down_a))
        down_c_rest, down_c, down_a_far = x(down_b_rest), y(down_a), z(down_a)
        hidden = finish(feed, sums, [(far_b, far(2)), (far_c, far(3))])
        down_lists = [
            [(down_weight, at(0)), (down_a, own(1)), (down_b_rest, far(2)), (down_b, own(2))],
            [(down_c_rest, far(3)), (down_c, own(3)), (down_a_far, far(1))],
        ]
    else:
        first = lambda: 0
        gate_list = [(lax.all_gather(gate_weight, "req", axis=0, tiled=True), first)]
        up_list = [(lax.all_gather(up_weight, "req", axis=0, tiled=True), first)]
        down_lists = [[(lax.all_gather(down_weight, "req", axis=1, tiled=True), first)]]
        hidden = finish(feed, widen(feed, (gate_list, up_list)), [])

    groups = []
    for pieces in down_lists:
        theirs, mine = narrow(hidden, [piece for piece, _ in pieces], ROWS)
        received = swapped(theirs, "hid", 1)
        groups.append((mine, received, [(piece.shape[1], place) for piece, place in pieces]))
    result = close(residual, groups)
    return result, states, jnp.concatenate([query_edges, edges], axis=-1)


def solution(mesh):
    return jax.shard_map(
        on_device,
        mesh=mesh,
        in_specs=(
            P(("req", "seq"), None),
            P(),
            P(None, "hid"),
            P(None, "hid"),
            P(),
            P(None, "hid"),
            P("hid"),
            P(None, "hid"),
            P(),
            P("hid", None),
            P(),
            P("req", "hid"),
            P("req", "hid"),
            P("hid", "req"),
            P("req", None),
            P("req", None),
        ),
        out_specs=(
            P(("req", "seq", "hid"), None),
            P(("req", "seq"), "hid", None, None),
            P(("req", "seq"), None, "hid"),
        ),
        check_vma=False,
    )
```

```python
import functools

import jax
import jax.numpy as jnp
from jax import lax
from jax.experimental import pallas as pl
from jax.experimental.pallas import tpu as pltpu
from jax.sharding import PartitionSpec as P

HK = 256
HV = 512
KCONV = 4
PAGE = 64
CONVW = 1024
EPSILON = 1e-06
TILE = 256
PAGES_T = TILE // PAGE
RIM = 16
BF16 = jnp.bfloat16
F32 = jnp.float32
WIDE = 256
WIDEN_VMEM = 30
FINISH_VMEM = 24
FRONT = 256
QUERY = 512
MIX = 256
ROWS = 512


def params(mebibytes):
    return pltpu.CompilerParams(vmem_limit_bytes=mebibytes * 1024 * 1024)


def cost(flops, moved):
    return pl.CostEstimate(flops=flops, bytes_accessed=moved, transcendentals=0)


def fixed(shape):
    return pl.BlockSpec(
        shape, lambda *_: (0,) * len(shape), pipeline_mode=pl.Buffered(1)
    )


def held(array):
    return pltpu.with_memory_space_constraint(array, pltpu.HBM)


def whole_smem():
    return pl.BlockSpec(memory_space=pltpu.SMEM)


def dot(a, b):
    return jnp.dot(a, b, preferred_element_type=F32)


def dot_nt(a, b):
    return lax.dot_general(a, b, (((1,), (1,)), ((), ())), preferred_element_type=F32)


def dot_tn(a, b):
    return lax.dot_general(a, b, (((0,), (0,)), ((), ())), preferred_element_type=F32)


def silu(x):
    return x / (1.0 + jnp.exp(-x))


def column(row):
    return jnp.transpose(jnp.broadcast_to(row, (128, row.shape[1])))[:, :1]


def normalised(x, gain):
    return x * lax.rsqrt(jnp.mean(x * x, axis=-1, keepdims=True) + EPSILON) * gain


def carried_flag(pages_ref, start_ref, page, count):
    page = lax.axis_index("seq") * count + page
    same = jnp.int32(0)
    for i in range(pages_ref.shape[1]):
        first = start_ref[0, i]
        same = jnp.where((page > first) & (page < first + pages_ref[0, i]), 1, same)
    return same.astype(F32)


def product(left, rows, weight_ref, columns, step=512):
    depth = weight_ref.shape[0]
    total = None
    for k in range(0, depth, step):
        span = pl.ds(k, min(step, depth - k))
        part = dot(left[rows, span], weight_ref[span, columns])
        total = part if total is None else total + part
    return total


def rms_columns(read, write, gain_ref, width):
    total = None
    for low in range(0, width, WIDE):
        x = read(pl.ds(low, WIDE))
        square = x * x
        part = square[:, : WIDE // 2] + square[:, WIDE // 2 :]
        total = part if total is None else total + part
    scale = lax.rsqrt(jnp.sum(total, axis=-1, keepdims=True) * (1.0 / width) + EPSILON)
    for low in range(0, width, WIDE):
        columns = pl.ds(low, WIDE)
        write(columns, read(columns) * scale * gain_ref[:, columns].astype(F32))


def norm_into(normed, gain_ref, blocks):
    for ref, source, target, count in blocks:
        def read(columns, ref=ref, source=source, count=count):
            return ref[pl.ds(source, count), columns].astype(F32)

        def write(columns, x, target=target, count=count):
            normed[pl.ds(target, count), columns] = x.astype(BF16)

        rms_columns(read, write, gain_ref, normed.shape[1])


def short_conv(projected, previous, carried, taps, j):
    now = projected[j * PAGE : (j + 1) * PAGE]
    before = previous if j == 0 else projected[j * PAGE - 8 : j * PAGE]
    widened = jnp.concatenate([before * carried, now], axis=0)
    mixed = taps[0:1] * now
    for i in range(1, KCONV):
        mixed = mixed + taps[i : i + 1] * widened[8 - i : 8 - i + PAGE]
    return mixed


def page_edge(low, j):
    return low[(j + 1) * PAGE - (KCONV - 1) : (j + 1) * PAGE]


def front_kernel(
    pages_ref, start_ref, tokens_ref, rim_ref, gain_ref, key_ref, first_ref, second_ref, down_ref, up_ref,
    bias_ref, conv_ref, normed_ref, sums_ref, lowered_ref, weighted_ref, value_ref, ends_ref, edges_ref,
    state_ref, normed, carry, state, decay, keys,
):
    step = pl.program_id(0)
    tile = tokens_ref.shape[0]
    pages = tile // PAGE

    @pl.when(step == 0)
    def _():
        state[...] = jnp.zeros_like(state)
        decay[...] = jnp.ones_like(decay)

    norm_into(
        normed, gain_ref,
        [(rim_ref, 0, tile, RIM)] + [(tokens_ref, r, r, 128) for r in range(0, tile, 128)],
    )
    normed_ref[...] = normed[:tile]
    lowrank = dot_nt(normed[:tile], down_ref[...]).astype(BF16)
    logits = dot(lowrank, up_ref[...]) + bias_ref[...]
    decay_log = (jnp.minimum(logits, 0.0) - jnp.log1p(jnp.exp(-jnp.abs(logits)))) / 16.0
    row = lax.broadcasted_iota(jnp.int32, (HK, HK), 0)
    col = lax.broadcasted_iota(jnp.int32, (HK, HK), 1)
    lower = jnp.where((row >= col) & ((row // PAGE) == (col // PAGE)), 1.0, 0.0).astype(F32)
    for r in range(0, tile, HK):
        sums_ref[pl.ds(r, HK), :] = jnp.dot(
            lower, decay_log[r : r + HK], preferred_element_type=F32, precision=lax.Precision.HIGHEST
        )
    carried = [
        carried_flag(pages_ref, start_ref, step * pages + j, pl.num_programs(0) * pages)
        for j in range(pages)
    ]
    ends = [sums_ref[pl.ds((j + 1) * PAGE - 8, 8), :][7:] for j in range(pages)]
    suffix = [None] * pages + [jnp.ones((1, HK), F32)]
    for j in reversed(range(pages)):
        kept = jnp.exp(ends[j])
        ends_ref[j] = jnp.broadcast_to(kept, (8, HK))
        suffix[j] = suffix[j + 1] * (kept * carried[j])

    for chunk, weight_ref in enumerate((key_ref, first_ref, second_ref)):
        columns = pl.ds(chunk * WIDE, WIDE)
        low = product(normed, slice(None), weight_ref, slice(None)).astype(BF16)
        projected = low[:tile].astype(F32)
        previous = jnp.where(step == 0, low[tile:].astype(F32)[RIM - 8 :], carry[:, columns])
        carry[:, columns] = projected[tile - 8 :]
        taps = conv_ref[:, pl.ds(HK + chunk * WIDE, WIDE)].astype(F32)
        for j in range(pages):
            mixed = short_conv(projected, previous, carried[j], taps, j)
            span = pl.ds(j * PAGE, PAGE)
            edges_ref[j, :, columns] = page_edge(low, j)
            if chunk == 0:
                key = silu(mixed) * HK ** (-0.5)
                sums = sums_ref[span, :]
                weighted = key * jnp.exp(ends[j] - sums)
                lowered_ref[span, :] = (key * jnp.exp(-sums)).astype(BF16)
                weighted_ref[span, :] = weighted.astype(BF16)
                keys[span, :] = (weighted * suffix[j + 1]).astype(BF16)
            else:
                value_ref[span, pl.ds((chunk - 1) * WIDE, WIDE)] = mixed.astype(BF16)
    state[...] = column(suffix[0]) * state[...] + dot_tn(keys[...], value_ref[...])
    decay[...] = decay[...] * suffix[0]

    @pl.when(step == pl.num_programs(0) - 1)
    def _():
        state_ref[:HK] = state[...].astype(BF16)
        block = jnp.concatenate([decay[...]] * (HV // HK), axis=1)
        state_ref[HK:] = jnp.concatenate([block] * (RIM // 8), axis=0).astype(BF16)


def column_block(height, i):
    return pl.BlockSpec((height, WIDE), lambda *_: (0, i), pipeline_mode=pl.Buffered(1))


def front(prompts, tokens, rim, gain, project, down, up, bias, conv):
    count, width = tokens.shape
    rank = down.shape[0]
    pages = count // PAGE
    tile = FRONT
    rows = lambda n: pl.BlockSpec((tile, n), lambda i: (i, 0))
    shape = jax.ShapeDtypeStruct
    return pl.pallas_call(
        front_kernel,
        name="front",
        grid=(count // tile,),
        in_specs=[
            whole_smem(), whole_smem(), rows(width), fixed((RIM, width)), fixed((1, width)),
            column_block(width, 1), column_block(width, 2), column_block(width, 3),
            fixed((rank, width)), fixed((rank, HK)), fixed((1, HK)), fixed((KCONV, CONVW)),
        ],
        out_specs=[
            rows(width), rows(HK), rows(HK), rows(HK), rows(HV),
            pl.BlockSpec((tile // PAGE, 8, HK), lambda i: (i, 0, 0)),
            pl.BlockSpec((tile // PAGE, KCONV - 1, HK + HV), lambda i: (i, 0, 0)),
            fixed((HK + RIM, HV)),
        ],
        out_shape=[
            shape((count, width), BF16), shape((count, HK), F32), shape((count, HK), BF16),
            shape((count, HK), BF16), shape((count, HV), BF16), shape((pages, 8, HK), F32),
            shape((pages, KCONV - 1, HK + HV), BF16), shape((HK + RIM, HV), BF16),
        ],
        scratch_shapes=[
            pltpu.VMEM((tile + RIM, width), BF16), pltpu.VMEM((8, HK + HV), F32),
            pltpu.VMEM((HK, HV), F32), pltpu.VMEM((8, HK), F32), pltpu.VMEM((tile, HK), BF16),
        ],
        compiler_params=params(24),
        cost_estimate=cost(1000, 1000),
    )(*prompts, held(tokens), rim, gain, *[held(project)] * 3, held(down), held(up), held(bias), held(conv))


def query_kernel(
    pages_ref, start_ref, normed_ref, rim_ref, gain_ref, query_ref, gate_ref, conv_ref, sums_ref,
    raised_ref, edges_ref, opening_ref, normed_rim, carry,
):
    step = pl.program_id(0)
    tile = normed_ref.shape[0]
    pages = tile // PAGE

    @pl.when(step == 0)
    def _():
        norm_into(normed_rim, gain_ref, [(rim_ref, 0, 0, RIM)])
        low = product(normed_rim, slice(None), query_ref, slice(None)).astype(BF16)
        carry[...] = low.astype(F32)[RIM - 8 :]

    low = product(normed_ref, slice(None), query_ref, slice(None)).astype(BF16)
    projected = low.astype(F32)
    previous = carry[...]
    taps = conv_ref[:, :HK].astype(F32)
    for j in range(pages):
        carried = carried_flag(pages_ref, start_ref, step * pages + j, pl.num_programs(0) * pages)
        mixed = short_conv(projected, previous, carried, taps, j)
        span = pl.ds(j * PAGE, PAGE)
        edges_ref[j] = page_edge(low, j)
        raised_ref[span, :] = (silu(mixed) * jnp.exp(sums_ref[span, :])).astype(BF16)
    carry[...] = projected[tile - 8 :]
    for at in range(0, HV, WIDE):
        columns = pl.ds(at, WIDE)
        opening_ref[:, columns] = silu(product(normed_ref, slice(None), gate_ref, columns)).astype(BF16)


def query(prompts, normed, rim, gain, project, gate, conv, sums):
    count, width = normed.shape
    pages = count // PAGE
    tile = QUERY
    rows = lambda n: pl.BlockSpec((tile, n), lambda i: (i, 0))
    shape = jax.ShapeDtypeStruct
    return pl.pallas_call(
        query_kernel,
        name="query",
        grid=(count // tile,),
        in_specs=[
            whole_smem(), whole_smem(), rows(width), fixed((RIM, width)), fixed((1, width)),
            column_block(width, 0), fixed((width, HV)), fixed((KCONV, CONVW)), rows(HK),
        ],
        out_specs=[
            rows(HK), pl.BlockSpec((tile // PAGE, KCONV - 1, HK), lambda i: (i, 0, 0)), rows(HV),
        ],
        out_shape=[
            shape((count, HK), BF16), shape((pages, KCONV - 1, HK), BF16), shape((count, HV), BF16),
        ],
        scratch_shapes=[pltpu.VMEM((RIM, width), BF16), pltpu.VMEM((8, HK), F32)],
        compiler_params=params(20),
        cost_estimate=cost(2 * count * width * (HK + HV), 2 * count * width),
    )(*prompts, normed, rim, gain, held(project), held(gate), held(conv), sums)


def composed(later, earlier):
    kept = column(later[HK:].astype(F32)[:1, :HK])
    return later[:HK].astype(F32) + kept * earlier[:HK].astype(F32)


def joined_kernel(later_ref, earlier_ref, out_ref):
    out_ref[:HK] = composed(later_ref, earlier_ref).astype(BF16)
    out_ref[HK:] = later_ref[HK:]


def joined(later, earlier):
    return pl.pallas_call(
        joined_kernel, name="joined",
        in_specs=[pl.BlockSpec(memory_space=pltpu.VMEM)] * 2,
        out_specs=pl.BlockSpec(memory_space=pltpu.VMEM),
        out_shape=jax.ShapeDtypeStruct(later.shape, BF16),
        compiler_params=params(6),
        cost_estimate=cost(1000, 1000),
    )(later, earlier)


def halves(count, tile):
    half = count // tile // 2
    return [
        pl.BlockSpec((tile, HV), lambda i: (jnp.minimum(i, half - 1), 0)),
        pl.BlockSpec((tile, HV), lambda i: (jnp.maximum(i - half, 0), 0)),
    ]


def pages_kernel(
    pages_ref, start_ref, raised_ref, lowered_ref, weighted_ref, value_ref, ends_ref, opening_ref, gain_ref,
    one_ref, two_ref, states_ref, low_ref, high_ref, memory,
):
    step = pl.program_id(0)

    @pl.when(step == 0)
    def _():
        memory[...] = composed(one_ref, two_ref)

    row = lax.broadcasted_iota(jnp.int32, (PAGE, PAGE), 0)
    col = lax.broadcasted_iota(jnp.int32, (PAGE, PAGE), 1)
    gain = gain_ref[...].astype(F32)
    held = memory[...]
    gated_tile = []
    for j in range(PAGES_T):
        span = pl.ds(j * PAGE, PAGE)
        raised, value = raised_ref[span, :], value_ref[span, :]
        held = held * carried_flag(pages_ref, start_ref, step * PAGES_T + j, pl.num_programs(0) * PAGES_T)
        scores = dot_nt(raised, lowered_ref[span, :])
        scores = jnp.where(row >= col, scores, 0.0).astype(BF16)
        attended = dot(scores, value) + dot(raised, held.astype(BF16))
        held = column(ends_ref[j][:1]) * held + dot_tn(weighted_ref[span, :], value)
        states_ref[j, 0] = held.astype(BF16)
        gated = normalised(attended, gain) * opening_ref[span, :].astype(F32)
        gated_tile.append(gated.astype(BF16))
    memory[...] = held
    half = pl.num_programs(0) // 2

    @pl.when(step < half)
    def _():
        low_ref[...] = jnp.concatenate(gated_tile, axis=0)

    @pl.when(step >= half)
    def _():
        high_ref[...] = jnp.concatenate(gated_tile, axis=0)


def pages(prompts, raised, lowered, weighted, value, ends, opening, gain, one, two):
    count = raised.shape[0]
    total = count // PAGE
    rows = lambda n: pl.BlockSpec((TILE, n), lambda i: (i, 0))
    return pl.pallas_call(
        pages_kernel,
        name="pages",
        grid=(count // TILE,),
        in_specs=[
            whole_smem(), whole_smem(), rows(HK), rows(HK), rows(HK), rows(HV),
            pl.BlockSpec((PAGES_T, 8, HK), lambda i: (i, 0, 0)), rows(HV), fixed((1, HV)),
            fixed((HK + RIM, HV)), fixed((HK + RIM, HV)),
        ],
        out_specs=[
            pl.BlockSpec((PAGES_T, 1, HK, HV), lambda i: (i, 0, 0, 0)), *halves(count, TILE),
        ],
        out_shape=[
            jax.ShapeDtypeStruct((total, 1, HK, HV), BF16),
            jax.ShapeDtypeStruct((count // 2, HV), BF16),
            jax.ShapeDtypeStruct((count // 2, HV), BF16),
        ],
        scratch_shapes=[pltpu.VMEM((HK, HV), F32)],
        compiler_params=params(12),
        cost_estimate=cost(1000, 1000),
    )(*prompts, raised, lowered, weighted, value, ends, opening, gain, one, two)


def mix_kernel(
    tokens_hbm, low_ref, high_ref, other_low_ref, other_high_ref, own_hbm, other_hbm, gain_ref,
    residual_ref, feed_ref, tokens, own_weight, other_weight, residual, token_sems, weight_sems,
):
    step = pl.program_id(0)
    tile, width = feed_ref.shape
    first = step < pl.num_programs(0) // 2

    def token_copy(i):
        rows = pl.ds(pl.multiple_of(i * tile, tile), tile)
        return pltpu.make_async_copy(tokens_hbm.at[rows, :], tokens.at[rows, :], token_sems.at[i])

    def weight_copies(i):
        columns = pl.ds(i * WIDE, WIDE)
        for j, (source, target) in enumerate(((own_hbm, own_weight), (other_hbm, other_weight))):
            yield pltpu.make_async_copy(source.at[:, columns], target.at[:, columns], weight_sems.at[j, i])

    @pl.when(step == 0)
    def _():
        for i in range(width // WIDE):
            for copy in weight_copies(i):
                copy.start()
            if i == 0:
                token_copy(0).start()
        for i in range(1, tokens.shape[0] // tile):
            token_copy(i).start()

    token_copy(step).wait()
    own = jnp.where(first, low_ref[...], high_ref[...])
    other = jnp.where(first, other_low_ref[...], other_high_ref[...])
    rows = pl.ds(pl.multiple_of(step * tile, tile), tile)
    for i in range(width // WIDE):
        columns = pl.ds(i * WIDE, WIDE)

        @pl.when(step == 0)
        def _():
            for copy in weight_copies(i):
                copy.wait()

        mixed = dot(own, own_weight[:, columns]) + dot(other, other_weight[:, columns])
        residual[:, columns] = (tokens[rows, columns].astype(F32) + mixed).astype(BF16)

    @pl.when(first == (lax.axis_index("hid") == 0))
    def _():
        residual_ref[...] = residual[...]

    def write(columns, x):
        feed_ref[:, columns] = x.astype(BF16)

    rms_columns(lambda columns: residual[:, columns].astype(F32), write, gain_ref, width)


def mix(hid_index, tokens, own, others, own_weight, other_weight, gain):
    count, width = tokens.shape
    tile = MIX
    half = count // tile // 2
    rows = pl.BlockSpec((tile, width), lambda i, s: (i, 0))
    halves = [
        pl.BlockSpec((tile, HV), lambda i, s: (jnp.minimum(i, half - 1), 0)),
        pl.BlockSpec((tile, HV), lambda i, s: (jnp.maximum(i - half, 0), 0)),
    ]
    in_hbm = pl.BlockSpec(memory_space=pltpu.HBM)
    mine = pl.BlockSpec((tile, width), lambda i, s: (jnp.clip(i - s[0] * half, 0, half - 1), 0))
    return pl.pallas_call(
        lambda s, *refs: mix_kernel(*refs),
        name="mix",
        grid_spec=pltpu.PrefetchScalarGridSpec(
            num_scalar_prefetch=1,
            grid=(count // tile,),
            in_specs=[in_hbm, *halves, *halves, in_hbm, in_hbm, fixed((1, width))],
            out_specs=[mine, rows],
            scratch_shapes=[
                pltpu.VMEM((count, width), BF16), pltpu.VMEM((HV, width), BF16),
                pltpu.VMEM((HV, width), BF16), pltpu.VMEM((tile, width), BF16),
                pltpu.SemaphoreType.DMA((count // tile,)), pltpu.SemaphoreType.DMA((2, width // WIDE)),
            ],
        ),
        out_shape=[
            jax.ShapeDtypeStruct((count // 2, width), BF16), jax.ShapeDtypeStruct((count, width), BF16),
        ],
        compiler_params=params(24),
        cost_estimate=cost(1000, 1000),
    )(hid_index, held(tokens), *own, *others, held(own_weight), other_weight, gain)


def widen_sums(places, pieces, feed_ref, rows):
    sums = {}
    for (matrix, place), ref in zip(places, pieces):
        columns = pl.ds(pl.multiple_of(place(), 128), ref.shape[0])
        part = dot(feed_ref[rows, columns], ref[...])
        sums[matrix] = part if matrix not in sums else sums[matrix] + part
    return sums


def widen_kernel(places, feed_ref, *refs):
    pieces, (gate_ref, up_ref) = refs[:-2], refs[-2:]
    for first in range(0, feed_ref.shape[0], ROWS):
        rows = pl.ds(first, ROWS)
        sums = widen_sums(places, pieces, feed_ref, rows)
        gate_ref[rows, :] = silu(sums[0]).astype(BF16)
        up_ref[rows, :] = sums[1]


def finish_kernel(places, feed_ref, gate_ref, up_ref, *refs):
    pieces, out_ref = refs[:-1], refs[-1]
    for first in range(0, feed_ref.shape[0], ROWS):
        rows = pl.ds(first, ROWS)
        total = up_ref[rows, :]
        if pieces:
            total = total + widen_sums(places, pieces, feed_ref, rows)[1]
        out_ref[rows, :] = (gate_ref[rows, :].astype(F32) * total).astype(BF16)


def widen_call(kernel, name, limit, kinds, feed, wholes, matrices):
    count, width = feed.shape
    pieces = [piece for matrix in matrices for piece, _ in matrix]
    places = [(i, place) for i, matrix in enumerate(matrices) for _, place in matrix]
    hidden = (wholes or pieces)[0].shape[1]
    block = pl.BlockSpec((count, WIDE), lambda i: (0, i))
    return pl.pallas_call(
        functools.partial(kernel, places),
        name=name,
        grid=(pl.cdiv(hidden, WIDE),),
        in_specs=[fixed((count, width))] + [block] * len(wholes)
        + [pl.BlockSpec((piece.shape[0], WIDE), lambda i: (0, i)) for piece in pieces],
        out_specs=[block] * len(kinds),
        out_shape=[jax.ShapeDtypeStruct((count, hidden), kind) for kind in kinds],
        compiler_params=params(limit),
        cost_estimate=cost(1000, 1000),
    )(feed, *wholes, *pieces)


def widen(feed, matrices):
    return widen_call(widen_kernel, "widen", WIDEN_VMEM, (BF16, F32), feed, (), matrices)


def finish(feed, wholes, pieces):
    return widen_call(finish_kernel, "finish", FINISH_VMEM, (BF16,), feed, wholes, ([], pieces))[0]


def narrow_kernel(block, hidden_hbm, *refs):
    count = (len(refs) - 5) // 2
    pieces, theirs_ref, own_ref, hidden = refs[:count], *refs[count : count + 3]
    weights, sem, sems = refs[count + 3 : -2], refs[-2], refs[-1]
    rows = hidden.shape[0] // 2
    mine = lax.axis_index("hid")
    wholes = [
        pltpu.make_async_copy(
            hidden_hbm.at[pl.ds(pl.multiple_of(half * rows, rows), rows), :],
            hidden.at[pl.ds(i * rows, rows), :],
            sem.at[i],
        )
        for i, half in enumerate((1 - mine, mine))
    ]
    copies = [
        pltpu.make_async_copy(ref, weight, sems.at[i])
        for i, (ref, weight) in enumerate(zip(pieces, weights))
    ]
    for copy in wholes + copies:
        copy.start()
    for copy in wholes:
        copy.wait()
    at = 0
    for copy, weight in zip(copies, weights):
        copy.wait()
        for low in range(0, weight.shape[1], WIDE):
            for first in range(0, 2 * rows, block):
                total = product(hidden, pl.ds(first, block), weight, pl.ds(low, WIDE)).astype(BF16)
                for out_ref, start in ((theirs_ref, 0), (own_ref, rows)):
                    if first < start + rows and start < first + block:
                        taken = total[max(start - first, 0) : start + rows - first]
                        out_ref[pl.ds(max(first - start, 0), taken.shape[0]), pl.ds(at, WIDE)] = taken
            at += WIDE


def narrow(hidden, pieces, block):
    count, depth = hidden.shape
    width = sum(piece.shape[1] for piece in pieces)
    return pl.pallas_call(
        functools.partial(narrow_kernel, block),
        name="narrow",
        in_specs=[pl.BlockSpec(memory_space=pl.ANY)] * (1 + len(pieces)),
        out_specs=[pl.BlockSpec(memory_space=pltpu.VMEM)] * 2,
        out_shape=[jax.ShapeDtypeStruct((count // 2, width), BF16)] * 2,
        scratch_shapes=[pltpu.VMEM((count, depth), BF16)]
        + [pltpu.VMEM(piece.shape, BF16) for piece in pieces]
        + [pltpu.SemaphoreType.DMA((2,)), pltpu.SemaphoreType.DMA((len(pieces),))],
        compiler_params=params(20),
        cost_estimate=cost(1000, 1000),
    )(hidden, *pieces)


def close_kernel(places, residual_ref, *refs):
    out_ref = refs[-1]
    for group, (own_ref, received_ref) in zip(places, zip(refs[:-1:2], refs[1:-1:2])):
        at = 0
        for size, place in group:
            columns, span = pl.ds(pl.multiple_of(place(), 128), size), pl.ds(at, size)
            total = own_ref[:, span].astype(F32) + received_ref[:, span].astype(F32)
            out_ref[:, columns] = (residual_ref[:, columns].astype(F32) + total).astype(BF16)
            at += size


def close(residual, groups):
    count, width = residual.shape
    rows = lambda n: pl.BlockSpec((TILE, n), lambda i: (i, 0))
    arrays = [array for own, received, _ in groups for array in (own, received)]
    return pl.pallas_call(
        functools.partial(close_kernel, [group[2] for group in groups]),
        name="close",
        grid=(count // TILE,),
        in_specs=[rows(width)] + [rows(array.shape[1]) for array in arrays],
        out_specs=rows(width),
        out_shape=jax.ShapeDtypeStruct((count, width), BF16),
        compiler_params=params(12),
        cost_estimate=cost(1000, 1000),
    )(residual, *arrays)


def shifted(value, steps):
    count = lax.axis_size("seq")
    return lax.ppermute(value, "seq", [(i, i + steps) for i in range(count - steps)])


def swapped(value, axis, flip):
    count = lax.axis_size(axis)
    return lax.ppermute(value, axis, [(i, i ^ flip) for i in range(count)])


def after(value, *others):
    return lax.optimization_barrier((value, *others))[0]


def on_device(
    tokens, attention_gain, project_weight, conv_weight, decay_down, decay_up, decay_bias,
    output_gate, head_gain, output_weight, mixer_gain, gate_weight, up_weight, down_weight,
    prompt_pages, prompt_start,
):
    count, width = tokens.shape
    prompts = (prompt_pages, prompt_start)
    two_by_two = lax.axis_size("req") == 4 and lax.axis_size("seq") % 2 == 0
    hid_index = lax.axis_index("hid").astype(jnp.int32)[None]
    x, y = functools.partial(swapped, axis="req", flip=1), functools.partial(swapped, axis="req", flip=2)
    z = functools.partial(swapped, axis="seq", flip=1)
    depth = gate_weight.shape[0]
    half = depth // 2

    tied = lax.optimization_barrier
    if two_by_two:
        parity = lax.rem(lax.axis_index("seq"), 2)
        up_mine = lax.dynamic_slice_in_dim(up_weight, parity * half, half, 0)
        up_a, up_b = x(up_mine), y(up_mine)
        gate_a, gate_b = x(gate_weight), y(gate_weight)
    rim = shifted(tokens[-RIM:], 1)
    rim, other_output = lax.optimization_barrier((rim, swapped(output_weight, "hid", 1)))

    normed, sums, lowered, weighted, value, ends, edges, state = front(
        prompts, tokens, rim, attention_gain[None], project_weight, decay_down.T, decay_up,
        decay_bias[None], conv_weight,
    )
    one = shifted(state, 1)
    both = joined(state, one)
    two = shifted(both, 2)
    if two_by_two:
        mine, rest = (
            lax.dynamic_slice_in_dim(down_weight, p * half, half, 1) for p in (parity, 1 - parity)
        )
        normed, gate_a, gate_b, both = tied((normed, gate_a, gate_b, both))
        gate_c = x(gate_b)
    raised, query_edges, opening = query(
        prompts, normed, rim, attention_gain[None], project_weight, output_gate, conv_weight, sums,
    )
    if two_by_two:
        raised, up_a, up_b = tied((raised, up_a, up_b))
        up_c, far_a = y(up_a), z(up_a)
    states, *gated = pages(
        prompts, raised, lowered, weighted, value, ends, opening, head_gain[None], one, two,
    )
    others = [swapped(part, "hid", 1) for part in gated]
    if two_by_two:
        far_b, down_b_rest, down_a = z(up_b), y(rest), x(mine)
        others, far_a, up_c = tied((others, far_a, up_c))
        far_c = z(up_c)
    residual, feed = mix(hid_index, tokens, gated, others, output_weight, other_output, mixer_gain[None])

    if two_by_two:
        feed, mine = tied((feed, mine))
        down_b = y(mine)
        at = lambda flip: lambda: (lax.axis_index("req") ^ flip) * depth
        own = lambda flip: lambda: at(flip)() + lax.rem(lax.axis_index("seq"), 2) * half
        far = lambda flip: lambda: at(flip)() + (1 - lax.rem(lax.axis_index("seq"), 2)) * half
        gate_list = [(held(gate_weight), at(0)), (gate_a, at(1)), (gate_b, at(2)), (gate_c, at(3))]
        up_list = [
            (held(up_weight), at(0)), (up_a, own(1)), (far_a, far(1)), (up_b, own(2)), (up_c, own(3)),
        ]
        sums = widen(feed, (gate_list, up_list))
        sums, down_b_rest, down_a = tied((sums, down_b_rest, down_a))
        down_c_rest, down_c, down_a_far = x(down_b_rest), y(down_a), z(down_a)
        hidden = finish(feed, sums, [(far_b, far(2)), (far_c, far(3))])
        down_lists = [
            [(held(down_weight), at(0)), (down_a, own(1)), (down_b_rest, far(2)), (down_b, own(2))],
            [(down_c_rest, far(3)), (down_c, own(3)), (down_a_far, far(1))],
        ]
    else:
        first = lambda: 0
        gate_list = [(lax.all_gather(gate_weight, "req", axis=0, tiled=True), first)]
        up_list = [(lax.all_gather(up_weight, "req", axis=0, tiled=True), first)]
        down_lists = [[(lax.all_gather(down_weight, "req", axis=1, tiled=True), first)]]
        hidden = finish(feed, widen(feed, (gate_list, up_list)), [])

    groups = []
    for pieces in down_lists:
        theirs, mine = narrow(hidden, [piece for piece, _ in pieces], ROWS)
        received = swapped(theirs, "hid", 1)
        groups.append((mine, received, [(piece.shape[1], place) for piece, place in pieces]))
    result = close(residual, groups)
    return result, states, jnp.concatenate([query_edges, edges], axis=-1)


def solution(mesh):
    return jax.shard_map(
        on_device,
        mesh=mesh,
        in_specs=(
            P(("req", "seq"), None),
            P(),
            P(None, "hid"),
            P(None, "hid"),
            P(),
            P(None, "hid"),
            P("hid"),
            P(None, "hid"),
            P(),
            P("hid", None),
            P(),
            P("req", "hid"),
            P("req", "hid"),
            P("hid", "req"),
            P("req", None),
            P("req", None),
        ),
        out_specs=(
            P(("req", "seq", "hid"), None),
            P(("req", "seq"), "hid", None, None),
            P(("req", "seq"), None, "hid"),
        ),
        check_vma=False,
    )
```

```python
import functools

import jax
import jax.numpy as jnp
from jax import lax
from jax.experimental import pallas as pl
from jax.experimental.pallas import tpu as pltpu
from jax.sharding import PartitionSpec as P

HK = 256
HV = 512
KCONV = 4
PAGE = 64
CONVW = 1024
EPSILON = 1e-06
TILE = 256
PAGES_T = TILE // PAGE
RIM = 16
BF16 = jnp.bfloat16
F32 = jnp.float32
WIDE = 256
WIDEN_VMEM = 30
FINISH_VMEM = 24
FRONT = 256
QUERY = 512
MIX = 256
ROWS = 512


def params(mebibytes):
    return pltpu.CompilerParams(vmem_limit_bytes=mebibytes * 1024 * 1024)


def cost(flops, moved):
    return pl.CostEstimate(flops=flops, bytes_accessed=moved, transcendentals=0)


def fixed(shape):
    return pl.BlockSpec(
        shape, lambda *_: (0,) * len(shape), pipeline_mode=pl.Buffered(1)
    )


def held(array):
    return pltpu.with_memory_space_constraint(array, pltpu.HBM)


def whole_smem():
    return pl.BlockSpec(memory_space=pltpu.SMEM)


def dot(a, b):
    return jnp.dot(a, b, preferred_element_type=F32)


def dot_nt(a, b):
    return lax.dot_general(a, b, (((1,), (1,)), ((), ())), preferred_element_type=F32)


def dot_tn(a, b):
    return lax.dot_general(a, b, (((0,), (0,)), ((), ())), preferred_element_type=F32)


def silu(x):
    return x / (1.0 + jnp.exp(-x))


def column(row):
    return jnp.transpose(jnp.broadcast_to(row, (128, row.shape[1])))[:, :1]


def normalised(x, gain):
    return x * lax.rsqrt(jnp.mean(x * x, axis=-1, keepdims=True) + EPSILON) * gain


def carried_flag(pages_ref, start_ref, page, count):
    page = lax.axis_index("seq") * count + page
    same = jnp.int32(0)
    for i in range(pages_ref.shape[1]):
        first = start_ref[0, i]
        same = jnp.where((page > first) & (page < first + pages_ref[0, i]), 1, same)
    return same.astype(F32)


def product(left, rows, weight_ref, columns, step=512):
    depth = weight_ref.shape[0]
    total = None
    for k in range(0, depth, step):
        span = pl.ds(k, min(step, depth - k))
        part = dot(left[rows, span], weight_ref[span, columns])
        total = part if total is None else total + part
    return total


def rms_columns(read, write, gain_ref, width):
    total = None
    for low in range(0, width, WIDE):
        x = read(pl.ds(low, WIDE))
        square = x * x
        part = square[:, : WIDE // 2] + square[:, WIDE // 2 :]
        total = part if total is None else total + part
    scale = lax.rsqrt(jnp.sum(total, axis=-1, keepdims=True) * (1.0 / width) + EPSILON)
    for low in range(0, width, WIDE):
        columns = pl.ds(low, WIDE)
        write(columns, read(columns) * scale * gain_ref[:, columns].astype(F32))


def norm_into(normed, gain_ref, blocks):
    for ref, source, target, count in blocks:
        def read(columns, ref=ref, source=source, count=count):
            return ref[pl.ds(source, count), columns].astype(F32)

        def write(columns, x, target=target, count=count):
            normed[pl.ds(target, count), columns] = x.astype(BF16)

        rms_columns(read, write, gain_ref, normed.shape[1])


def short_conv(projected, previous, carried, taps, j):
    now = projected[j * PAGE : (j + 1) * PAGE]
    before = previous if j == 0 else projected[j * PAGE - 8 : j * PAGE]
    widened = jnp.concatenate([before * carried, now], axis=0)
    mixed = taps[0:1] * now
    for i in range(1, KCONV):
        mixed = mixed + taps[i : i + 1] * widened[8 - i : 8 - i + PAGE]
    return mixed


def page_edge(low, j):
    return low[(j + 1) * PAGE - (KCONV - 1) : (j + 1) * PAGE]


def front_kernel(
    pages_ref, start_ref, tokens_ref, rim_ref, gain_ref, key_ref, first_ref, second_ref, down_ref, up_ref,
    bias_ref, conv_ref, normed_ref, sums_ref, lowered_ref, weighted_ref, value_ref, ends_ref, edges_ref,
    state_ref, normed, carry, state, decay, keys,
):
    step = pl.program_id(0)
    tile = tokens_ref.shape[0]
    pages = tile // PAGE

    @pl.when(step == 0)
    def _():
        state[...] = jnp.zeros_like(state)
        decay[...] = jnp.ones_like(decay)

    norm_into(
        normed, gain_ref,
        [(rim_ref, 0, tile, RIM)] + [(tokens_ref, r, r, 128) for r in range(0, tile, 128)],
    )
    normed_ref[...] = normed[:tile]
    lowrank = dot_nt(normed[:tile], down_ref[...]).astype(BF16)
    logits = dot(lowrank, up_ref[...]) + bias_ref[...]
    decay_log = (jnp.minimum(logits, 0.0) - jnp.log1p(jnp.exp(-jnp.abs(logits)))) / 16.0
    row = lax.broadcasted_iota(jnp.int32, (HK, HK), 0)
    col = lax.broadcasted_iota(jnp.int32, (HK, HK), 1)
    lower = jnp.where((row >= col) & ((row // PAGE) == (col // PAGE)), 1.0, 0.0).astype(F32)
    for r in range(0, tile, HK):
        sums_ref[pl.ds(r, HK), :] = jnp.dot(
            lower, decay_log[r : r + HK], preferred_element_type=F32, precision=lax.Precision.HIGHEST
        )
    carried = [
        carried_flag(pages_ref, start_ref, step * pages + j, pl.num_programs(0) * pages)
        for j in range(pages)
    ]
    ends = [sums_ref[pl.ds((j + 1) * PAGE - 8, 8), :][7:] for j in range(pages)]
    suffix = [None] * pages + [jnp.ones((1, HK), F32)]
    for j in reversed(range(pages)):
        kept = jnp.exp(ends[j])
        ends_ref[j] = jnp.broadcast_to(kept, (8, HK))
        suffix[j] = suffix[j + 1] * (kept * carried[j])

    for chunk, weight_ref in enumerate((key_ref, first_ref, second_ref)):
        columns = pl.ds(chunk * WIDE, WIDE)
        low = product(normed, slice(None), weight_ref, slice(None)).astype(BF16)
        projected = low[:tile].astype(F32)
        previous = jnp.where(step == 0, low[tile:].astype(F32)[RIM - 8 :], carry[:, columns])
        carry[:, columns] = projected[tile - 8 :]
        taps = conv_ref[:, pl.ds(HK + chunk * WIDE, WIDE)].astype(F32)
        for j in range(pages):
            mixed = short_conv(projected, previous, carried[j], taps, j)
            span = pl.ds(j * PAGE, PAGE)
            edges_ref[j, :, columns] = page_edge(low, j)
            if chunk == 0:
                key = silu(mixed) * HK ** (-0.5)
                sums = sums_ref[span, :]
                weighted = key * jnp.exp(ends[j] - sums)
                lowered_ref[span, :] = (key * jnp.exp(-sums)).astype(BF16)
                weighted_ref[span, :] = weighted.astype(BF16)
                keys[span, :] = (weighted * suffix[j + 1]).astype(BF16)
            else:
                value_ref[span, pl.ds((chunk - 1) * WIDE, WIDE)] = mixed.astype(BF16)
    state[...] = column(suffix[0]) * state[...] + dot_tn(keys[...], value_ref[...])
    decay[...] = decay[...] * suffix[0]

    @pl.when(step == pl.num_programs(0) - 1)
    def _():
        state_ref[:HK] = state[...].astype(BF16)
        block = jnp.concatenate([decay[...]] * (HV // HK), axis=1)
        state_ref[HK:] = jnp.concatenate([block] * (RIM // 8), axis=0).astype(BF16)


def column_block(height, i):
    return pl.BlockSpec((height, WIDE), lambda *_: (0, i), pipeline_mode=pl.Buffered(1))


def front(prompts, tokens, rim, gain, project, down, up, bias, conv):
    count, width = tokens.shape
    rank = down.shape[0]
    pages = count // PAGE
    tile = FRONT
    rows = lambda n: pl.BlockSpec((tile, n), lambda i: (i, 0))
    shape = jax.ShapeDtypeStruct
    return pl.pallas_call(
        front_kernel,
        name="front",
        grid=(count // tile,),
        in_specs=[
            whole_smem(), whole_smem(), rows(width), fixed((RIM, width)), fixed((1, width)),
            column_block(width, 1), column_block(width, 2), column_block(width, 3),
            fixed((rank, width)), fixed((rank, HK)), fixed((1, HK)), fixed((KCONV, CONVW)),
        ],
        out_specs=[
            rows(width), rows(HK), rows(HK), rows(HK), rows(HV),
            pl.BlockSpec((tile // PAGE, 8, HK), lambda i: (i, 0, 0)),
            pl.BlockSpec((tile // PAGE, KCONV - 1, HK + HV), lambda i: (i, 0, 0)),
            fixed((HK + RIM, HV)),
        ],
        out_shape=[
            shape((count, width), BF16), shape((count, HK), F32), shape((count, HK), BF16),
            shape((count, HK), BF16), shape((count, HV), BF16), shape((pages, 8, HK), F32),
            shape((pages, KCONV - 1, HK + HV), BF16), shape((HK + RIM, HV), BF16),
        ],
        scratch_shapes=[
            pltpu.VMEM((tile + RIM, width), BF16), pltpu.VMEM((8, HK + HV), F32),
            pltpu.VMEM((HK, HV), F32), pltpu.VMEM((8, HK), F32), pltpu.VMEM((tile, HK), BF16),
        ],
        compiler_params=params(24),
        cost_estimate=cost(1000, 1000),
    )(*prompts, held(tokens), rim, gain, *[held(project)] * 3, held(down), held(up), held(bias), held(conv))


def query_kernel(
    pages_ref, start_ref, normed_ref, rim_ref, gain_ref, query_ref, gate_ref, conv_ref, sums_ref,
    raised_ref, edges_ref, opening_ref, normed_rim, carry,
):
    step = pl.program_id(0)
    tile = normed_ref.shape[0]
    pages = tile // PAGE

    @pl.when(step == 0)
    def _():
        norm_into(normed_rim, gain_ref, [(rim_ref, 0, 0, RIM)])
        low = product(normed_rim, slice(None), query_ref, slice(None)).astype(BF16)
        carry[...] = low.astype(F32)[RIM - 8 :]

    low = product(normed_ref, slice(None), query_ref, slice(None)).astype(BF16)
    projected = low.astype(F32)
    previous = carry[...]
    taps = conv_ref[:, :HK].astype(F32)
    for j in range(pages):
        carried = carried_flag(pages_ref, start_ref, step * pages + j, pl.num_programs(0) * pages)
        mixed = short_conv(projected, previous, carried, taps, j)
        span = pl.ds(j * PAGE, PAGE)
        edges_ref[j] = page_edge(low, j)
        raised_ref[span, :] = (silu(mixed) * jnp.exp(sums_ref[span, :])).astype(BF16)
    carry[...] = projected[tile - 8 :]
    for at in range(0, HV, WIDE):
        columns = pl.ds(at, WIDE)
        opening_ref[:, columns] = silu(product(normed_ref, slice(None), gate_ref, columns)).astype(BF16)


def query(prompts, normed, rim, gain, project, gate, conv, sums):
    count, width = normed.shape
    pages = count // PAGE
    tile = QUERY
    rows = lambda n: pl.BlockSpec((tile, n), lambda i: (i, 0))
    shape = jax.ShapeDtypeStruct
    return pl.pallas_call(
        query_kernel,
        name="query",
        grid=(count // tile,),
        in_specs=[
            whole_smem(), whole_smem(), rows(width), fixed((RIM, width)), fixed((1, width)),
            column_block(width, 0), fixed((width, HV)), fixed((KCONV, CONVW)), rows(HK),
        ],
        out_specs=[
            rows(HK), pl.BlockSpec((tile // PAGE, KCONV - 1, HK), lambda i: (i, 0, 0)), rows(HV),
        ],
        out_shape=[
            shape((count, HK), BF16), shape((pages, KCONV - 1, HK), BF16), shape((count, HV), BF16),
        ],
        scratch_shapes=[pltpu.VMEM((RIM, width), BF16), pltpu.VMEM((8, HK), F32)],
        compiler_params=params(20),
        cost_estimate=cost(2 * count * width * (HK + HV), 2 * count * width),
    )(*prompts, normed, rim, gain, held(project), held(gate), held(conv), sums)


def composed(later, earlier):
    kept = column(later[HK:].astype(F32)[:1, :HK])
    return later[:HK].astype(F32) + kept * earlier[:HK].astype(F32)


def joined_kernel(later_ref, earlier_ref, out_ref):
    out_ref[:HK] = composed(later_ref, earlier_ref).astype(BF16)
    out_ref[HK:] = later_ref[HK:]


def joined(later, earlier):
    return pl.pallas_call(
        joined_kernel, name="joined",
        in_specs=[pl.BlockSpec(memory_space=pltpu.VMEM)] * 2,
        out_specs=pl.BlockSpec(memory_space=pltpu.VMEM),
        out_shape=jax.ShapeDtypeStruct(later.shape, BF16),
        compiler_params=params(6),
        cost_estimate=cost(1000, 1000),
    )(later, earlier)


def halves(count, tile):
    half = count // tile // 2
    return [
        pl.BlockSpec((tile, HV), lambda i: (jnp.minimum(i, half - 1), 0)),
        pl.BlockSpec((tile, HV), lambda i: (jnp.maximum(i - half, 0), 0)),
    ]


def pages_kernel(
    pages_ref, start_ref, raised_ref, lowered_ref, weighted_ref, value_ref, ends_ref, opening_ref, gain_ref,
    one_ref, two_ref, states_ref, low_ref, high_ref, memory,
):
    step = pl.program_id(0)

    @pl.when(step == 0)
    def _():
        memory[...] = composed(one_ref, two_ref)

    row = lax.broadcasted_iota(jnp.int32, (PAGE, PAGE), 0)
    col = lax.broadcasted_iota(jnp.int32, (PAGE, PAGE), 1)
    gain = gain_ref[...].astype(F32)
    held = memory[...]
    gated_tile = []
    for j in range(PAGES_T):
        span = pl.ds(j * PAGE, PAGE)
        raised, value = raised_ref[span, :], value_ref[span, :]
        held = held * carried_flag(pages_ref, start_ref, step * PAGES_T + j, pl.num_programs(0) * PAGES_T)
        scores = dot_nt(raised, lowered_ref[span, :])
        scores = jnp.where(row >= col, scores, 0.0).astype(BF16)
        attended = dot(scores, value) + dot(raised, held.astype(BF16))
        held = column(ends_ref[j][:1]) * held + dot_tn(weighted_ref[span, :], value)
        states_ref[j, 0] = held.astype(BF16)
        gated = normalised(attended, gain) * opening_ref[span, :].astype(F32)
        gated_tile.append(gated.astype(BF16))
    memory[...] = held
    half = pl.num_programs(0) // 2

    @pl.when(step < half)
    def _():
        low_ref[...] = jnp.concatenate(gated_tile, axis=0)

    @pl.when(step >= half)
    def _():
        high_ref[...] = jnp.concatenate(gated_tile, axis=0)


def pages(prompts, raised, lowered, weighted, value, ends, opening, gain, one, two):
    count = raised.shape[0]
    total = count // PAGE
    rows = lambda n: pl.BlockSpec((TILE, n), lambda i: (i, 0))
    return pl.pallas_call(
        pages_kernel,
        name="pages",
        grid=(count // TILE,),
        in_specs=[
            whole_smem(), whole_smem(), rows(HK), rows(HK), rows(HK), rows(HV),
            pl.BlockSpec((PAGES_T, 8, HK), lambda i: (i, 0, 0)), rows(HV), fixed((1, HV)),
            fixed((HK + RIM, HV)), fixed((HK + RIM, HV)),
        ],
        out_specs=[
            pl.BlockSpec((PAGES_T, 1, HK, HV), lambda i: (i, 0, 0, 0)), *halves(count, TILE),
        ],
        out_shape=[
            jax.ShapeDtypeStruct((total, 1, HK, HV), BF16),
            jax.ShapeDtypeStruct((count // 2, HV), BF16),
            jax.ShapeDtypeStruct((count // 2, HV), BF16),
        ],
        scratch_shapes=[pltpu.VMEM((HK, HV), F32)],
        compiler_params=params(12),
        cost_estimate=cost(1000, 1000),
    )(*prompts, raised, lowered, weighted, value, ends, opening, gain, one, two)


def mix_kernel(
    tokens_ref, low_ref, high_ref, other_low_ref, other_high_ref, own_weight_ref, other_weight_ref,
    gain_ref, residual_ref, feed_ref, residual,
):
    first = pl.program_id(0) < pl.num_programs(0) // 2
    own = jnp.where(first, low_ref[...], high_ref[...])
    other = jnp.where(first, other_low_ref[...], other_high_ref[...])
    width = tokens_ref.shape[1]
    for at in range(0, width, WIDE):
        columns = pl.ds(at, WIDE)
        mixed = dot(own, own_weight_ref[:, columns]) + dot(other, other_weight_ref[:, columns])
        residual[:, columns] = (tokens_ref[:, columns].astype(F32) + mixed).astype(BF16)

    @pl.when(first == (lax.axis_index("hid") == 0))
    def _():
        residual_ref[...] = residual[...]

    def write(columns, x):
        feed_ref[:, columns] = x.astype(BF16)

    rms_columns(lambda columns: residual[:, columns].astype(F32), write, gain_ref, width)


def mix(hid_index, tokens, own, others, own_weight, other_weight, gain):
    count, width = tokens.shape
    tile = MIX
    half = count // tile // 2
    rows = pl.BlockSpec((tile, width), lambda i, s: (i, 0))
    halves = [
        pl.BlockSpec((tile, HV), lambda i, s: (jnp.minimum(i, half - 1), 0)),
        pl.BlockSpec((tile, HV), lambda i, s: (jnp.maximum(i - half, 0), 0)),
    ]
    mine = pl.BlockSpec((tile, width), lambda i, s: (jnp.clip(i - s[0] * half, 0, half - 1), 0))
    return pl.pallas_call(
        lambda s, *refs: mix_kernel(*refs),
        name="mix",
        grid_spec=pltpu.PrefetchScalarGridSpec(
            num_scalar_prefetch=1,
            grid=(count // tile,),
            in_specs=[rows, *halves, *halves, fixed((HV, width)), fixed((HV, width)), fixed((1, width))],
            out_specs=[mine, rows],
            scratch_shapes=[pltpu.VMEM((tile, width), BF16)],
        ),
        out_shape=[
            jax.ShapeDtypeStruct((count // 2, width), BF16), jax.ShapeDtypeStruct((count, width), BF16),
        ],
        compiler_params=params(20),
        cost_estimate=cost(1000, 1000),
    )(hid_index, held(tokens), *own, *others, held(own_weight), other_weight, gain)


def widen_sums(places, pieces, feed_ref, rows):
    sums = {}
    for (matrix, place), ref in zip(places, pieces):
        columns = pl.ds(pl.multiple_of(place(), 128), ref.shape[0])
        part = dot(feed_ref[rows, columns], ref[...])
        sums[matrix] = part if matrix not in sums else sums[matrix] + part
    return sums


def widen_kernel(places, feed_ref, *refs):
    pieces, (gate_ref, up_ref) = refs[:-2], refs[-2:]
    for first in range(0, feed_ref.shape[0], ROWS):
        rows = pl.ds(first, ROWS)
        sums = widen_sums(places, pieces, feed_ref, rows)
        gate_ref[rows, :] = silu(sums[0]).astype(BF16)
        up_ref[rows, :] = sums[1]


def finish_kernel(places, feed_ref, gate_ref, up_ref, *refs):
    pieces, out_ref = refs[:-1], refs[-1]
    for first in range(0, feed_ref.shape[0], ROWS):
        rows = pl.ds(first, ROWS)
        total = up_ref[rows, :]
        if pieces:
            total = total + widen_sums(places, pieces, feed_ref, rows)[1]
        out_ref[rows, :] = (gate_ref[rows, :].astype(F32) * total).astype(BF16)


def widen_call(kernel, name, limit, kinds, feed, wholes, matrices):
    count, width = feed.shape
    pieces = [piece for matrix in matrices for piece, _ in matrix]
    places = [(i, place) for i, matrix in enumerate(matrices) for _, place in matrix]
    hidden = (wholes or pieces)[0].shape[1]
    block = pl.BlockSpec((count, WIDE), lambda i: (0, i))
    return pl.pallas_call(
        functools.partial(kernel, places),
        name=name,
        grid=(pl.cdiv(hidden, WIDE),),
        in_specs=[fixed((count, width))] + [block] * len(wholes)
        + [pl.BlockSpec((piece.shape[0], WIDE), lambda i: (0, i)) for piece in pieces],
        out_specs=[block] * len(kinds),
        out_shape=[jax.ShapeDtypeStruct((count, hidden), kind) for kind in kinds],
        compiler_params=params(limit),
        cost_estimate=cost(1000, 1000),
    )(feed, *wholes, *pieces)


def widen(feed, matrices):
    return widen_call(widen_kernel, "widen", WIDEN_VMEM, (BF16, F32), feed, (), matrices)


def finish(feed, wholes, pieces):
    return widen_call(finish_kernel, "finish", FINISH_VMEM, (BF16,), feed, wholes, ([], pieces))[0]


def narrow_kernel(block, hidden_hbm, *refs):
    count = (len(refs) - 5) // 2
    pieces, theirs_ref, own_ref, hidden = refs[:count], *refs[count : count + 3]
    weights, sem, sems = refs[count + 3 : -2], refs[-2], refs[-1]
    rows = hidden.shape[0] // 2
    mine = lax.axis_index("hid")
    wholes = [
        pltpu.make_async_copy(
            hidden_hbm.at[pl.ds(pl.multiple_of(half * rows, rows), rows), :],
            hidden.at[pl.ds(i * rows, rows), :],
            sem.at[i],
        )
        for i, half in enumerate((1 - mine, mine))
    ]
    copies = [
        pltpu.make_async_copy(ref, weight, sems.at[i])
        for i, (ref, weight) in enumerate(zip(pieces, weights))
    ]
    for copy in wholes + copies:
        copy.start()
    for copy in wholes:
        copy.wait()
    at = 0
    for copy, weight in zip(copies, weights):
        copy.wait()
        for low in range(0, weight.shape[1], WIDE):
            for first in range(0, 2 * rows, block):
                total = product(hidden, pl.ds(first, block), weight, pl.ds(low, WIDE)).astype(BF16)
                for out_ref, start in ((theirs_ref, 0), (own_ref, rows)):
                    if first < start + rows and start < first + block:
                        taken = total[max(start - first, 0) : start + rows - first]
                        out_ref[pl.ds(max(first - start, 0), taken.shape[0]), pl.ds(at, WIDE)] = taken
            at += WIDE


def narrow(hidden, pieces, block):
    count, depth = hidden.shape
    width = sum(piece.shape[1] for piece in pieces)
    return pl.pallas_call(
        functools.partial(narrow_kernel, block),
        name="narrow",
        in_specs=[pl.BlockSpec(memory_space=pl.ANY)] * (1 + len(pieces)),
        out_specs=[pl.BlockSpec(memory_space=pltpu.VMEM)] * 2,
        out_shape=[jax.ShapeDtypeStruct((count // 2, width), BF16)] * 2,
        scratch_shapes=[pltpu.VMEM((count, depth), BF16)]
        + [pltpu.VMEM(piece.shape, BF16) for piece in pieces]
        + [pltpu.SemaphoreType.DMA((2,)), pltpu.SemaphoreType.DMA((len(pieces),))],
        compiler_params=params(20),
        cost_estimate=cost(1000, 1000),
    )(hidden, *pieces)


def close_kernel(places, residual_ref, *refs):
    out_ref = refs[-1]
    for group, (own_ref, received_ref) in zip(places, zip(refs[:-1:2], refs[1:-1:2])):
        at = 0
        for size, place in group:
            columns, span = pl.ds(pl.multiple_of(place(), 128), size), pl.ds(at, size)
            total = own_ref[:, span].astype(F32) + received_ref[:, span].astype(F32)
            out_ref[:, columns] = (residual_ref[:, columns].astype(F32) + total).astype(BF16)
            at += size


def close(residual, groups):
    count, width = residual.shape
    rows = lambda n: pl.BlockSpec((TILE, n), lambda i: (i, 0))
    arrays = [array for own, received, _ in groups for array in (own, received)]
    return pl.pallas_call(
        functools.partial(close_kernel, [group[2] for group in groups]),
        name="close",
        grid=(count // TILE,),
        in_specs=[rows(width)] + [rows(array.shape[1]) for array in arrays],
        out_specs=rows(width),
        out_shape=jax.ShapeDtypeStruct((count, width), BF16),
        compiler_params=params(12),
        cost_estimate=cost(1000, 1000),
    )(residual, *arrays)


def shifted(value, steps):
    count = lax.axis_size("seq")
    return lax.ppermute(value, "seq", [(i, i + steps) for i in range(count - steps)])


def swapped(value, axis, flip):
    count = lax.axis_size(axis)
    return lax.ppermute(value, axis, [(i, i ^ flip) for i in range(count)])


def after(value, *others):
    return lax.optimization_barrier((value, *others))[0]


def on_device(
    tokens, attention_gain, project_weight, conv_weight, decay_down, decay_up, decay_bias,
    output_gate, head_gain, output_weight, mixer_gain, gate_weight, up_weight, down_weight,
    prompt_pages, prompt_start,
):
    count, width = tokens.shape
    prompts = (prompt_pages, prompt_start)
    two_by_two = lax.axis_size("req") == 4 and lax.axis_size("seq") % 2 == 0
    hid_index = lax.axis_index("hid").astype(jnp.int32)[None]
    x, y = functools.partial(swapped, axis="req", flip=1), functools.partial(swapped, axis="req", flip=2)
    z = functools.partial(swapped, axis="seq", flip=1)
    depth = gate_weight.shape[0]
    half = depth // 2

    tied = lax.optimization_barrier
    if two_by_two:
        parity = lax.rem(lax.axis_index("seq"), 2)
        up_mine = lax.dynamic_slice_in_dim(up_weight, parity * half, half, 0)
        up_a, up_b = x(up_mine), y(up_mine)
        gate_a, gate_b = x(gate_weight), y(gate_weight)
    rim = shifted(tokens[-RIM:], 1)
    rim, other_output = lax.optimization_barrier((rim, swapped(output_weight, "hid", 1)))

    normed, sums, lowered, weighted, value, ends, edges, state = front(
        prompts, tokens, rim, attention_gain[None], project_weight, decay_down.T, decay_up,
        decay_bias[None], conv_weight,
    )
    one = shifted(state, 1)
    both = joined(state, one)
    two = shifted(both, 2)
    if two_by_two:
        mine, rest = (
            lax.dynamic_slice_in_dim(down_weight, p * half, half, 1) for p in (parity, 1 - parity)
        )
        normed, gate_a, gate_b, both = tied((normed, gate_a, gate_b, both))
        gate_c = x(gate_b)
    raised, query_edges, opening = query(
        prompts, normed, rim, attention_gain[None], project_weight, output_gate, conv_weight, sums,
    )
    if two_by_two:
        raised, up_a, up_b = tied((raised, up_a, up_b))
        up_c, far_a = y(up_a), z(up_a)
    states, *gated = pages(
        prompts, raised, lowered, weighted, value, ends, opening, head_gain[None], one, two,
    )
    others = [swapped(part, "hid", 1) for part in gated]
    if two_by_two:
        far_b, down_b_rest, down_a = z(up_b), y(rest), x(mine)
        others, far_a, up_c = tied((others, far_a, up_c))
        far_c = z(up_c)
    residual, feed = mix(hid_index, tokens, gated, others, output_weight, other_output, mixer_gain[None])

    if two_by_two:
        feed, mine = tied((feed, mine))
        down_b = y(mine)
        at = lambda flip: lambda: (lax.axis_index("req") ^ flip) * depth
        own = lambda flip: lambda: at(flip)() + lax.rem(lax.axis_index("seq"), 2) * half
        far = lambda flip: lambda: at(flip)() + (1 - lax.rem(lax.axis_index("seq"), 2)) * half
        gate_list = [(held(gate_weight), at(0)), (gate_a, at(1)), (gate_b, at(2)), (gate_c, at(3))]
        up_list = [
            (held(up_weight), at(0)), (up_a, own(1)), (far_a, far(1)), (up_b, own(2)), (up_c, own(3)),
        ]
        sums = widen(feed, (gate_list, up_list))
        sums, down_b_rest, down_a = tied((sums, down_b_rest, down_a))
        down_c_rest, down_c, down_a_far = x(down_b_rest), y(down_a), z(down_a)
        hidden = finish(feed, sums, [(far_b, far(2)), (far_c, far(3))])
        down_lists = [
            [(held(down_weight), at(0)), (down_a, own(1)), (down_b_rest, far(2)), (down_b, own(2))],
            [(down_c_rest, far(3)), (down_c, own(3)), (down_a_far, far(1))],
        ]
    else:
        first = lambda: 0
        gate_list = [(lax.all_gather(gate_weight, "req", axis=0, tiled=True), first)]
        up_list = [(lax.all_gather(up_weight, "req", axis=0, tiled=True), first)]
        down_lists = [[(lax.all_gather(down_weight, "req", axis=1, tiled=True), first)]]
        hidden = finish(feed, widen(feed, (gate_list, up_list)), [])

    groups = []
    for pieces in down_lists:
        theirs, mine = narrow(hidden, [piece for piece, _ in pieces], ROWS)
        received = swapped(theirs, "hid", 1)
        groups.append((mine, received, [(piece.shape[1], place) for piece, place in pieces]))
    result = close(residual, groups)
    return result, states, jnp.concatenate([query_edges, edges], axis=-1)


def solution(mesh):
    return jax.shard_map(
        on_device,
        mesh=mesh,
        in_specs=(
            P(("req", "seq"), None),
            P(),
            P(None, "hid"),
            P(None, "hid"),
            P(),
            P(None, "hid"),
            P("hid"),
            P(None, "hid"),
            P(),
            P("hid", None),
            P(),
            P("req", "hid"),
            P("req", "hid"),
            P("hid", "req"),
            P("req", None),
            P("req", None),
        ),
        out_specs=(
            P(("req", "seq", "hid"), None),
            P(("req", "seq"), "hid", None, None),
            P(("req", "seq"), None, "hid"),
        ),
        check_vma=False,
    )
```

```python
import functools

import jax
import jax.numpy as jnp
from jax import lax
from jax.experimental import pallas as pl
from jax.experimental.pallas import tpu as pltpu
from jax.sharding import PartitionSpec as P

HK = 256
HV = 512
KCONV = 4
PAGE = 64
CONVW = 1024
EPSILON = 1e-06
TILE = 256
PAGES_T = TILE // PAGE
RIM = 16
BF16 = jnp.bfloat16
F32 = jnp.float32
WIDE = 256
WIDEN_VMEM = 30
FINISH_VMEM = 24
FRONT = 256
QUERY = 512
MIX = 256
ROWS = 512


def params(mebibytes):
    return pltpu.CompilerParams(vmem_limit_bytes=mebibytes * 1024 * 1024)


def cost(flops, moved):
    return pl.CostEstimate(flops=flops, bytes_accessed=moved, transcendentals=0)


def fixed(shape):
    return pl.BlockSpec(
        shape, lambda *_: (0,) * len(shape), pipeline_mode=pl.Buffered(1)
    )


def held(array):
    return pltpu.with_memory_space_constraint(array, pltpu.HBM)


def whole_smem():
    return pl.BlockSpec(memory_space=pltpu.SMEM)


def dot(a, b):
    return jnp.dot(a, b, preferred_element_type=F32)


def dot_nt(a, b):
    return lax.dot_general(a, b, (((1,), (1,)), ((), ())), preferred_element_type=F32)


def dot_tn(a, b):
    return lax.dot_general(a, b, (((0,), (0,)), ((), ())), preferred_element_type=F32)


def silu(x):
    return x / (1.0 + jnp.exp(-x))


def column(row):
    return jnp.transpose(jnp.broadcast_to(row, (128, row.shape[1])))[:, :1]


def normalised(x, gain):
    return x * lax.rsqrt(jnp.mean(x * x, axis=-1, keepdims=True) + EPSILON) * gain


def carried_flag(pages_ref, start_ref, page, count):
    page = lax.axis_index("seq") * count + page
    same = jnp.int32(0)
    for i in range(pages_ref.shape[1]):
        first = start_ref[0, i]
        same = jnp.where((page > first) & (page < first + pages_ref[0, i]), 1, same)
    return same.astype(F32)


def product(left, rows, weight_ref, columns, step=512):
    depth = weight_ref.shape[0]
    total = None
    for k in range(0, depth, step):
        span = pl.ds(k, min(step, depth - k))
        part = dot(left[rows, span], weight_ref[span, columns])
        total = part if total is None else total + part
    return total


def rms_columns(read, write, gain_ref, width):
    total = None
    for low in range(0, width, WIDE):
        x = read(pl.ds(low, WIDE))
        square = x * x
        part = square[:, : WIDE // 2] + square[:, WIDE // 2 :]
        total = part if total is None else total + part
    scale = lax.rsqrt(jnp.sum(total, axis=-1, keepdims=True) * (1.0 / width) + EPSILON)
    for low in range(0, width, WIDE):
        columns = pl.ds(low, WIDE)
        write(columns, read(columns) * scale * gain_ref[:, columns].astype(F32))


def norm_into(normed, gain_ref, blocks):
    for ref, source, target, count in blocks:
        def read(columns, ref=ref, source=source, count=count):
            return ref[pl.ds(source, count), columns].astype(F32)

        def write(columns, x, target=target, count=count):
            normed[pl.ds(target, count), columns] = x.astype(BF16)

        rms_columns(read, write, gain_ref, normed.shape[1])


def short_conv(projected, previous, carried, taps, j):
    now = projected[j * PAGE : (j + 1) * PAGE]
    before = previous if j == 0 else projected[j * PAGE - 8 : j * PAGE]
    widened = jnp.concatenate([before * carried, now], axis=0)
    mixed = taps[0:1] * now
    for i in range(1, KCONV):
        mixed = mixed + taps[i : i + 1] * widened[8 - i : 8 - i + PAGE]
    return mixed


def page_edge(low, j):
    return low[(j + 1) * PAGE - (KCONV - 1) : (j + 1) * PAGE]


def front_kernel(
    pages_ref, start_ref, tokens_ref, rim_ref, gain_ref, key_ref, first_ref, second_ref, down_ref, up_ref,
    bias_ref, conv_ref, normed_ref, sums_ref, lowered_ref, weighted_ref, value_ref, ends_ref, edges_ref,
    state_ref, normed, carry, state, decay, keys,
):
    step = pl.program_id(0)
    tile = tokens_ref.shape[0]
    pages = tile // PAGE

    @pl.when(step == 0)
    def _():
        state[...] = jnp.zeros_like(state)
        decay[...] = jnp.ones_like(decay)

    norm_into(
        normed, gain_ref,
        [(rim_ref, 0, tile, RIM)] + [(tokens_ref, r, r, 128) for r in range(0, tile, 128)],
    )
    normed_ref[...] = normed[:tile]
    lowrank = dot_nt(normed[:tile], down_ref[...]).astype(BF16)
    logits = dot(lowrank, up_ref[...]) + bias_ref[...]
    decay_log = (jnp.minimum(logits, 0.0) - jnp.log1p(jnp.exp(-jnp.abs(logits)))) / 16.0
    row = lax.broadcasted_iota(jnp.int32, (HK, HK), 0)
    col = lax.broadcasted_iota(jnp.int32, (HK, HK), 1)
    lower = jnp.where((row >= col) & ((row // PAGE) == (col // PAGE)), 1.0, 0.0).astype(F32)
    for r in range(0, tile, HK):
        sums_ref[pl.ds(r, HK), :] = jnp.dot(
            lower, decay_log[r : r + HK], preferred_element_type=F32, precision=lax.Precision.HIGHEST
        )
    carried = [
        carried_flag(pages_ref, start_ref, step * pages + j, pl.num_programs(0) * pages)
        for j in range(pages)
    ]
    ends = [sums_ref[pl.ds((j + 1) * PAGE - 8, 8), :][7:] for j in range(pages)]
    suffix = [None] * pages + [jnp.ones((1, HK), F32)]
    for j in reversed(range(pages)):
        kept = jnp.exp(ends[j])
        ends_ref[j] = jnp.broadcast_to(kept, (8, HK))
        suffix[j] = suffix[j + 1] * (kept * carried[j])

    for chunk, weight_ref in enumerate((key_ref, first_ref, second_ref)):
        columns = pl.ds(chunk * WIDE, WIDE)
        low = product(normed, slice(None), weight_ref, slice(None)).astype(BF16)
        projected = low[:tile].astype(F32)
        previous = jnp.where(step == 0, low[tile:].astype(F32)[RIM - 8 :], carry[:, columns])
        carry[:, columns] = projected[tile - 8 :]
        taps = conv_ref[:, pl.ds(HK + chunk * WIDE, WIDE)].astype(F32)
        for j in range(pages):
            mixed = short_conv(projected, previous, carried[j], taps, j)
            span = pl.ds(j * PAGE, PAGE)
            edges_ref[j, :, columns] = page_edge(low, j)
            if chunk == 0:
                key = silu(mixed) * HK ** (-0.5)
                sums = sums_ref[span, :]
                weighted = key * jnp.exp(ends[j] - sums)
                lowered_ref[span, :] = (key * jnp.exp(-sums)).astype(BF16)
                weighted_ref[span, :] = weighted.astype(BF16)
                keys[span, :] = (weighted * suffix[j + 1]).astype(BF16)
            else:
                value_ref[span, pl.ds((chunk - 1) * WIDE, WIDE)] = mixed.astype(BF16)
    state[...] = column(suffix[0]) * state[...] + dot_tn(keys[...], value_ref[...])
    decay[...] = decay[...] * suffix[0]

    @pl.when(step == pl.num_programs(0) - 1)
    def _():
        state_ref[:HK] = state[...].astype(BF16)
        block = jnp.concatenate([decay[...]] * (HV // HK), axis=1)
        state_ref[HK:] = jnp.concatenate([block] * (RIM // 8), axis=0).astype(BF16)


def column_block(height, i):
    return pl.BlockSpec((height, WIDE), lambda *_: (0, i), pipeline_mode=pl.Buffered(1))


def front(prompts, tokens, rim, gain, project, down, up, bias, conv):
    count, width = tokens.shape
    rank = down.shape[0]
    pages = count // PAGE
    tile = FRONT
    rows = lambda n: pl.BlockSpec((tile, n), lambda i: (i, 0))
    shape = jax.ShapeDtypeStruct
    return pl.pallas_call(
        front_kernel,
        name="front",
        grid=(count // tile,),
        in_specs=[
            whole_smem(), whole_smem(), rows(width), fixed((RIM, width)), fixed((1, width)),
            column_block(width, 1), column_block(width, 2), column_block(width, 3),
            fixed((rank, width)), fixed((rank, HK)), fixed((1, HK)), fixed((KCONV, CONVW)),
        ],
        out_specs=[
            rows(width), rows(HK), rows(HK), rows(HK), rows(HV),
            pl.BlockSpec((tile // PAGE, 8, HK), lambda i: (i, 0, 0)),
            pl.BlockSpec((tile // PAGE, KCONV - 1, HK + HV), lambda i: (i, 0, 0)),
            fixed((HK + RIM, HV)),
        ],
        out_shape=[
            shape((count, width), BF16), shape((count, HK), F32), shape((count, HK), BF16),
            shape((count, HK), BF16), shape((count, HV), BF16), shape((pages, 8, HK), F32),
            shape((pages, KCONV - 1, HK + HV), BF16), shape((HK + RIM, HV), BF16),
        ],
        scratch_shapes=[
            pltpu.VMEM((tile + RIM, width), BF16), pltpu.VMEM((8, HK + HV), F32),
            pltpu.VMEM((HK, HV), F32), pltpu.VMEM((8, HK), F32), pltpu.VMEM((tile, HK), BF16),
        ],
        compiler_params=params(24),
        cost_estimate=cost(1000, 1000),
    )(*prompts, held(tokens), rim, gain, *[held(project)] * 3, held(down), held(up), held(bias), held(conv))


def query_kernel(
    pages_ref, start_ref, normed_ref, rim_ref, gain_ref, query_ref, gate_ref, conv_ref, sums_ref,
    raised_ref, edges_ref, opening_ref, normed_rim, carry,
):
    step = pl.program_id(0)
    tile = normed_ref.shape[0]
    pages = tile // PAGE

    @pl.when(step == 0)
    def _():
        norm_into(normed_rim, gain_ref, [(rim_ref, 0, 0, RIM)])
        low = product(normed_rim, slice(None), query_ref, slice(None)).astype(BF16)
        carry[...] = low.astype(F32)[RIM - 8 :]

    low = product(normed_ref, slice(None), query_ref, slice(None)).astype(BF16)
    projected = low.astype(F32)
    previous = carry[...]
    taps = conv_ref[:, :HK].astype(F32)
    for j in range(pages):
        carried = carried_flag(pages_ref, start_ref, step * pages + j, pl.num_programs(0) * pages)
        mixed = short_conv(projected, previous, carried, taps, j)
        span = pl.ds(j * PAGE, PAGE)
        edges_ref[j] = page_edge(low, j)
        raised_ref[span, :] = (silu(mixed) * jnp.exp(sums_ref[span, :])).astype(BF16)
    carry[...] = projected[tile - 8 :]
    for at in range(0, HV, WIDE):
        columns = pl.ds(at, WIDE)
        opening_ref[:, columns] = silu(product(normed_ref, slice(None), gate_ref, columns)).astype(BF16)


def query(prompts, normed, rim, gain, project, gate, conv, sums):
    count, width = normed.shape
    pages = count // PAGE
    tile = QUERY
    rows = lambda n: pl.BlockSpec((tile, n), lambda i: (i, 0))
    shape = jax.ShapeDtypeStruct
    return pl.pallas_call(
        query_kernel,
        name="query",
        grid=(count // tile,),
        in_specs=[
            whole_smem(), whole_smem(), rows(width), fixed((RIM, width)), fixed((1, width)),
            column_block(width, 0), fixed((width, HV)), fixed((KCONV, CONVW)), rows(HK),
        ],
        out_specs=[
            rows(HK), pl.BlockSpec((tile // PAGE, KCONV - 1, HK), lambda i: (i, 0, 0)), rows(HV),
        ],
        out_shape=[
            shape((count, HK), BF16), shape((pages, KCONV - 1, HK), BF16), shape((count, HV), BF16),
        ],
        scratch_shapes=[pltpu.VMEM((RIM, width), BF16), pltpu.VMEM((8, HK), F32)],
        compiler_params=params(20),
        cost_estimate=cost(2 * count * width * (HK + HV), 2 * count * width),
    )(*prompts, normed, rim, gain, held(project), held(gate), held(conv), sums)


def composed(later, earlier):
    kept = column(later[HK:].astype(F32)[:1, :HK])
    return later[:HK].astype(F32) + kept * earlier[:HK].astype(F32)


def joined_kernel(later_ref, earlier_ref, out_ref):
    out_ref[:HK] = composed(later_ref, earlier_ref).astype(BF16)
    out_ref[HK:] = later_ref[HK:]


def joined(later, earlier):
    return pl.pallas_call(
        joined_kernel, name="joined",
        in_specs=[pl.BlockSpec(memory_space=pltpu.VMEM)] * 2,
        out_specs=pl.BlockSpec(memory_space=pltpu.VMEM),
        out_shape=jax.ShapeDtypeStruct(later.shape, BF16),
        compiler_params=params(6),
        cost_estimate=cost(1000, 1000),
    )(later, earlier)


def halves(count, tile):
    half = count // tile // 2
    return [
        pl.BlockSpec((tile, HV), lambda i: (jnp.minimum(i, half - 1), 0)),
        pl.BlockSpec((tile, HV), lambda i: (jnp.maximum(i - half, 0), 0)),
    ]


def pages_kernel(
    pages_ref, start_ref, raised_ref, lowered_ref, weighted_ref, value_ref, ends_ref, opening_ref, gain_ref,
    one_ref, two_ref, states_ref, low_ref, high_ref, memory,
):
    step = pl.program_id(0)

    @pl.when(step == 0)
    def _():
        memory[...] = composed(one_ref, two_ref)

    row = lax.broadcasted_iota(jnp.int32, (PAGE, PAGE), 0)
    col = lax.broadcasted_iota(jnp.int32, (PAGE, PAGE), 1)
    gain = gain_ref[...].astype(F32)
    held = memory[...]
    gated_tile = []
    for j in range(PAGES_T):
        span = pl.ds(j * PAGE, PAGE)
        raised, value = raised_ref[span, :], value_ref[span, :]
        held = held * carried_flag(pages_ref, start_ref, step * PAGES_T + j, pl.num_programs(0) * PAGES_T)
        scores = dot_nt(raised, lowered_ref[span, :])
        scores = jnp.where(row >= col, scores, 0.0).astype(BF16)
        attended = dot(scores, value) + dot(raised, held.astype(BF16))
        held = column(ends_ref[j][:1]) * held + dot_tn(weighted_ref[span, :], value)
        states_ref[j, 0] = held.astype(BF16)
        gated = normalised(attended, gain) * opening_ref[span, :].astype(F32)
        gated_tile.append(gated.astype(BF16))
    memory[...] = held
    half = pl.num_programs(0) // 2

    @pl.when(step < half)
    def _():
        low_ref[...] = jnp.concatenate(gated_tile, axis=0)

    @pl.when(step >= half)
    def _():
        high_ref[...] = jnp.concatenate(gated_tile, axis=0)


def pages(prompts, raised, lowered, weighted, value, ends, opening, gain, one, two):
    count = raised.shape[0]
    total = count // PAGE
    rows = lambda n: pl.BlockSpec((TILE, n), lambda i: (i, 0))
    return pl.pallas_call(
        pages_kernel,
        name="pages",
        grid=(count // TILE,),
        in_specs=[
            whole_smem(), whole_smem(), rows(HK), rows(HK), rows(HK), rows(HV),
            pl.BlockSpec((PAGES_T, 8, HK), lambda i: (i, 0, 0)), rows(HV), fixed((1, HV)),
            fixed((HK + RIM, HV)), fixed((HK + RIM, HV)),
        ],
        out_specs=[
            pl.BlockSpec((PAGES_T, 1, HK, HV), lambda i: (i, 0, 0, 0)), *halves(count, TILE),
        ],
        out_shape=[
            jax.ShapeDtypeStruct((total, 1, HK, HV), BF16),
            jax.ShapeDtypeStruct((count // 2, HV), BF16),
            jax.ShapeDtypeStruct((count // 2, HV), BF16),
        ],
        scratch_shapes=[pltpu.VMEM((HK, HV), F32)],
        compiler_params=params(12),
        cost_estimate=cost(1000, 1000),
    )(*prompts, raised, lowered, weighted, value, ends, opening, gain, one, two)


def mix_kernel(
    tokens_ref, low_ref, high_ref, other_low_ref, other_high_ref, own_weight_ref, other_weight_ref,
    gain_ref, residual_ref, feed_ref, residual,
):
    first = pl.program_id(0) < pl.num_programs(0) // 2
    own = jnp.where(first, low_ref[...], high_ref[...])
    other = jnp.where(first, other_low_ref[...], other_high_ref[...])
    width = tokens_ref.shape[1]
    for at in range(0, width, WIDE):
        columns = pl.ds(at, WIDE)
        mixed = dot(own, own_weight_ref[:, columns]) + dot(other, other_weight_ref[:, columns])
        residual[:, columns] = (tokens_ref[:, columns].astype(F32) + mixed).astype(BF16)

    @pl.when(first == (lax.axis_index("hid") == 0))
    def _():
        residual_ref[...] = residual[...]

    def write(columns, x):
        feed_ref[:, columns] = x.astype(BF16)

    rms_columns(lambda columns: residual[:, columns].astype(F32), write, gain_ref, width)


def mix(hid_index, tokens, own, others, own_weight, other_weight, gain):
    count, width = tokens.shape
    tile = MIX
    half = count // tile // 2
    rows = pl.BlockSpec((tile, width), lambda i, s: (i, 0))
    halves = [
        pl.BlockSpec((tile, HV), lambda i, s: (jnp.minimum(i, half - 1), 0)),
        pl.BlockSpec((tile, HV), lambda i, s: (jnp.maximum(i - half, 0), 0)),
    ]
    mine = pl.BlockSpec((tile, width), lambda i, s: (jnp.clip(i - s[0] * half, 0, half - 1), 0))
    return pl.pallas_call(
        lambda s, *refs: mix_kernel(*refs),
        name="mix",
        grid_spec=pltpu.PrefetchScalarGridSpec(
            num_scalar_prefetch=1,
            grid=(count // tile,),
            in_specs=[rows, *halves, *halves, fixed((HV, width)), fixed((HV, width)), fixed((1, width))],
            out_specs=[mine, rows],
            scratch_shapes=[pltpu.VMEM((tile, width), BF16)],
        ),
        out_shape=[
            jax.ShapeDtypeStruct((count // 2, width), BF16), jax.ShapeDtypeStruct((count, width), BF16),
        ],
        compiler_params=params(20),
        cost_estimate=cost(1000, 1000),
    )(hid_index, held(tokens), *own, *others, held(own_weight), other_weight, gain)


def widen_sums(places, pieces, feed_ref, rows):
    sums = {}
    for (matrix, place), ref in zip(places, pieces):
        columns = pl.ds(pl.multiple_of(place(), 128), ref.shape[0])
        part = dot(feed_ref[rows, columns], ref[...])
        sums[matrix] = part if matrix not in sums else sums[matrix] + part
    return sums


def widen_kernel(places, feed_ref, *refs):
    pieces, (gate_ref, up_ref) = refs[:-2], refs[-2:]
    for first in range(0, feed_ref.shape[0], ROWS):
        rows = pl.ds(first, ROWS)
        sums = widen_sums(places, pieces, feed_ref, rows)
        gate_ref[rows, :] = silu(sums[0]).astype(BF16)
        up_ref[rows, :] = sums[1].astype(BF16)


def finish_kernel(places, feed_ref, gate_ref, up_ref, *refs):
    pieces, out_ref = refs[:-1], refs[-1]
    for first in range(0, feed_ref.shape[0], ROWS):
        rows = pl.ds(first, ROWS)
        total = up_ref[rows, :].astype(F32)
        if pieces:
            total = total + widen_sums(places, pieces, feed_ref, rows)[1]
        out_ref[rows, :] = (gate_ref[rows, :].astype(F32) * total).astype(BF16)


def widen_call(kernel, name, limit, kinds, feed, wholes, matrices):
    count, width = feed.shape
    pieces = [piece for matrix in matrices for piece, _ in matrix]
    places = [(i, place) for i, matrix in enumerate(matrices) for _, place in matrix]
    hidden = (wholes or pieces)[0].shape[1]
    block = pl.BlockSpec((count, WIDE), lambda i: (0, i))
    return pl.pallas_call(
        functools.partial(kernel, places),
        name=name,
        grid=(pl.cdiv(hidden, WIDE),),
        in_specs=[fixed((count, width))] + [block] * len(wholes)
        + [pl.BlockSpec((piece.shape[0], WIDE), lambda i: (0, i)) for piece in pieces],
        out_specs=[block] * len(kinds),
        out_shape=[jax.ShapeDtypeStruct((count, hidden), kind) for kind in kinds],
        compiler_params=params(limit),
        cost_estimate=cost(1000, 1000),
    )(feed, *wholes, *pieces)


def widen(feed, matrices):
    return widen_call(widen_kernel, "widen", WIDEN_VMEM, (BF16, BF16), feed, (), matrices)


def finish(feed, wholes, pieces):
    return widen_call(finish_kernel, "finish", FINISH_VMEM, (BF16,), feed, wholes, ([], pieces))[0]


def narrow_kernel(block, hidden_hbm, *refs):
    count = (len(refs) - 5) // 2
    pieces, theirs_ref, own_ref, hidden = refs[:count], *refs[count : count + 3]
    weights, sem, sems = refs[count + 3 : -2], refs[-2], refs[-1]
    rows = hidden.shape[0] // 2
    mine = lax.axis_index("hid")
    wholes = [
        pltpu.make_async_copy(
            hidden_hbm.at[pl.ds(pl.multiple_of(half * rows, rows), rows), :],
            hidden.at[pl.ds(i * rows, rows), :],
            sem.at[i],
        )
        for i, half in enumerate((1 - mine, mine))
    ]
    copies = [
        pltpu.make_async_copy(ref, weight, sems.at[i])
        for i, (ref, weight) in enumerate(zip(pieces, weights))
    ]
    for copy in wholes + copies:
        copy.start()
    for copy in wholes:
        copy.wait()
    at = 0
    for copy, weight in zip(copies, weights):
        copy.wait()
        for low in range(0, weight.shape[1], WIDE):
            for first in range(0, 2 * rows, block):
                total = product(hidden, pl.ds(first, block), weight, pl.ds(low, WIDE)).astype(BF16)
                for out_ref, start in ((theirs_ref, 0), (own_ref, rows)):
                    if first < start + rows and start < first + block:
                        taken = total[max(start - first, 0) : start + rows - first]
                        out_ref[pl.ds(max(first - start, 0), taken.shape[0]), pl.ds(at, WIDE)] = taken
            at += WIDE


def narrow(hidden, pieces, block):
    count, depth = hidden.shape
    width = sum(piece.shape[1] for piece in pieces)
    return pl.pallas_call(
        functools.partial(narrow_kernel, block),
        name="narrow",
        in_specs=[pl.BlockSpec(memory_space=pl.ANY)] * (1 + len(pieces)),
        out_specs=[pl.BlockSpec(memory_space=pltpu.VMEM)] * 2,
        out_shape=[jax.ShapeDtypeStruct((count // 2, width), BF16)] * 2,
        scratch_shapes=[pltpu.VMEM((count, depth), BF16)]
        + [pltpu.VMEM(piece.shape, BF16) for piece in pieces]
        + [pltpu.SemaphoreType.DMA((2,)), pltpu.SemaphoreType.DMA((len(pieces),))],
        compiler_params=params(20),
        cost_estimate=cost(1000, 1000),
    )(hidden, *pieces)


def close_kernel(places, residual_ref, *refs):
    out_ref = refs[-1]
    for group, (own_ref, received_ref) in zip(places, zip(refs[:-1:2], refs[1:-1:2])):
        at = 0
        for size, place in group:
            columns, span = pl.ds(pl.multiple_of(place(), 128), size), pl.ds(at, size)
            total = own_ref[:, span].astype(F32) + received_ref[:, span].astype(F32)
            out_ref[:, columns] = (residual_ref[:, columns].astype(F32) + total).astype(BF16)
            at += size


def close(residual, groups):
    count, width = residual.shape
    rows = lambda n: pl.BlockSpec((TILE, n), lambda i: (i, 0))
    arrays = [array for own, received, _ in groups for array in (own, received)]
    return pl.pallas_call(
        functools.partial(close_kernel, [group[2] for group in groups]),
        name="close",
        grid=(count // TILE,),
        in_specs=[rows(width)] + [rows(array.shape[1]) for array in arrays],
        out_specs=rows(width),
        out_shape=jax.ShapeDtypeStruct((count, width), BF16),
        compiler_params=params(12),
        cost_estimate=cost(1000, 1000),
    )(residual, *arrays)


def shifted(value, steps):
    count = lax.axis_size("seq")
    return lax.ppermute(value, "seq", [(i, i + steps) for i in range(count - steps)])


def swapped(value, axis, flip):
    count = lax.axis_size(axis)
    return lax.ppermute(value, axis, [(i, i ^ flip) for i in range(count)])


def after(value, *others):
    return lax.optimization_barrier((value, *others))[0]


def on_device(
    tokens, attention_gain, project_weight, conv_weight, decay_down, decay_up, decay_bias,
    output_gate, head_gain, output_weight, mixer_gain, gate_weight, up_weight, down_weight,
    prompt_pages, prompt_start,
):
    count, width = tokens.shape
    prompts = (prompt_pages, prompt_start)
    two_by_two = lax.axis_size("req") == 4 and lax.axis_size("seq") % 2 == 0
    hid_index = lax.axis_index("hid").astype(jnp.int32)[None]
    x, y = functools.partial(swapped, axis="req", flip=1), functools.partial(swapped, axis="req", flip=2)
    z = functools.partial(swapped, axis="seq", flip=1)
    depth = gate_weight.shape[0]
    half = depth // 2

    tied = lax.optimization_barrier
    if two_by_two:
        parity = lax.rem(lax.axis_index("seq"), 2)
        up_mine = lax.dynamic_slice_in_dim(up_weight, parity * half, half, 0)
        up_a, up_b = x(up_mine), y(up_mine)
        gate_a, gate_b = x(gate_weight), y(gate_weight)
    rim = shifted(tokens[-RIM:], 1)
    rim, other_output = lax.optimization_barrier((rim, swapped(output_weight, "hid", 1)))

    normed, sums, lowered, weighted, value, ends, edges, state = front(
        prompts, tokens, rim, attention_gain[None], project_weight, decay_down.T, decay_up,
        decay_bias[None], conv_weight,
    )
    one = shifted(state, 1)
    both = joined(state, one)
    two = shifted(both, 2)
    if two_by_two:
        mine, rest = (
            lax.dynamic_slice_in_dim(down_weight, p * half, half, 1) for p in (parity, 1 - parity)
        )
        normed, gate_a, gate_b, both = tied((normed, gate_a, gate_b, both))
        gate_c = x(gate_b)
    raised, query_edges, opening = query(
        prompts, normed, rim, attention_gain[None], project_weight, output_gate, conv_weight, sums,
    )
    if two_by_two:
        raised, up_a, up_b = tied((raised, up_a, up_b))
        up_c, far_a = y(up_a), z(up_a)
    states, *gated = pages(
        prompts, raised, lowered, weighted, value, ends, opening, head_gain[None], one, two,
    )
    others = [swapped(part, "hid", 1) for part in gated]
    if two_by_two:
        far_b, down_b_rest, down_a = z(up_b), y(rest), x(mine)
        others, far_a, up_c = tied((others, far_a, up_c))
        far_c = z(up_c)
    residual, feed = mix(hid_index, tokens, gated, others, output_weight, other_output, mixer_gain[None])

    if two_by_two:
        feed, mine = tied((feed, mine))
        down_b = y(mine)
        at = lambda flip: lambda: (lax.axis_index("req") ^ flip) * depth
        own = lambda flip: lambda: at(flip)() + lax.rem(lax.axis_index("seq"), 2) * half
        far = lambda flip: lambda: at(flip)() + (1 - lax.rem(lax.axis_index("seq"), 2)) * half
        gate_list = [(held(gate_weight), at(0)), (gate_a, at(1)), (gate_b, at(2)), (gate_c, at(3))]
        up_list = [
            (held(up_weight), at(0)), (up_a, own(1)), (far_a, far(1)), (up_b, own(2)), (up_c, own(3)),
        ]
        sums = widen(feed, (gate_list, up_list))
        sums, down_b_rest, down_a = tied((sums, down_b_rest, down_a))
        down_c_rest, down_c, down_a_far = x(down_b_rest), y(down_a), z(down_a)
        hidden = finish(feed, sums, [(far_b, far(2)), (far_c, far(3))])
        down_lists = [
            [(held(down_weight), at(0)), (down_a, own(1)), (down_b_rest, far(2)), (down_b, own(2))],
            [(down_c_rest, far(3)), (down_c, own(3)), (down_a_far, far(1))],
        ]
    else:
        first = lambda: 0
        gate_list = [(lax.all_gather(gate_weight, "req", axis=0, tiled=True), first)]
        up_list = [(lax.all_gather(up_weight, "req", axis=0, tiled=True), first)]
        down_lists = [[(lax.all_gather(down_weight, "req", axis=1, tiled=True), first)]]
        hidden = finish(feed, widen(feed, (gate_list, up_list)), [])

    groups = []
    for pieces in down_lists:
        theirs, mine = narrow(hidden, [piece for piece, _ in pieces], ROWS)
        received = swapped(theirs, "hid", 1)
        groups.append((mine, received, [(piece.shape[1], place) for piece, place in pieces]))
    result = close(residual, groups)
    return result, states, jnp.concatenate([query_edges, edges], axis=-1)


def solution(mesh):
    return jax.shard_map(
        on_device,
        mesh=mesh,
        in_specs=(
            P(("req", "seq"), None),
            P(),
            P(None, "hid"),
            P(None, "hid"),
            P(),
            P(None, "hid"),
            P("hid"),
            P(None, "hid"),
            P(),
            P("hid", None),
            P(),
            P("req", "hid"),
            P("req", "hid"),
            P("hid", "req"),
            P("req", None),
            P("req", None),
        ),
        out_specs=(
            P(("req", "seq", "hid"), None),
            P(("req", "seq"), "hid", None, None),
            P(("req", "seq"), None, "hid"),
        ),
        check_vma=False,
    )
```

```python
import functools

import jax
import jax.numpy as jnp
from jax import lax
from jax.experimental import pallas as pl
from jax.experimental.pallas import tpu as pltpu
from jax.sharding import PartitionSpec as P

HK = 256
HV = 512
KCONV = 4
PAGE = 64
CONVW = 1024
EPSILON = 1e-06
TILE = 256
PAGES_T = TILE // PAGE
RIM = 16
BF16 = jnp.bfloat16
F32 = jnp.float32
WIDE = 256
WIDEN_VMEM = 30
FINISH_VMEM = 24
FRONT = 256
QUERY = 512
MIX = 256
ROWS = 512


def params(mebibytes):
    return pltpu.CompilerParams(vmem_limit_bytes=mebibytes * 1024 * 1024)


def cost(flops, moved):
    return pl.CostEstimate(flops=flops, bytes_accessed=moved, transcendentals=0)


def fixed(shape):
    return pl.BlockSpec(
        shape, lambda *_: (0,) * len(shape), pipeline_mode=pl.Buffered(1)
    )


def held(array):
    return pltpu.with_memory_space_constraint(array, pltpu.HBM)


def whole_smem():
    return pl.BlockSpec(memory_space=pltpu.SMEM)


def dot(a, b):
    return jnp.dot(a, b, preferred_element_type=F32)


def dot_nt(a, b):
    return lax.dot_general(a, b, (((1,), (1,)), ((), ())), preferred_element_type=F32)


def dot_tn(a, b):
    return lax.dot_general(a, b, (((0,), (0,)), ((), ())), preferred_element_type=F32)


def silu(x):
    return x / (1.0 + jnp.exp(-x))


def column(row):
    return jnp.transpose(jnp.broadcast_to(row, (128, row.shape[1])))[:, :1]


def normalised(x, gain):
    return x * lax.rsqrt(jnp.mean(x * x, axis=-1, keepdims=True) + EPSILON) * gain


def carried_flag(pages_ref, start_ref, page, count):
    page = lax.axis_index("seq") * count + page
    same = jnp.int32(0)
    for i in range(pages_ref.shape[1]):
        first = start_ref[0, i]
        same = jnp.where((page > first) & (page < first + pages_ref[0, i]), 1, same)
    return same.astype(F32)


def product(left, rows, weight_ref, columns, step=512):
    depth = weight_ref.shape[0]
    total = None
    for k in range(0, depth, step):
        span = pl.ds(k, min(step, depth - k))
        part = dot(left[rows, span], weight_ref[span, columns])
        total = part if total is None else total + part
    return total


def rms_columns(read, write, gain_ref, width):
    total = None
    for low in range(0, width, WIDE):
        x = read(pl.ds(low, WIDE))
        square = x * x
        part = square[:, : WIDE // 2] + square[:, WIDE // 2 :]
        total = part if total is None else total + part
    scale = lax.rsqrt(jnp.sum(total, axis=-1, keepdims=True) * (1.0 / width) + EPSILON)
    for low in range(0, width, WIDE):
        columns = pl.ds(low, WIDE)
        write(columns, read(columns) * scale * gain_ref[:, columns].astype(F32))


def norm_into(normed, gain_ref, blocks):
    for ref, source, target, count in blocks:
        def read(columns, ref=ref, source=source, count=count):
            return ref[pl.ds(source, count), columns].astype(F32)

        def write(columns, x, target=target, count=count):
            normed[pl.ds(target, count), columns] = x.astype(BF16)

        rms_columns(read, write, gain_ref, normed.shape[1])


def short_conv(projected, previous, carried, taps, j):
    now = projected[j * PAGE : (j + 1) * PAGE]
    before = previous if j == 0 else projected[j * PAGE - 8 : j * PAGE]
    widened = jnp.concatenate([before * carried, now], axis=0)
    mixed = taps[0:1] * now
    for i in range(1, KCONV):
        mixed = mixed + taps[i : i + 1] * widened[8 - i : 8 - i + PAGE]
    return mixed


def page_edge(low, j):
    return low[(j + 1) * PAGE - (KCONV - 1) : (j + 1) * PAGE]


def front_kernel(
    pages_ref, start_ref, tokens_ref, rim_ref, gain_ref, key_ref, first_ref, second_ref, down_ref, up_ref,
    bias_ref, conv_ref, normed_ref, sums_ref, lowered_ref, weighted_ref, value_ref, ends_ref, edges_ref,
    state_ref, normed, carry, state, decay, keys,
):
    step = pl.program_id(0)
    tile = tokens_ref.shape[0]
    pages = tile // PAGE

    @pl.when(step == 0)
    def _():
        state[...] = jnp.zeros_like(state)
        decay[...] = jnp.ones_like(decay)

    norm_into(
        normed, gain_ref,
        [(rim_ref, 0, tile, RIM)] + [(tokens_ref, r, r, 128) for r in range(0, tile, 128)],
    )
    normed_ref[...] = normed[:tile]
    lowrank = dot_nt(normed[:tile], down_ref[...]).astype(BF16)
    logits = dot(lowrank, up_ref[...]) + bias_ref[...]
    decay_log = (jnp.minimum(logits, 0.0) - jnp.log1p(jnp.exp(-jnp.abs(logits)))) / 16.0
    row = lax.broadcasted_iota(jnp.int32, (HK, HK), 0)
    col = lax.broadcasted_iota(jnp.int32, (HK, HK), 1)
    lower = jnp.where((row >= col) & ((row // PAGE) == (col // PAGE)), 1.0, 0.0).astype(F32)
    for r in range(0, tile, HK):
        sums_ref[pl.ds(r, HK), :] = jnp.dot(
            lower, decay_log[r : r + HK], preferred_element_type=F32, precision=lax.Precision.HIGHEST
        )
    carried = [
        carried_flag(pages_ref, start_ref, step * pages + j, pl.num_programs(0) * pages)
        for j in range(pages)
    ]
    ends = [sums_ref[pl.ds((j + 1) * PAGE - 8, 8), :][7:] for j in range(pages)]
    suffix = [None] * pages + [jnp.ones((1, HK), F32)]
    for j in reversed(range(pages)):
        kept = jnp.exp(ends[j])
        ends_ref[j] = jnp.broadcast_to(kept, (8, HK))
        suffix[j] = suffix[j + 1] * (kept * carried[j])

    for chunk, weight_ref in enumerate((key_ref, first_ref, second_ref)):
        columns = pl.ds(chunk * WIDE, WIDE)
        low = product(normed, slice(None), weight_ref, slice(None)).astype(BF16)
        projected = low[:tile].astype(F32)
        previous = jnp.where(step == 0, low[tile:].astype(F32)[RIM - 8 :], carry[:, columns])
        carry[:, columns] = projected[tile - 8 :]
        taps = conv_ref[:, pl.ds(HK + chunk * WIDE, WIDE)].astype(F32)
        for j in range(pages):
            mixed = short_conv(projected, previous, carried[j], taps, j)
            span = pl.ds(j * PAGE, PAGE)
            edges_ref[j, :, columns] = page_edge(low, j)
            if chunk == 0:
                key = silu(mixed) * HK ** (-0.5)
                sums = sums_ref[span, :]
                weighted = key * jnp.exp(ends[j] - sums)
                lowered_ref[span, :] = (key * jnp.exp(-sums)).astype(BF16)
                weighted_ref[span, :] = weighted.astype(BF16)
                keys[span, :] = (weighted * suffix[j + 1]).astype(BF16)
            else:
                value_ref[span, pl.ds((chunk - 1) * WIDE, WIDE)] = mixed.astype(BF16)
    state[...] = column(suffix[0]) * state[...] + dot_tn(keys[...], value_ref[...])
    decay[...] = decay[...] * suffix[0]

    @pl.when(step == pl.num_programs(0) - 1)
    def _():
        state_ref[:HK] = state[...].astype(BF16)
        block = jnp.concatenate([decay[...]] * (HV // HK), axis=1)
        state_ref[HK:] = jnp.concatenate([block] * (RIM // 8), axis=0).astype(BF16)


def column_block(height, i):
    return pl.BlockSpec((height, WIDE), lambda *_: (0, i), pipeline_mode=pl.Buffered(1))


def front(prompts, tokens, rim, gain, project, down, up, bias, conv):
    count, width = tokens.shape
    rank = down.shape[0]
    pages = count // PAGE
    tile = FRONT
    rows = lambda n: pl.BlockSpec((tile, n), lambda i: (i, 0))
    shape = jax.ShapeDtypeStruct
    return pl.pallas_call(
        front_kernel,
        name="front",
        grid=(count // tile,),
        in_specs=[
            whole_smem(), whole_smem(), rows(width), fixed((RIM, width)), fixed((1, width)),
            column_block(width, 1), column_block(width, 2), column_block(width, 3),
            fixed((rank, width)), fixed((rank, HK)), fixed((1, HK)), fixed((KCONV, CONVW)),
        ],
        out_specs=[
            rows(width), rows(HK), rows(HK), rows(HK), rows(HV),
            pl.BlockSpec((tile // PAGE, 8, HK), lambda i: (i, 0, 0)),
            pl.BlockSpec((tile // PAGE, KCONV - 1, HK + HV), lambda i: (i, 0, 0)),
            fixed((HK + RIM, HV)),
        ],
        out_shape=[
            shape((count, width), BF16), shape((count, HK), F32), shape((count, HK), BF16),
            shape((count, HK), BF16), shape((count, HV), BF16), shape((pages, 8, HK), F32),
            shape((pages, KCONV - 1, HK + HV), BF16), shape((HK + RIM, HV), BF16),
        ],
        scratch_shapes=[
            pltpu.VMEM((tile + RIM, width), BF16), pltpu.VMEM((8, HK + HV), F32),
            pltpu.VMEM((HK, HV), F32), pltpu.VMEM((8, HK), F32), pltpu.VMEM((tile, HK), BF16),
        ],
        compiler_params=params(24),
        cost_estimate=cost(1000, 1000),
    )(*prompts, held(tokens), rim, gain, *[held(project)] * 3, held(down), held(up), held(bias), held(conv))


def query_kernel(
    pages_ref, start_ref, normed_ref, rim_ref, gain_ref, query_ref, gate_ref, conv_ref, sums_ref,
    raised_ref, edges_ref, opening_ref, normed_rim, carry,
):
    step = pl.program_id(0)
    tile = normed_ref.shape[0]
    pages = tile // PAGE

    @pl.when(step == 0)
    def _():
        norm_into(normed_rim, gain_ref, [(rim_ref, 0, 0, RIM)])
        low = product(normed_rim, slice(None), query_ref, slice(None)).astype(BF16)
        carry[...] = low.astype(F32)[RIM - 8 :]

    low = product(normed_ref, slice(None), query_ref, slice(None)).astype(BF16)
    projected = low.astype(F32)
    previous = carry[...]
    taps = conv_ref[:, :HK].astype(F32)
    for j in range(pages):
        carried = carried_flag(pages_ref, start_ref, step * pages + j, pl.num_programs(0) * pages)
        mixed = short_conv(projected, previous, carried, taps, j)
        span = pl.ds(j * PAGE, PAGE)
        edges_ref[j] = page_edge(low, j)
        raised_ref[span, :] = (silu(mixed) * jnp.exp(sums_ref[span, :])).astype(BF16)
    carry[...] = projected[tile - 8 :]
    for at in range(0, HV, WIDE):
        columns = pl.ds(at, WIDE)
        opening_ref[:, columns] = silu(product(normed_ref, slice(None), gate_ref, columns)).astype(BF16)


def query(prompts, normed, rim, gain, project, gate, conv, sums):
    count, width = normed.shape
    pages = count // PAGE
    tile = QUERY
    rows = lambda n: pl.BlockSpec((tile, n), lambda i: (i, 0))
    shape = jax.ShapeDtypeStruct
    return pl.pallas_call(
        query_kernel,
        name="query",
        grid=(count // tile,),
        in_specs=[
            whole_smem(), whole_smem(), rows(width), fixed((RIM, width)), fixed((1, width)),
            column_block(width, 0), fixed((width, HV)), fixed((KCONV, CONVW)), rows(HK),
        ],
        out_specs=[
            rows(HK), pl.BlockSpec((tile // PAGE, KCONV - 1, HK), lambda i: (i, 0, 0)), rows(HV),
        ],
        out_shape=[
            shape((count, HK), BF16), shape((pages, KCONV - 1, HK), BF16), shape((count, HV), BF16),
        ],
        scratch_shapes=[pltpu.VMEM((RIM, width), BF16), pltpu.VMEM((8, HK), F32)],
        compiler_params=params(20),
        cost_estimate=cost(2 * count * width * (HK + HV), 2 * count * width),
    )(*prompts, normed, rim, gain, held(project), held(gate), held(conv), sums)


def composed(later, earlier):
    kept = column(later[HK:].astype(F32)[:1, :HK])
    return later[:HK].astype(F32) + kept * earlier[:HK].astype(F32)


def joined_kernel(later_ref, earlier_ref, out_ref):
    out_ref[:HK] = composed(later_ref, earlier_ref).astype(BF16)
    out_ref[HK:] = later_ref[HK:]


def joined(later, earlier):
    return pl.pallas_call(
        joined_kernel, name="joined",
        in_specs=[pl.BlockSpec(memory_space=pltpu.VMEM)] * 2,
        out_specs=pl.BlockSpec(memory_space=pltpu.VMEM),
        out_shape=jax.ShapeDtypeStruct(later.shape, BF16),
        compiler_params=params(6),
        cost_estimate=cost(1000, 1000),
    )(later, earlier)


def halves(count, tile):
    half = count // tile // 2
    return [
        pl.BlockSpec((tile, HV), lambda i: (jnp.minimum(i, half - 1), 0)),
        pl.BlockSpec((tile, HV), lambda i: (jnp.maximum(i - half, 0), 0)),
    ]


def pages_kernel(
    pages_ref, start_ref, raised_ref, lowered_ref, weighted_ref, value_ref, ends_ref, opening_ref, gain_ref,
    one_ref, two_ref, states_ref, low_ref, high_ref, memory,
):
    step = pl.program_id(0)

    @pl.when(step == 0)
    def _():
        memory[...] = composed(one_ref, two_ref)

    row = lax.broadcasted_iota(jnp.int32, (PAGE, PAGE), 0)
    col = lax.broadcasted_iota(jnp.int32, (PAGE, PAGE), 1)
    gain = gain_ref[...].astype(F32)
    held = memory[...]
    gated_tile = []
    for j in range(PAGES_T):
        span = pl.ds(j * PAGE, PAGE)
        raised, value = raised_ref[span, :], value_ref[span, :]
        held = held * carried_flag(pages_ref, start_ref, step * PAGES_T + j, pl.num_programs(0) * PAGES_T)
        scores = dot_nt(raised, lowered_ref[span, :])
        scores = jnp.where(row >= col, scores, 0.0).astype(BF16)
        attended = dot(scores, value) + dot(raised, held.astype(BF16))
        held = column(ends_ref[j][:1]) * held + dot_tn(weighted_ref[span, :], value)
        states_ref[j, 0] = held.astype(BF16)
        gated = normalised(attended, gain) * opening_ref[span, :].astype(F32)
        gated_tile.append(gated.astype(BF16))
    memory[...] = held
    half = pl.num_programs(0) // 2

    @pl.when(step < half)
    def _():
        low_ref[...] = jnp.concatenate(gated_tile, axis=0)

    @pl.when(step >= half)
    def _():
        high_ref[...] = jnp.concatenate(gated_tile, axis=0)


def pages(prompts, raised, lowered, weighted, value, ends, opening, gain, one, two):
    count = raised.shape[0]
    total = count // PAGE
    rows = lambda n: pl.BlockSpec((TILE, n), lambda i: (i, 0))
    return pl.pallas_call(
        pages_kernel,
        name="pages",
        grid=(count // TILE,),
        in_specs=[
            whole_smem(), whole_smem(), rows(HK), rows(HK), rows(HK), rows(HV),
            pl.BlockSpec((PAGES_T, 8, HK), lambda i: (i, 0, 0)), rows(HV), fixed((1, HV)),
            fixed((HK + RIM, HV)), fixed((HK + RIM, HV)),
        ],
        out_specs=[
            pl.BlockSpec((PAGES_T, 1, HK, HV), lambda i: (i, 0, 0, 0)), *halves(count, TILE),
        ],
        out_shape=[
            jax.ShapeDtypeStruct((total, 1, HK, HV), BF16),
            jax.ShapeDtypeStruct((count // 2, HV), BF16),
            jax.ShapeDtypeStruct((count // 2, HV), BF16),
        ],
        scratch_shapes=[pltpu.VMEM((HK, HV), F32)],
        compiler_params=params(12),
        cost_estimate=cost(1000, 1000),
    )(*prompts, raised, lowered, weighted, value, ends, opening, gain, one, two)


def mix_kernel(
    tokens_ref, low_ref, high_ref, other_low_ref, other_high_ref, own_weight_ref, other_weight_ref,
    gain_ref, residual_ref, feed_ref, residual,
):
    first = pl.program_id(0) < pl.num_programs(0) // 2
    own = jnp.where(first, low_ref[...], high_ref[...])
    other = jnp.where(first, other_low_ref[...], other_high_ref[...])
    width = tokens_ref.shape[1]
    for at in range(0, width, WIDE):
        columns = pl.ds(at, WIDE)
        mixed = dot(own, own_weight_ref[:, columns]) + dot(other, other_weight_ref[:, columns])
        residual[:, columns] = (tokens_ref[:, columns].astype(F32) + mixed).astype(BF16)

    @pl.when(first == (lax.axis_index("hid") == 0))
    def _():
        residual_ref[...] = residual[...]

    def write(columns, x):
        feed_ref[:, columns] = x.astype(BF16)

    rms_columns(lambda columns: residual[:, columns].astype(F32), write, gain_ref, width)


def mix(hid_index, tokens, own, others, own_weight, other_weight, gain):
    count, width = tokens.shape
    tile = MIX
    half = count // tile // 2
    rows = pl.BlockSpec((tile, width), lambda i, s: (i, 0))
    halves = [
        pl.BlockSpec((tile, HV), lambda i, s: (jnp.minimum(i, half - 1), 0)),
        pl.BlockSpec((tile, HV), lambda i, s: (jnp.maximum(i - half, 0), 0)),
    ]
    mine = pl.BlockSpec((tile, width), lambda i, s: (jnp.clip(i - s[0] * half, 0, half - 1), 0))
    return pl.pallas_call(
        lambda s, *refs: mix_kernel(*refs),
        name="mix",
        grid_spec=pltpu.PrefetchScalarGridSpec(
            num_scalar_prefetch=1,
            grid=(count // tile,),
            in_specs=[rows, *halves, *halves, fixed((HV, width)), fixed((HV, width)), fixed((1, width))],
            out_specs=[mine, rows],
            scratch_shapes=[pltpu.VMEM((tile, width), BF16)],
        ),
        out_shape=[
            jax.ShapeDtypeStruct((count // 2, width), BF16), jax.ShapeDtypeStruct((count, width), BF16),
        ],
        compiler_params=params(20),
        cost_estimate=cost(1000, 1000),
    )(hid_index, held(tokens), *own, *others, held(own_weight), other_weight, gain)


def widen_sums(places, pieces, feed_ref, rows):
    sums = {}
    for (matrix, place), ref in zip(places, pieces):
        columns = pl.ds(pl.multiple_of(place(), 128), ref.shape[0])
        part = dot(feed_ref[rows, columns], ref[...])
        sums[matrix] = part if matrix not in sums else sums[matrix] + part
    return sums


def widen_kernel(places, feed_ref, *refs):
    pieces, (gate_ref, up_ref) = refs[:-2], refs[-2:]
    for first in range(0, feed_ref.shape[0], ROWS):
        rows = pl.ds(first, ROWS)
        sums = widen_sums(places, pieces, feed_ref, rows)
        gate_ref[rows, :] = silu(sums[0]).astype(BF16)
        up_ref[rows, :] = sums[1]


def finish_kernel(places, feed_ref, gate_ref, up_ref, *refs):
    pieces, out_ref = refs[:-1], refs[-1]
    for first in range(0, feed_ref.shape[0], ROWS):
        rows = pl.ds(first, ROWS)
        total = up_ref[rows, :]
        if pieces:
            total = total + widen_sums(places, pieces, feed_ref, rows)[1]
        out_ref[rows, :] = (gate_ref[rows, :].astype(F32) * total).astype(BF16)


def widen_call(kernel, name, limit, kinds, feed, wholes, matrices):
    count, width = feed.shape
    pieces = [piece for matrix in matrices for piece, _ in matrix]
    places = [(i, place) for i, matrix in enumerate(matrices) for _, place in matrix]
    hidden = (wholes or pieces)[0].shape[1]
    block = pl.BlockSpec((count, WIDE), lambda i: (0, i))
    return pl.pallas_call(
        functools.partial(kernel, places),
        name=name,
        grid=(pl.cdiv(hidden, WIDE),),
        in_specs=[fixed((count, width))] + [block] * len(wholes)
        + [pl.BlockSpec((piece.shape[0], WIDE), lambda i: (0, i)) for piece in pieces],
        out_specs=[block] * len(kinds),
        out_shape=[jax.ShapeDtypeStruct((count, hidden), kind) for kind in kinds],
        compiler_params=params(limit),
        cost_estimate=cost(1000, 1000),
    )(feed, *wholes, *pieces)


def widen(feed, matrices):
    return widen_call(widen_kernel, "widen", WIDEN_VMEM, (BF16, F32), feed, (), matrices)


def finish(feed, wholes, pieces):
    return widen_call(finish_kernel, "finish", FINISH_VMEM, (BF16,), feed, wholes, ([], pieces))[0]


def narrow_kernel(block, hidden_hbm, *refs):
    count = (len(refs) - 5) // 2
    pieces, theirs_ref, own_ref, hidden = refs[:count], *refs[count : count + 3]
    weights, sem, sems = refs[count + 3 : -2], refs[-2], refs[-1]
    rows = hidden.shape[0] // 2
    mine = lax.axis_index("hid")
    wholes = [
        pltpu.make_async_copy(
            hidden_hbm.at[pl.ds(pl.multiple_of(half * rows, rows), rows), :],
            hidden.at[pl.ds(i * rows, rows), :],
            sem.at[i],
        )
        for i, half in enumerate((1 - mine, mine))
    ]
    copies = [
        pltpu.make_async_copy(ref, weight, sems.at[i])
        for i, (ref, weight) in enumerate(zip(pieces, weights))
    ]
    for copy in wholes + copies:
        copy.start()
    for copy in wholes:
        copy.wait()
    at = 0
    for copy, weight in zip(copies, weights):
        copy.wait()
        for low in range(0, weight.shape[1], WIDE):
            for first in range(0, 2 * rows, block):
                total = product(hidden, pl.ds(first, block), weight, pl.ds(low, WIDE)).astype(BF16)
                for out_ref, start in ((theirs_ref, 0), (own_ref, rows)):
                    if first < start + rows and start < first + block:
                        taken = total[max(start - first, 0) : start + rows - first]
                        out_ref[pl.ds(max(first - start, 0), taken.shape[0]), pl.ds(at, WIDE)] = taken
            at += WIDE


def narrow(hidden, pieces, block):
    count, depth = hidden.shape
    width = sum(piece.shape[1] for piece in pieces)
    return pl.pallas_call(
        functools.partial(narrow_kernel, block),
        name="narrow",
        in_specs=[pl.BlockSpec(memory_space=pl.ANY)] * (1 + len(pieces)),
        out_specs=[pl.BlockSpec(memory_space=pltpu.VMEM)] * 2,
        out_shape=[jax.ShapeDtypeStruct((count // 2, width), BF16)] * 2,
        scratch_shapes=[pltpu.VMEM((count, depth), BF16)]
        + [pltpu.VMEM(piece.shape, BF16) for piece in pieces]
        + [pltpu.SemaphoreType.DMA((2,)), pltpu.SemaphoreType.DMA((len(pieces),))],
        compiler_params=params(20),
        cost_estimate=cost(1000, 1000),
    )(hidden, *pieces)


def close_kernel(places, residual_ref, *refs):
    out_ref = refs[-1]
    for group, (own_ref, received_ref) in zip(places, zip(refs[:-1:2], refs[1:-1:2])):
        at = 0
        for size, place in group:
            columns, span = pl.ds(pl.multiple_of(place(), 128), size), pl.ds(at, size)
            total = own_ref[:, span].astype(F32) + received_ref[:, span].astype(F32)
            out_ref[:, columns] = (residual_ref[:, columns].astype(F32) + total).astype(BF16)
            at += size


def close(residual, groups):
    count, width = residual.shape
    rows = lambda n: pl.BlockSpec((TILE, n), lambda i: (i, 0))
    arrays = [array for own, received, _ in groups for array in (own, received)]
    return pl.pallas_call(
        functools.partial(close_kernel, [group[2] for group in groups]),
        name="close",
        grid=(count // TILE,),
        in_specs=[rows(width)] + [rows(array.shape[1]) for array in arrays],
        out_specs=rows(width),
        out_shape=jax.ShapeDtypeStruct((count, width), BF16),
        compiler_params=params(12),
        cost_estimate=cost(1000, 1000),
    )(residual, *arrays)


def shifted(value, steps):
    count = lax.axis_size("seq")
    return lax.ppermute(value, "seq", [(i, i + steps) for i in range(count - steps)])


def swapped(value, axis, flip):
    count = lax.axis_size(axis)
    return lax.ppermute(value, axis, [(i, i ^ flip) for i in range(count)])


def after(value, *others):
    return lax.optimization_barrier((value, *others))[0]


def on_device(
    tokens, attention_gain, project_weight, conv_weight, decay_down, decay_up, decay_bias,
    output_gate, head_gain, output_weight, mixer_gain, gate_weight, up_weight, down_weight,
    prompt_pages, prompt_start,
):
    count, width = tokens.shape
    prompts = (prompt_pages, prompt_start)
    two_by_two = lax.axis_size("req") == 4 and lax.axis_size("seq") % 2 == 0
    hid_index = lax.axis_index("hid").astype(jnp.int32)[None]
    x, y = functools.partial(swapped, axis="req", flip=1), functools.partial(swapped, axis="req", flip=2)
    z = functools.partial(swapped, axis="seq", flip=1)
    depth = gate_weight.shape[0]
    half = depth // 2

    tied = lax.optimization_barrier
    if two_by_two:
        parity = lax.rem(lax.axis_index("seq"), 2)
        up_mine = lax.dynamic_slice_in_dim(up_weight, parity * half, half, 0)
        up_a, up_b = x(up_mine), y(up_mine)
        gate_a, gate_b = x(gate_weight), y(gate_weight)
    rim = shifted(tokens[-RIM:], 1)
    rim, other_output = lax.optimization_barrier((rim, swapped(output_weight, "hid", 1)))

    normed, sums, lowered, weighted, value, ends, edges, state = front(
        prompts, tokens, rim, attention_gain[None], project_weight, decay_down.T, decay_up,
        decay_bias[None], conv_weight,
    )
    one = shifted(state, 1)
    both = joined(state, one)
    two = shifted(both, 2)
    if two_by_two:
        mine, rest = (
            lax.dynamic_slice_in_dim(down_weight, p * half, half, 1) for p in (parity, 1 - parity)
        )
        normed, gate_a, gate_b, both = tied((normed, gate_a, gate_b, both))
        gate_c = x(gate_b)
    raised, query_edges, opening = query(
        prompts, normed, rim, attention_gain[None], project_weight, output_gate, conv_weight, sums,
    )
    if two_by_two:
        raised, up_a, up_b = tied((raised, up_a, up_b))
        up_c, far_a = y(up_a), z(up_a)
    states, *gated = pages(
        prompts, raised, lowered, weighted, value, ends, opening, head_gain[None], one, two,
    )
    others = [swapped(part, "hid", 1) for part in gated]
    if two_by_two:
        far_b, down_b_rest, down_a = z(up_b), y(rest), x(mine)
        others, far_a, up_c = tied((others, far_a, up_c))
        far_c = z(up_c)
    residual, feed = mix(hid_index, tokens, gated, others, output_weight, other_output, mixer_gain[None])

    if two_by_two:
        feed, mine = tied((feed, mine))
        down_b = y(mine)
        at = lambda flip: lambda: (lax.axis_index("req") ^ flip) * depth
        own = lambda flip: lambda: at(flip)() + lax.rem(lax.axis_index("seq"), 2) * half
        far = lambda flip: lambda: at(flip)() + (1 - lax.rem(lax.axis_index("seq"), 2)) * half
        gate_list = [(held(gate_weight), at(0)), (gate_a, at(1)), (gate_b, at(2)), (gate_c, at(3))]
        up_list = [
            (held(up_weight), at(0)), (up_a, own(1)), (far_a, far(1)), (up_b, own(2)), (up_c, own(3)),
        ]
        sums = widen(feed, (gate_list, up_list))
        sums, down_b_rest, down_a = tied((sums, down_b_rest, down_a))
        down_c_rest, down_c, down_a_far = x(down_b_rest), y(down_a), z(down_a)
        hidden = finish(feed, sums, [(far_b, far(2)), (far_c, far(3))])
        down_lists = [
            [(held(down_weight), at(0)), (down_a, own(1)), (down_b_rest, far(2)), (down_b, own(2))],
            [(down_c_rest, far(3)), (down_c, own(3)), (down_a_far, far(1))],
        ]
    else:
        first = lambda: 0
        gate_list = [(lax.all_gather(gate_weight, "req", axis=0, tiled=True), first)]
        up_list = [(lax.all_gather(up_weight, "req", axis=0, tiled=True), first)]
        down_lists = [[(lax.all_gather(down_weight, "req", axis=1, tiled=True), first)]]
        hidden = finish(feed, widen(feed, (gate_list, up_list)), [])

    groups = []
    for pieces in down_lists:
        theirs, mine = narrow(hidden, [piece for piece, _ in pieces], ROWS // 2)
        received = swapped(theirs, "hid", 1)
        groups.append((mine, received, [(piece.shape[1], place) for piece, place in pieces]))
    result = close(residual, groups)
    return result, states, jnp.concatenate([query_edges, edges], axis=-1)


def solution(mesh):
    return jax.shard_map(
        on_device,
        mesh=mesh,
        in_specs=(
            P(("req", "seq"), None),
            P(),
            P(None, "hid"),
            P(None, "hid"),
            P(),
            P(None, "hid"),
            P("hid"),
            P(None, "hid"),
            P(),
            P("hid", None),
            P(),
            P("req", "hid"),
            P("req", "hid"),
            P("hid", "req"),
            P("req", None),
            P("req", None),
        ),
        out_specs=(
            P(("req", "seq", "hid"), None),
            P(("req", "seq"), "hid", None, None),
            P(("req", "seq"), None, "hid"),
        ),
        check_vma=False,
    )
```

```python
import functools

import jax
import jax.numpy as jnp
from jax import lax
from jax.experimental import pallas as pl
from jax.experimental.pallas import tpu as pltpu
from jax.sharding import PartitionSpec as P

HK = 256
HV = 512
KCONV = 4
PAGE = 64
CONVW = 1024
EPSILON = 1e-06
TILE = 256
PAGES_T = TILE // PAGE
RIM = 16
BF16 = jnp.bfloat16
F32 = jnp.float32
WIDE = 256
WIDEN_VMEM = 30
FINISH_VMEM = 24
FRONT = 256
QUERY = 512
MIX = 256
ROWS = 512


def params(mebibytes):
    return pltpu.CompilerParams(vmem_limit_bytes=mebibytes * 1024 * 1024)


def cost(flops, moved):
    return pl.CostEstimate(flops=flops, bytes_accessed=moved, transcendentals=0)


def fixed(shape):
    return pl.BlockSpec(
        shape, lambda *_: (0,) * len(shape), pipeline_mode=pl.Buffered(1)
    )


def held(array):
    return pltpu.with_memory_space_constraint(array, pltpu.HBM)


def whole_smem():
    return pl.BlockSpec(memory_space=pltpu.SMEM)


def dot(a, b):
    return jnp.dot(a, b, preferred_element_type=F32)


def dot_nt(a, b):
    return lax.dot_general(a, b, (((1,), (1,)), ((), ())), preferred_element_type=F32)


def dot_tn(a, b):
    return lax.dot_general(a, b, (((0,), (0,)), ((), ())), preferred_element_type=F32)


def silu(x):
    return x / (1.0 + jnp.exp(-x))


def column(row):
    return jnp.transpose(jnp.broadcast_to(row, (128, row.shape[1])))[:, :1]


def normalised(x, gain):
    return x * lax.rsqrt(jnp.mean(x * x, axis=-1, keepdims=True) + EPSILON) * gain


def carried_flag(pages_ref, start_ref, page, count):
    page = lax.axis_index("seq") * count + page
    same = jnp.int32(0)
    for i in range(pages_ref.shape[1]):
        first = start_ref[0, i]
        same = jnp.where((page > first) & (page < first + pages_ref[0, i]), 1, same)
    return same.astype(F32)


def product(left, rows, weight_ref, columns, step=512):
    depth = weight_ref.shape[0]
    total = None
    for k in range(0, depth, step):
        span = pl.ds(k, min(step, depth - k))
        part = dot(left[rows, span], weight_ref[span, columns])
        total = part if total is None else total + part
    return total


def rms_columns(read, write, gain_ref, width):
    total = None
    for low in range(0, width, WIDE):
        x = read(pl.ds(low, WIDE))
        square = x * x
        part = square[:, : WIDE // 2] + square[:, WIDE // 2 :]
        total = part if total is None else total + part
    scale = lax.rsqrt(jnp.sum(total, axis=-1, keepdims=True) * (1.0 / width) + EPSILON)
    for low in range(0, width, WIDE):
        columns = pl.ds(low, WIDE)
        write(columns, read(columns) * scale * gain_ref[:, columns].astype(F32))


def norm_into(normed, gain_ref, blocks):
    for ref, source, target, count in blocks:
        def read(columns, ref=ref, source=source, count=count):
            return ref[pl.ds(source, count), columns].astype(F32)

        def write(columns, x, target=target, count=count):
            normed[pl.ds(target, count), columns] = x.astype(BF16)

        rms_columns(read, write, gain_ref, normed.shape[1])


def short_conv(projected, previous, carried, taps, j):
    now = projected[j * PAGE : (j + 1) * PAGE]
    before = previous if j == 0 else projected[j * PAGE - 8 : j * PAGE]
    widened = jnp.concatenate([before * carried, now], axis=0)
    mixed = taps[0:1] * now
    for i in range(1, KCONV):
        mixed = mixed + taps[i : i + 1] * widened[8 - i : 8 - i + PAGE]
    return mixed


def page_edge(low, j):
    return low[(j + 1) * PAGE - (KCONV - 1) : (j + 1) * PAGE]


def front_kernel(
    pages_ref, start_ref, tokens_ref, rim_ref, gain_ref, key_ref, first_ref, second_ref, down_ref, up_ref,
    bias_ref, conv_ref, normed_ref, sums_ref, lowered_ref, weighted_ref, value_ref, ends_ref, edges_ref,
    state_ref, normed, carry, state, decay, keys,
):
    step = pl.program_id(0)
    tile = tokens_ref.shape[0]
    pages = tile // PAGE

    @pl.when(step == 0)
    def _():
        state[...] = jnp.zeros_like(state)
        decay[...] = jnp.ones_like(decay)

    norm_into(
        normed, gain_ref,
        [(rim_ref, 0, tile, RIM)] + [(tokens_ref, r, r, 128) for r in range(0, tile, 128)],
    )
    normed_ref[...] = normed[:tile]
    lowrank = dot_nt(normed[:tile], down_ref[...]).astype(BF16)
    logits = dot(lowrank, up_ref[...]) + bias_ref[...]
    decay_log = (jnp.minimum(logits, 0.0) - jnp.log1p(jnp.exp(-jnp.abs(logits)))) / 16.0
    row = lax.broadcasted_iota(jnp.int32, (HK, HK), 0)
    col = lax.broadcasted_iota(jnp.int32, (HK, HK), 1)
    lower = jnp.where((row >= col) & ((row // PAGE) == (col // PAGE)), 1.0, 0.0).astype(F32)
    for r in range(0, tile, HK):
        sums_ref[pl.ds(r, HK), :] = jnp.dot(
            lower, decay_log[r : r + HK], preferred_element_type=F32, precision=lax.Precision.HIGHEST
        )
    carried = [
        carried_flag(pages_ref, start_ref, step * pages + j, pl.num_programs(0) * pages)
        for j in range(pages)
    ]
    ends = [sums_ref[pl.ds((j + 1) * PAGE - 8, 8), :][7:] for j in range(pages)]
    suffix = [None] * pages + [jnp.ones((1, HK), F32)]
    for j in reversed(range(pages)):
        kept = jnp.exp(ends[j])
        ends_ref[j] = jnp.broadcast_to(kept, (8, HK))
        suffix[j] = suffix[j + 1] * (kept * carried[j])

    for chunk, weight_ref in enumerate((key_ref, first_ref, second_ref)):
        columns = pl.ds(chunk * WIDE, WIDE)
        low = product(normed, slice(None), weight_ref, slice(None)).astype(BF16)
        projected = low[:tile].astype(F32)
        previous = jnp.where(step == 0, low[tile:].astype(F32)[RIM - 8 :], carry[:, columns])
        carry[:, columns] = projected[tile - 8 :]
        taps = conv_ref[:, pl.ds(HK + chunk * WIDE, WIDE)].astype(F32)
        for j in range(pages):
            mixed = short_conv(projected, previous, carried[j], taps, j)
            span = pl.ds(j * PAGE, PAGE)
            edges_ref[j, :, columns] = page_edge(low, j)
            if chunk == 0:
                key = silu(mixed) * HK ** (-0.5)
                sums = sums_ref[span, :]
                weighted = key * jnp.exp(ends[j] - sums)
                lowered_ref[span, :] = (key * jnp.exp(-sums)).astype(BF16)
                weighted_ref[span, :] = weighted.astype(BF16)
                keys[span, :] = (weighted * suffix[j + 1]).astype(BF16)
            else:
                value_ref[span, pl.ds((chunk - 1) * WIDE, WIDE)] = mixed.astype(BF16)
    state[...] = column(suffix[0]) * state[...] + dot_tn(keys[...], value_ref[...])
    decay[...] = decay[...] * suffix[0]

    @pl.when(step == pl.num_programs(0) - 1)
    def _():
        state_ref[:HK] = state[...].astype(BF16)
        block = jnp.concatenate([decay[...]] * (HV // HK), axis=1)
        state_ref[HK:] = jnp.concatenate([block] * (RIM // 8), axis=0).astype(BF16)


def column_block(height, i):
    return pl.BlockSpec((height, WIDE), lambda *_: (0, i), pipeline_mode=pl.Buffered(1))


def front(prompts, tokens, rim, gain, project, down, up, bias, conv):
    count, width = tokens.shape
    rank = down.shape[0]
    pages = count // PAGE
    tile = FRONT
    rows = lambda n: pl.BlockSpec((tile, n), lambda i: (i, 0))
    shape = jax.ShapeDtypeStruct
    return pl.pallas_call(
        front_kernel,
        name="front",
        grid=(count // tile,),
        in_specs=[
            whole_smem(), whole_smem(), rows(width), fixed((RIM, width)), fixed((1, width)),
            column_block(width, 1), column_block(width, 2), column_block(width, 3),
            fixed((rank, width)), fixed((rank, HK)), fixed((1, HK)), fixed((KCONV, CONVW)),
        ],
        out_specs=[
            rows(width), rows(HK), rows(HK), rows(HK), rows(HV),
            pl.BlockSpec((tile // PAGE, 8, HK), lambda i: (i, 0, 0)),
            pl.BlockSpec((tile // PAGE, KCONV - 1, HK + HV), lambda i: (i, 0, 0)),
            fixed((HK + RIM, HV)),
        ],
        out_shape=[
            shape((count, width), BF16), shape((count, HK), F32), shape((count, HK), BF16),
            shape((count, HK), BF16), shape((count, HV), BF16), shape((pages, 8, HK), F32),
            shape((pages, KCONV - 1, HK + HV), BF16), shape((HK + RIM, HV), BF16),
        ],
        scratch_shapes=[
            pltpu.VMEM((tile + RIM, width), BF16), pltpu.VMEM((8, HK + HV), F32),
            pltpu.VMEM((HK, HV), F32), pltpu.VMEM((8, HK), F32), pltpu.VMEM((tile, HK), BF16),
        ],
        compiler_params=params(24),
        cost_estimate=cost(1000, 1000),
    )(*prompts, held(tokens), rim, gain, *[held(project)] * 3, held(down), held(up), held(bias), held(conv))


def query_kernel(
    pages_ref, start_ref, normed_ref, rim_ref, gain_ref, query_ref, gate_ref, conv_ref, sums_ref,
    raised_ref, edges_ref, opening_ref, normed_rim, carry,
):
    step = pl.program_id(0)
    tile = normed_ref.shape[0]
    pages = tile // PAGE

    @pl.when(step == 0)
    def _():
        norm_into(normed_rim, gain_ref, [(rim_ref, 0, 0, RIM)])
        low = product(normed_rim, slice(None), query_ref, slice(None)).astype(BF16)
        carry[...] = low.astype(F32)[RIM - 8 :]

    low = product(normed_ref, slice(None), query_ref, slice(None)).astype(BF16)
    projected = low.astype(F32)
    previous = carry[...]
    taps = conv_ref[:, :HK].astype(F32)
    for j in range(pages):
        carried = carried_flag(pages_ref, start_ref, step * pages + j, pl.num_programs(0) * pages)
        mixed = short_conv(projected, previous, carried, taps, j)
        span = pl.ds(j * PAGE, PAGE)
        edges_ref[j] = page_edge(low, j)
        raised_ref[span, :] = (silu(mixed) * jnp.exp(sums_ref[span, :])).astype(BF16)
    carry[...] = projected[tile - 8 :]
    for at in range(0, HV, WIDE):
        columns = pl.ds(at, WIDE)
        opening_ref[:, columns] = silu(product(normed_ref, slice(None), gate_ref, columns)).astype(BF16)


def query(prompts, normed, rim, gain, project, gate, conv, sums):
    count, width = normed.shape
    pages = count // PAGE
    tile = QUERY
    rows = lambda n: pl.BlockSpec((tile, n), lambda i: (i, 0))
    shape = jax.ShapeDtypeStruct
    return pl.pallas_call(
        query_kernel,
        name="query",
        grid=(count // tile,),
        in_specs=[
            whole_smem(), whole_smem(), rows(width), fixed((RIM, width)), fixed((1, width)),
            column_block(width, 0), fixed((width, HV)), fixed((KCONV, CONVW)), rows(HK),
        ],
        out_specs=[
            rows(HK), pl.BlockSpec((tile // PAGE, KCONV - 1, HK), lambda i: (i, 0, 0)), rows(HV),
        ],
        out_shape=[
            shape((count, HK), BF16), shape((pages, KCONV - 1, HK), BF16), shape((count, HV), BF16),
        ],
        scratch_shapes=[pltpu.VMEM((RIM, width), BF16), pltpu.VMEM((8, HK), F32)],
        compiler_params=params(20),
        cost_estimate=cost(2 * count * width * (HK + HV), 2 * count * width),
    )(*prompts, normed, rim, gain, held(project), held(gate), held(conv), sums)


def composed(later, earlier):
    kept = column(later[HK:].astype(F32)[:1, :HK])
    return later[:HK].astype(F32) + kept * earlier[:HK].astype(F32)


def joined_kernel(later_ref, earlier_ref, out_ref):
    out_ref[:HK] = composed(later_ref, earlier_ref).astype(BF16)
    out_ref[HK:] = later_ref[HK:]


def joined(later, earlier):
    return pl.pallas_call(
        joined_kernel, name="joined",
        in_specs=[pl.BlockSpec(memory_space=pltpu.VMEM)] * 2,
        out_specs=pl.BlockSpec(memory_space=pltpu.VMEM),
        out_shape=jax.ShapeDtypeStruct(later.shape, BF16),
        compiler_params=params(6),
        cost_estimate=cost(1000, 1000),
    )(later, earlier)


def halves(count, tile):
    half = count // tile // 2
    return [
        pl.BlockSpec((tile, HV), lambda i: (jnp.minimum(i, half - 1), 0)),
        pl.BlockSpec((tile, HV), lambda i: (jnp.maximum(i - half, 0), 0)),
    ]


def pages_kernel(
    pages_ref, start_ref, raised_ref, lowered_ref, weighted_ref, value_ref, ends_ref, opening_ref, gain_ref,
    one_ref, two_ref, states_ref, low_ref, high_ref, memory,
):
    step = pl.program_id(0)

    @pl.when(step == 0)
    def _():
        memory[...] = composed(one_ref, two_ref)

    row = lax.broadcasted_iota(jnp.int32, (PAGE, PAGE), 0)
    col = lax.broadcasted_iota(jnp.int32, (PAGE, PAGE), 1)
    gain = gain_ref[...].astype(F32)
    held = memory[...]
    gated_tile = []
    for j in range(PAGES_T):
        span = pl.ds(j * PAGE, PAGE)
        raised, value = raised_ref[span, :], value_ref[span, :]
        held = held * carried_flag(pages_ref, start_ref, step * PAGES_T + j, pl.num_programs(0) * PAGES_T)
        scores = dot_nt(raised, lowered_ref[span, :])
        scores = jnp.where(row >= col, scores, 0.0).astype(BF16)
        attended = dot(scores, value) + dot(raised, held.astype(BF16))
        held = column(ends_ref[j][:1]) * held + dot_tn(weighted_ref[span, :], value)
        states_ref[j, 0] = held.astype(BF16)
        gated = normalised(attended, gain) * opening_ref[span, :].astype(F32)
        gated_tile.append(gated.astype(BF16))
    memory[...] = held
    half = pl.num_programs(0) // 2

    @pl.when(step < half)
    def _():
        low_ref[...] = jnp.concatenate(gated_tile, axis=0)

    @pl.when(step >= half)
    def _():
        high_ref[...] = jnp.concatenate(gated_tile, axis=0)


def pages(prompts, raised, lowered, weighted, value, ends, opening, gain, one, two):
    count = raised.shape[0]
    total = count // PAGE
    rows = lambda n: pl.BlockSpec((TILE, n), lambda i: (i, 0))
    return pl.pallas_call(
        pages_kernel,
        name="pages",
        grid=(count // TILE,),
        in_specs=[
            whole_smem(), whole_smem(), rows(HK), rows(HK), rows(HK), rows(HV),
            pl.BlockSpec((PAGES_T, 8, HK), lambda i: (i, 0, 0)), rows(HV), fixed((1, HV)),
            fixed((HK + RIM, HV)), fixed((HK + RIM, HV)),
        ],
        out_specs=[
            pl.BlockSpec((PAGES_T, 1, HK, HV), lambda i: (i, 0, 0, 0)), *halves(count, TILE),
        ],
        out_shape=[
            jax.ShapeDtypeStruct((total, 1, HK, HV), BF16),
            jax.ShapeDtypeStruct((count // 2, HV), BF16),
            jax.ShapeDtypeStruct((count // 2, HV), BF16),
        ],
        scratch_shapes=[pltpu.VMEM((HK, HV), F32)],
        compiler_params=params(12),
        cost_estimate=cost(1000, 1000),
    )(*prompts, raised, lowered, weighted, value, ends, opening, gain, one, two)


def mix_kernel(
    tokens_ref, low_ref, high_ref, other_low_ref, other_high_ref, own_weight_ref, other_weight_ref,
    gain_ref, residual_ref, feed_ref, residual,
):
    first = pl.program_id(0) < pl.num_programs(0) // 2
    own = jnp.where(first, low_ref[...], high_ref[...])
    other = jnp.where(first, other_low_ref[...], other_high_ref[...])
    width = tokens_ref.shape[1]
    for at in range(0, width, WIDE):
        columns = pl.ds(at, WIDE)
        mixed = dot(own, own_weight_ref[:, columns]) + dot(other, other_weight_ref[:, columns])
        residual[:, columns] = (tokens_ref[:, columns].astype(F32) + mixed).astype(BF16)

    @pl.when(first == (lax.axis_index("hid") == 0))
    def _():
        residual_ref[...] = residual[...]

    def write(columns, x):
        feed_ref[:, columns] = x.astype(BF16)

    rms_columns(lambda columns: residual[:, columns].astype(F32), write, gain_ref, width)


def mix(hid_index, tokens, own, others, own_weight, other_weight, gain):
    count, width = tokens.shape
    tile = MIX
    half = count // tile // 2
    rows = pl.BlockSpec((tile, width), lambda i, s: (i, 0))
    halves = [
        pl.BlockSpec((tile, HV), lambda i, s: (jnp.minimum(i, half - 1), 0)),
        pl.BlockSpec((tile, HV), lambda i, s: (jnp.maximum(i - half, 0), 0)),
    ]
    mine = pl.BlockSpec((tile, width), lambda i, s: (jnp.clip(i - s[0] * half, 0, half - 1), 0))
    return pl.pallas_call(
        lambda s, *refs: mix_kernel(*refs),
        name="mix",
        grid_spec=pltpu.PrefetchScalarGridSpec(
            num_scalar_prefetch=1,
            grid=(count // tile,),
            in_specs=[rows, *halves, *halves, fixed((HV, width)), fixed((HV, width)), fixed((1, width))],
            out_specs=[mine, rows],
            scratch_shapes=[pltpu.VMEM((tile, width), BF16)],
        ),
        out_shape=[
            jax.ShapeDtypeStruct((count // 2, width), BF16), jax.ShapeDtypeStruct((count, width), BF16),
        ],
        compiler_params=params(20),
        cost_estimate=cost(1000, 1000),
    )(hid_index, held(tokens), *own, *others, held(own_weight), other_weight, gain)


def widen_sums(places, pieces, feed_ref, rows):
    sums = {}
    for (matrix, place), ref in zip(places, pieces):
        columns = pl.ds(pl.multiple_of(place(), 128), ref.shape[0])
        part = dot(feed_ref[rows, columns], ref[...])
        sums[matrix] = part if matrix not in sums else sums[matrix] + part
    return sums


def widen_kernel(places, feed_ref, *refs):
    pieces, (gate_ref, up_ref) = refs[:-2], refs[-2:]
    for first in range(0, feed_ref.shape[0], ROWS):
        rows = pl.ds(first, ROWS)
        sums = widen_sums(places, pieces, feed_ref, rows)
        gate_ref[rows, :] = silu(sums[0]).astype(BF16)
        up_ref[rows, :] = sums[1]


def finish_kernel(places, feed_any, gate_ref, up_ref, *refs):
    pieces, (out_ref, feed, sems) = refs[:-3], refs[-3:]

    @pl.when(pl.program_id(0) == 0)
    def _():
        copies = []
        for j, ((_, place), ref) in enumerate(zip(places, pieces)):
            size = ref.shape[0]
            columns = pl.ds(pl.multiple_of(place(), 128), size)
            copies.append(
                pltpu.make_async_copy(feed_any.at[:, columns], feed.at[:, pl.ds(j * size, size)], sems.at[j])
            )
        for copy in copies:
            copy.start()
        for copy in copies:
            copy.wait()

    for first in range(0, feed.shape[0], ROWS):
        rows = pl.ds(first, ROWS)
        total = up_ref[rows, :]
        for j, ref in enumerate(pieces):
            size = ref.shape[0]
            total = total + dot(feed[rows, pl.ds(j * size, size)], ref[...])
        out_ref[rows, :] = (gate_ref[rows, :].astype(F32) * total).astype(BF16)


def widen_call(kernel, name, limit, kinds, feed, wholes, matrices, feed_spec, scratch=()):
    count, width = feed.shape
    pieces = [piece for matrix in matrices for piece, _ in matrix]
    places = [(i, place) for i, matrix in enumerate(matrices) for _, place in matrix]
    hidden = (wholes or pieces)[0].shape[1]
    block = pl.BlockSpec((count, WIDE), lambda i: (0, i))
    return pl.pallas_call(
        functools.partial(kernel, places),
        name=name,
        grid=(pl.cdiv(hidden, WIDE),),
        in_specs=[feed_spec] + [block] * len(wholes)
        + [pl.BlockSpec((piece.shape[0], WIDE), lambda i: (0, i)) for piece in pieces],
        out_specs=[block] * len(kinds),
        out_shape=[jax.ShapeDtypeStruct((count, hidden), kind) for kind in kinds],
        scratch_shapes=list(scratch),
        compiler_params=params(limit),
        cost_estimate=cost(1000, 1000),
    )(feed, *wholes, *pieces)


def widen(feed, matrices):
    return widen_call(
        widen_kernel, "widen", WIDEN_VMEM, (BF16, F32), feed, (), matrices, fixed(feed.shape)
    )


def finish(feed, wholes, pieces):
    depth = sum(piece.shape[0] for piece, _ in pieces)
    scratch = (
        pltpu.VMEM((feed.shape[0], max(depth, 128)), BF16),
        pltpu.SemaphoreType.DMA((max(len(pieces), 1),)),
    )
    return widen_call(
        finish_kernel, "finish", FINISH_VMEM, (BF16,), feed, wholes, ([], pieces),
        pl.BlockSpec(memory_space=pl.ANY), scratch,
    )[0]


def narrow_kernel(block, hidden_hbm, *refs):
    count = (len(refs) - 5) // 2
    pieces, theirs_ref, own_ref, hidden = refs[:count], *refs[count : count + 3]
    weights, sem, sems = refs[count + 3 : -2], refs[-2], refs[-1]
    rows = hidden.shape[0] // 2
    mine = lax.axis_index("hid")
    wholes = [
        pltpu.make_async_copy(
            hidden_hbm.at[pl.ds(pl.multiple_of(half * rows, rows), rows), :],
            hidden.at[pl.ds(i * rows, rows), :],
            sem.at[i],
        )
        for i, half in enumerate((1 - mine, mine))
    ]
    copies = [
        pltpu.make_async_copy(ref, weight, sems.at[i])
        for i, (ref, weight) in enumerate(zip(pieces, weights))
    ]
    for copy in wholes + copies:
        copy.start()
    for copy in wholes:
        copy.wait()
    at = 0
    for copy, weight in zip(copies, weights):
        copy.wait()
        for low in range(0, weight.shape[1], WIDE):
            for first in range(0, 2 * rows, block):
                total = product(hidden, pl.ds(first, block), weight, pl.ds(low, WIDE)).astype(BF16)
                for out_ref, start in ((theirs_ref, 0), (own_ref, rows)):
                    if first < start + rows and start < first + block:
                        taken = total[max(start - first, 0) : start + rows - first]
                        out_ref[pl.ds(max(first - start, 0), taken.shape[0]), pl.ds(at, WIDE)] = taken
            at += WIDE


def narrow(hidden, pieces, block):
    count, depth = hidden.shape
    width = sum(piece.shape[1] for piece in pieces)
    return pl.pallas_call(
        functools.partial(narrow_kernel, block),
        name="narrow",
        in_specs=[pl.BlockSpec(memory_space=pl.ANY)] * (1 + len(pieces)),
        out_specs=[pl.BlockSpec(memory_space=pltpu.VMEM)] * 2,
        out_shape=[jax.ShapeDtypeStruct((count // 2, width), BF16)] * 2,
        scratch_shapes=[pltpu.VMEM((count, depth), BF16)]
        + [pltpu.VMEM(piece.shape, BF16) for piece in pieces]
        + [pltpu.SemaphoreType.DMA((2,)), pltpu.SemaphoreType.DMA((len(pieces),))],
        compiler_params=params(20),
        cost_estimate=cost(1000, 1000),
    )(hidden, *pieces)


def close_kernel(places, residual_ref, *refs):
    out_ref = refs[-1]
    for group, (own_ref, received_ref) in zip(places, zip(refs[:-1:2], refs[1:-1:2])):
        at = 0
        for size, place in group:
            columns, span = pl.ds(pl.multiple_of(place(), 128), size), pl.ds(at, size)
            total = own_ref[:, span].astype(F32) + received_ref[:, span].astype(F32)
            out_ref[:, columns] = (residual_ref[:, columns].astype(F32) + total).astype(BF16)
            at += size


def close(residual, groups):
    count, width = residual.shape
    rows = lambda n: pl.BlockSpec((TILE, n), lambda i: (i, 0))
    arrays = [array for own, received, _ in groups for array in (own, received)]
    return pl.pallas_call(
        functools.partial(close_kernel, [group[2] for group in groups]),
        name="close",
        grid=(count // TILE,),
        in_specs=[rows(width)] + [rows(array.shape[1]) for array in arrays],
        out_specs=rows(width),
        out_shape=jax.ShapeDtypeStruct((count, width), BF16),
        compiler_params=params(12),
        cost_estimate=cost(1000, 1000),
    )(residual, *arrays)


def shifted(value, steps):
    count = lax.axis_size("seq")
    return lax.ppermute(value, "seq", [(i, i + steps) for i in range(count - steps)])


def swapped(value, axis, flip):
    count = lax.axis_size(axis)
    return lax.ppermute(value, axis, [(i, i ^ flip) for i in range(count)])


def after(value, *others):
    return lax.optimization_barrier((value, *others))[0]


def on_device(
    tokens, attention_gain, project_weight, conv_weight, decay_down, decay_up, decay_bias,
    output_gate, head_gain, output_weight, mixer_gain, gate_weight, up_weight, down_weight,
    prompt_pages, prompt_start,
):
    count, width = tokens.shape
    prompts = (prompt_pages, prompt_start)
    two_by_two = lax.axis_size("req") == 4 and lax.axis_size("seq") % 2 == 0
    hid_index = lax.axis_index("hid").astype(jnp.int32)[None]
    x, y = functools.partial(swapped, axis="req", flip=1), functools.partial(swapped, axis="req", flip=2)
    z = functools.partial(swapped, axis="seq", flip=1)
    depth = gate_weight.shape[0]
    half = depth // 2

    tied = lax.optimization_barrier
    if two_by_two:
        parity = lax.rem(lax.axis_index("seq"), 2)
        up_mine = lax.dynamic_slice_in_dim(up_weight, parity * half, half, 0)
        up_a, up_b = x(up_mine), y(up_mine)
        gate_a, gate_b = x(gate_weight), y(gate_weight)
    rim = shifted(tokens[-RIM:], 1)
    rim, other_output = lax.optimization_barrier((rim, swapped(output_weight, "hid", 1)))

    normed, sums, lowered, weighted, value, ends, edges, state = front(
        prompts, tokens, rim, attention_gain[None], project_weight, decay_down.T, decay_up,
        decay_bias[None], conv_weight,
    )
    one = shifted(state, 1)
    both = joined(state, one)
    two = shifted(both, 2)
    if two_by_two:
        mine, rest = (
            lax.dynamic_slice_in_dim(down_weight, p * half, half, 1) for p in (parity, 1 - parity)
        )
        normed, gate_a, gate_b, both = tied((normed, gate_a, gate_b, both))
        gate_c = x(gate_b)
    raised, query_edges, opening = query(
        prompts, normed, rim, attention_gain[None], project_weight, output_gate, conv_weight, sums,
    )
    if two_by_two:
        raised, up_a, up_b = tied((raised, up_a, up_b))
        up_c, far_a = y(up_a), z(up_a)
    states, *gated = pages(
        prompts, raised, lowered, weighted, value, ends, opening, head_gain[None], one, two,
    )
    others = [swapped(part, "hid", 1) for part in gated]
    if two_by_two:
        far_b, down_b_rest, down_a = z(up_b), y(rest), x(mine)
        others, far_a, up_c = tied((others, far_a, up_c))
        far_c = z(up_c)
    residual, feed = mix(hid_index, tokens, gated, others, output_weight, other_output, mixer_gain[None])

    if two_by_two:
        feed, mine = tied((feed, mine))
        down_b = y(mine)
        at = lambda flip: lambda: (lax.axis_index("req") ^ flip) * depth
        own = lambda flip: lambda: at(flip)() + lax.rem(lax.axis_index("seq"), 2) * half
        far = lambda flip: lambda: at(flip)() + (1 - lax.rem(lax.axis_index("seq"), 2)) * half
        gate_list = [(held(gate_weight), at(0)), (gate_a, at(1)), (gate_b, at(2)), (gate_c, at(3))]
        up_list = [
            (held(up_weight), at(0)), (up_a, own(1)), (far_a, far(1)), (up_b, own(2)), (up_c, own(3)),
        ]
        sums = widen(feed, (gate_list, up_list))
        sums, down_b_rest, down_a = tied((sums, down_b_rest, down_a))
        down_c_rest, down_c, down_a_far = x(down_b_rest), y(down_a), z(down_a)
        hidden = finish(feed, sums, [(far_b, far(2)), (far_c, far(3))])
        down_lists = [
            [(held(down_weight), at(0)), (down_a, own(1)), (down_b_rest, far(2)), (down_b, own(2))],
            [(down_c_rest, far(3)), (down_c, own(3)), (down_a_far, far(1))],
        ]
    else:
        first = lambda: 0
        gate_list = [(lax.all_gather(gate_weight, "req", axis=0, tiled=True), first)]
        up_list = [(lax.all_gather(up_weight, "req", axis=0, tiled=True), first)]
        down_lists = [[(lax.all_gather(down_weight, "req", axis=1, tiled=True), first)]]
        hidden = finish(feed, widen(feed, (gate_list, up_list)), [])

    groups = []
    for pieces in down_lists:
        theirs, mine = narrow(hidden, [piece for piece, _ in pieces], ROWS)
        received = swapped(theirs, "hid", 1)
        groups.append((mine, received, [(piece.shape[1], place) for piece, place in pieces]))
    result = close(residual, groups)
    return result, states, jnp.concatenate([query_edges, edges], axis=-1)


def solution(mesh):
    return jax.shard_map(
        on_device,
        mesh=mesh,
        in_specs=(
            P(("req", "seq"), None),
            P(),
            P(None, "hid"),
            P(None, "hid"),
            P(),
            P(None, "hid"),
            P("hid"),
            P(None, "hid"),
            P(),
            P("hid", None),
            P(),
            P("req", "hid"),
            P("req", "hid"),
            P("hid", "req"),
            P("req", None),
            P("req", None),
        ),
        out_specs=(
            P(("req", "seq", "hid"), None),
            P(("req", "seq"), "hid", None, None),
            P(("req", "seq"), None, "hid"),
        ),
        check_vma=False,
    )
```
